32 devices in a mesh: freq: 2 (over y), tm: 16 (over z, x, core).
Axes of the slice: x: 2, y: 2, z: 4, core: 2. Of those that a mesh axis runs over, the one named last changes fastest.
Arguments:
- tokens: bfloat16 [2, 8, 1024, 768], P(None, 'freq', 'tm'), may hold values from -6 to 6
- out_grad: bfloat16 [2, 8, 1024, 768], P(None, 'freq', 'tm'), may hold values from -6 to 6
- lengths: int32 [2], replicated, may hold values from 128 to 1024, as said below
- norm1_gain: float32 [768], replicated, may hold values from 0.1 to 1.9
- norm1_shift: float32 [768], replicated, may hold values from -1.75 to 1.75
- w_qkv: bfloat16 [768, 2304], replicated, may hold values from -0.21875 to 0.21875
- query_bias: float32 [768], replicated, may hold values from -3 to 3
- value_bias: float32 [768], replicated, may hold values from -0.125 to 0.125
- w_proj: bfloat16 [768, 768], replicated, may hold values from -6 to 6
- proj_bias: float32 [768], replicated, may hold values from -1.75 to 1.75
- norm2_gain: float32 [768], replicated, may hold values from 0.1 to 1.9
- norm2_shift: float32 [768], replicated, may hold values from -1.75 to 1.75
- w_fc1: bfloat16 [768, 3072], replicated, may hold values from -0.21875 to 0.21875
- fc1_bias: float32 [3072], replicated, may hold values from -3 to 3
- w_fc2: bfloat16 [3072, 768], replicated, may hold values from -0.109375 to 0.109375
- fc2_bias: float32 [768], replicated, may hold values from -1.75 to 1.75
- moment: float32 [7090176], P(('freq', 'tm'))
- ema_decay: float32 [1], replicated, may hold values from 0.5 to 0.95
Outputs:
- mixed: bfloat16 [2, 8, 1024, 768], P(None, 'freq', 'tm')
- input_grad: bfloat16 [2, 8, 1024, 768], P(None, 'freq', 'tm')
- weight_grad: float32 [7090176], P(('freq', 'tm'))
- new_moment: float32 [7090176], P(('freq', 'tm'))
The draws below stay inside these ranges and needn't reach their ends.
Inputs may be any that keep to these rules, and one draw needn't show every extreme that they name: `lengths`: at least one clip slot, drawn from the seed, is 1024 frames long.
All inputs are finite; a program needn't handle non-finite values.
Results may differ from the reference program's by a relative error of at most 0.013.
Values may be sent and summed in bfloat16 or wider, within the bound.
No kernel may reach another device: no remote copies, remote signals or barrier semaphores. Data moves between devices by JAX's collectives and lax.ppermute only.
A program may use at most 512 MiB of HBM per device.

```python
import math
import jax
import jax.numpy as jnp
from jax import lax

D = 768
HEADS = 12
HEAD_DIM = 64
FF = 3072
FREQ = 8
CLIPS = 2
TIME = 1024
NPARAM = 7087104
NPAD = 7090176


def draw_lengths(key, part):
    key = jax.random.fold_in(key, 17)
    first_key, second_key = jax.random.split(key)
    shortest = max(1, TIME // 8)
    drawn = jax.random.randint(first_key, (CLIPS,), shortest, TIME + 1)
    longest = jax.random.randint(second_key, (), 0, CLIPS)
    return jnp.where(jnp.arange(CLIPS) == longest, TIME, drawn).astype(jnp.int32)


def draw_moment(key, part):
    key = jax.random.fold_in(key, 29)
    value_key, factor_key = jax.random.split(key)
    base = 0.5 * math.sqrt(float(CLIPS * FREQ * TIME))
    entries = jnp.clip(jax.random.normal(value_key, (NPAD,), jnp.float32), -4.0, 4.0)
    factor = jnp.exp(jax.random.uniform(factor_key, (NPAD,), jnp.float32, math.log(0.5), math.log(2.0)))
    return (base * entries * factor).astype(jnp.float32)


def block_scale(rng, dims, cuts, smallest, high):
    level = 1.0
    for axis_at, parts in cuts:
        steps = jax.random.uniform(jax.random.fold_in(jax.random.fold_in(rng, 6), axis_at), (parts,), jnp.float32, smallest / len(cuts), high / len(cuts))
        level = level * jnp.repeat(jnp.exp(steps), dims[axis_at] // parts).reshape((-1,) + (1,) * (len(dims) - 1 - axis_at))
    return level


def noise(rng, shape, deviation, limit, cuts=(), held_as=jnp.bfloat16):
    values = jax.random.normal(rng, shape, jnp.float32) * deviation
    if len(cuts) > 0:
        values = block_scale(rng, shape, cuts, -0.22, 0.18) * values
    return jnp.clip(values, min=-limit, max=limit).astype(held_as)


def setup_inputs(seed: int = 0) -> dict:
    key_list = jax.random.split(jax.random.key(seed), 19)
    return {
        "tokens": noise(key_list[0], (CLIPS, FREQ, TIME, D), 1.0, 6.0, ((1, 2), (2, 16))),
        "out_grad": noise(key_list[1], (CLIPS, FREQ, TIME, D), 1.0, 6.0, ((1, 2), (2, 16))),
        "lengths": draw_lengths(jax.random.fold_in(key_list[18], 71), 0),
        "norm1_gain": jnp.clip(1.0 + 0.18 * jax.random.normal(key_list[3], (D,), jnp.float32), 0.1, 1.9),
        "norm1_shift": noise(key_list[4], (D,), 0.3, 1.75, (), jnp.float32),
        "w_qkv": noise(key_list[5], (D, 3 * D), D ** -0.5, 0.21875),
        "query_bias": noise(key_list[6], (D,), 0.5, 3.0, (), jnp.float32),
        "value_bias": noise(key_list[7], (D,), 0.02, 0.125, (), jnp.float32),
        "w_proj": noise(key_list[8], (D, D), (max(1, (8 * D) // (FREQ * TIME))) ** -0.5, 6.0),
        "proj_bias": noise(key_list[9], (D,), 0.3, 1.75, (), jnp.float32),
        "norm2_gain": jnp.clip(1.0 + 0.18 * jax.random.normal(key_list[10], (D,), jnp.float32), 0.1, 1.9),
        "norm2_shift": noise(key_list[11], (D,), 0.3, 1.75, (), jnp.float32),
        "w_fc1": noise(key_list[12], (D, FF), D ** -0.5, 0.21875),
        "fc1_bias": noise(key_list[13], (FF,), 0.5, 3.0, (), jnp.float32),
        "w_fc2": noise(key_list[14], (FF, D), FF ** -0.5, 0.109375),
        "fc2_bias": noise(key_list[15], (D,), 0.3, 1.75, (), jnp.float32),
        "moment": draw_moment(jax.random.fold_in(key_list[18], 71), 0),
        "ema_decay": jnp.clip(jax.random.uniform(key_list[17], (1,), jnp.float32, 0.5, 0.95), 0.5, 0.95),
    }


@jax.custom_vjp
def low(v):
    return lax.optimization_barrier(v.astype(jnp.bfloat16)).astype(jnp.float32)

@jax.custom_vjp
def low_back(v):
    return v

def low_keep(v):
    return (low(v), None)

def low_pass(kept, grad):
    return (grad,)

def back_keep(v):
    return (v, None)

def back_low(kept, grad):
    return (low(grad),)
low.defvjp(low_keep, low_pass)
low_back.defvjp(back_keep, back_low)
EPSILON = 1e-06
NEGATIVE = -1e+30
HIGHEST = lax.Precision.HIGHEST

def layer_norm(values, scaling, offset):
    row_mean = lax.optimization_barrier(jnp.mean(values, axis=-1, keepdims=True))
    centred = values - row_mean
    spread = lax.optimization_barrier(jnp.mean(centred * centred, axis=-1, keepdims=True))
    return centred * lax.rsqrt(spread + EPSILON) * scaling + offset

def product(left, right):
    return jnp.dot(left, right, precision=HIGHEST, preferred_element_type=jnp.float32)

def clip_attention(queries, key_rows, values, alive_keys):
    patches = queries.shape[0]
    query_block = math.gcd(patches, 256)
    score_scale = HEAD_DIM ** (-0.5)

    def one_block(block_queries):
        scores = jnp.einsum('qhd,khd->hqk', block_queries, key_rows, precision=HIGHEST) * score_scale
        scores = low_back(scores)
        scores = jnp.where(alive_keys[None, None, :], scores, NEGATIVE)
        largest = lax.optimization_barrier(jnp.max(scores, axis=-1, keepdims=True))
        weights = jnp.exp(scores - largest)
        probs_full = weights / lax.optimization_barrier(jnp.sum(weights, axis=-1, keepdims=True))
        return jnp.einsum('hqk,khd->qhd', low(probs_full), values, precision=HIGHEST)
    blocks = queries.reshape(patches // query_block, query_block, HEADS, HEAD_DIM)
    return lax.map(jax.checkpoint(one_block), blocks).reshape(patches, HEADS, HEAD_DIM)

def forward(inputs, alive_mask, norm1_gain, norm1_shift, w_qkv, query_bias, value_bias, w_proj, proj_bias, norm2_gain, norm2_shift, w_fc1, fc1_bias, w_fc2, fc2_bias):
    clip_count, patches, model_width = inputs.shape
    flat_rows = inputs.reshape(clip_count * patches, model_width)
    normed = low(layer_norm(flat_rows, norm1_gain, norm1_shift))
    mixed_qkv = product(normed, w_qkv)
    queries = low_back(low(mixed_qkv[:, :model_width] + query_bias))
    key_rows = low_back(low(mixed_qkv[:, model_width:2 * model_width]))
    values = low_back(low(mixed_qkv[:, 2 * model_width:] + value_bias))
    head_shape = (clip_count, patches, HEADS, HEAD_DIM)
    attended = lax.map(lambda clip_group: clip_attention(clip_group[0], clip_group[1], clip_group[2], clip_group[3]), (queries.reshape(head_shape), key_rows.reshape(head_shape), values.reshape(head_shape), alive_mask))
    attended = low_back(low(attended.reshape(clip_count * patches, model_width)))
    branch = low_back(product(attended, w_proj) + proj_bias)
    hidden = flat_rows + branch
    normed2 = low(layer_norm(hidden, norm2_gain, norm2_shift))
    preactive = low_back(product(normed2, w_fc1) + fc1_bias)
    activated = low(jax.nn.gelu(preactive, approximate=False))
    branch2 = low_back(product(activated, w_fc2) + fc2_bias)
    keep_rows = alive_mask.astype(jnp.float32).reshape(clip_count * patches, 1)
    return (hidden + branch2) * keep_rows

def reference(tokens, out_grad, lengths, norm1_gain, norm1_shift, w_qkv, query_bias, value_bias, w_proj, proj_bias, norm2_gain, norm2_shift, w_fc1, fc1_bias, w_fc2, fc2_bias, moment, ema_decay):
    patches = FREQ * TIME
    frames = lax.broadcasted_iota(jnp.int32, (CLIPS, FREQ, TIME), 2)
    alive_mask = (frames < lengths.astype(jnp.int32)[:, None, None]).reshape(CLIPS, patches)
    inputs = tokens.astype(jnp.float32).reshape(CLIPS, patches, D)
    params = (norm1_gain.astype(jnp.float32), norm1_shift.astype(jnp.float32), w_qkv.astype(jnp.float32), query_bias.astype(jnp.float32), value_bias.astype(jnp.float32), w_proj.astype(jnp.float32), proj_bias.astype(jnp.float32), norm2_gain.astype(jnp.float32), norm2_shift.astype(jnp.float32), w_fc1.astype(jnp.float32), fc1_bias.astype(jnp.float32), w_fc2.astype(jnp.float32), fc2_bias.astype(jnp.float32))

    def apply(values, weights):
        return forward(values, alive_mask, *weights)
    result, pull_back = jax.vjp(apply, inputs, params)
    cotangent = out_grad.astype(jnp.float32).reshape(CLIPS * patches, D)
    input_part, weight_parts = pull_back(cotangent)
    mixed_out = result.astype(jnp.bfloat16).reshape(CLIPS, FREQ, TIME, D)
    input_grad = input_part.astype(jnp.bfloat16).reshape(CLIPS, FREQ, TIME, D)
    joined = jnp.concatenate([gradient.reshape(-1) for gradient in weight_parts])
    weight_grad = jnp.concatenate([joined, jnp.zeros((NPAD - NPARAM,), jnp.float32)])
    new_moment = ema_decay[0] * moment + (1.0 - ema_decay[0]) * weight_grad
    return (mixed_out, input_grad, weight_grad, new_moment)
```

```python
import functools
import math

import jax
import jax.numpy as jnp
from jax import lax
from jax.experimental import pallas as pl
from jax.experimental.pallas import tpu as pltpu
from jax.sharding import Mesh
from jax.sharding import PartitionSpec as P

HEADS = 12
HEAD_DIM = 64
GROUPS = 4
GROUP_HEADS = HEADS // GROUPS
PAIR = 2 * HEAD_DIM
EPSILON = 1e-06
NEGATIVE = -1e30
LOG2E = math.log2(math.e)
LN2 = math.log(2.0)
SCALE = HEAD_DIM**-0.5
VMEM_LIMIT = 60 * 2**20
BF16 = jnp.bfloat16
F32 = jnp.float32


def dot32(left, right, contract):
    return lax.dot_general(left, right, ((contract[:1], contract[1:]), ((), ())), preferred_element_type=F32)


def rows_of(kv_ref, block, times, freqs):
    late, early = block // times, block % times
    return jnp.concatenate([kv_ref[f, early, late, 0] for f in freqs], axis=0)


def attend_kernel(frames, full_ref, rest_ref, kv_ref, q_ref, low_ref, out_ref, lse_ref, acc, top, q_pad, scores, tops):
    clip = pl.program_id(0)
    freqs, times, _, _, part_rows, _ = kv_ref.shape
    pieces, _, width = q_ref.shape
    rows = freqs * part_rows
    full, rest = full_ref[clip], rest_ref[clip]
    for p in range(pieces):
        q_pad[:HEAD_DIM, p * width : (p + 1) * width] = q_ref[p]
    q_pad[HEAD_DIM:, :] = jnp.zeros((HEAD_DIM, pieces * width), BF16)
    acc[...] = jnp.zeros_like(acc)
    top[...] = jnp.full_like(top, NEGATIVE)
    ones = jnp.ones((16, rows), BF16)

    def load(block):
        return rows_of(kv_ref, block, times, range(freqs))

    def consume(pair, block_scores, block_top):
        old = top[...]
        new = jnp.maximum(old, block_top)
        probs = jnp.exp2(block_scores - new).astype(BF16)
        top[...] = new
        values = jnp.concatenate([pair.T[HEAD_DIM:], ones], axis=0)
        acc[...] = acc[...] * jnp.exp2(old - new) + dot32(values, probs, (1, 0))

    @pl.when(rest > 0)
    def _():
        pair = load(full)
        alive = lax.broadcasted_iota(jnp.int32, (rows, 1), 0) % frames < rest
        block_scores = jnp.where(alive, dot32(pair, q_pad[...], (1, 0)), NEGATIVE)
        consume(pair, block_scores, jnp.max(block_scores, axis=0, keepdims=True))

    def score(block, slot):
        block_scores = dot32(load(block), q_pad[...], (1, 0))
        scores[slot] = block_scores
        tops[slot] = jnp.max(block_scores, axis=0, keepdims=True)

    @pl.when(full > 0)
    def _():
        score(0, 0)

    def two_blocks(step, _):
        for slot in range(2):
            block = 2 * step + slot
            score(jnp.minimum(block + 1, full - 1), 1 - slot)
            consume(load(block), scores[slot], tops[slot])
        return 0

    lax.fori_loop(0, full // 2, two_blocks, 0)

    @pl.when(full % 2 == 1)
    def _():
        consume(load(full - 1), scores[0], tops[0])

    total = acc[HEAD_DIM : HEAD_DIM + 1, :]
    attended = acc[:HEAD_DIM, :] / total
    out_ref[0] = attended
    low = attended.astype(BF16)
    for p in range(pieces):
        low_ref[p] = low[:, p * width : (p + 1) * width]
    lse_ref[0] = top[...] + jnp.log2(total)


def attend(full, rest, kv, q, head, frames):
    freqs, times, lates, clips, part_rows, _ = kv.shape
    pieces, _, width = q.shape
    width //= clips
    queries = pieces * width
    rows = freqs * part_rows
    pairs = clips * rows * times * lates * queries
    return pl.pallas_call(
        functools.partial(attend_kernel, frames),
        grid_spec=pltpu.PrefetchScalarGridSpec(
            num_scalar_prefetch=2,
            grid=(clips,),
            in_specs=[
                pl.BlockSpec((freqs, times, lates, 1, part_rows, PAIR), lambda c, *_: (0, 0, 0, c, 0, 0)),
                pl.BlockSpec((pieces, HEAD_DIM, width), lambda c, *_: (0, head, c)),
            ],
            out_specs=[
                pl.BlockSpec((pieces, HEAD_DIM, width), lambda c, *_: (0, 0, c)),
                pl.BlockSpec((1, HEAD_DIM, queries), lambda c, *_: (c, 0, 0)),
                pl.BlockSpec((1, 1, queries), lambda c, *_: (c, 0, 0)),
            ],
            scratch_shapes=[
                pltpu.VMEM((HEAD_DIM + 16, queries), F32),
                pltpu.VMEM((1, queries), F32),
                pltpu.VMEM((PAIR, queries), BF16),
                pltpu.VMEM((2, rows, queries), F32),
                pltpu.VMEM((2, 1, queries), F32),
            ],
        ),
        out_shape=[
            jax.ShapeDtypeStruct((pieces, HEAD_DIM, clips * width), BF16),
            jax.ShapeDtypeStruct((clips, HEAD_DIM, queries), F32),
            jax.ShapeDtypeStruct((clips, 1, queries), F32),
        ],
        compiler_params=pltpu.CompilerParams(vmem_limit_bytes=VMEM_LIMIT),
        cost_estimate=pl.CostEstimate(flops=1024 * pairs, bytes_accessed=2 * kv.size, transcendentals=pairs),
    )(full, rest, kv, q)


def attend_back_kernel(
    frames, cuts, full_ref, rest_ref, kv_ref, q_ref, grad_ref, out_ref, lse_ref, back_kv_ref, back_q_ref,
    back_q, q_cols, grad_cols, q_rows, grad_rows, delta,
):
    clip = pl.program_id(0)
    freqs, times, lates, _, part_rows, _ = kv_ref.shape
    pieces, _, width = q_ref.shape
    rows = freqs * part_rows
    full, rest = full_ref[clip], rest_ref[clip]
    zero = jnp.zeros((HEAD_DIM, width), BF16)
    for p in range(pieces):
        cols = slice(p * width, (p + 1) * width)
        query = jnp.concatenate([q_ref[p], zero], axis=0)
        grad = jnp.concatenate([zero, grad_ref[p]], axis=0)
        q_cols[:, cols] = query
        grad_cols[:, cols] = grad
        q_rows[cols, :] = query.T
        grad_rows[cols, :] = grad.T
        delta[:, cols] = jnp.sum(grad_ref[p].astype(F32) * out_ref[0, :, cols], axis=0, keepdims=True)
    back_q[...] = jnp.zeros_like(back_q)
    cut = rows // cuts
    is_key = lax.broadcasted_iota(jnp.int32, (1, PAIR), 1) < HEAD_DIM
    factor = jnp.where(is_key, jnp.float32(LN2), jnp.float32(1.0))

    def step(block, masked):
        late, early = block // times, block % times
        all_pairs = rows_of(kv_ref, block, times, range(freqs))
        for k in range(cuts):
            pair = all_pairs[k * cut : (k + 1) * cut]
            probs = jnp.exp2(dot32(pair, q_cols[...], (1, 0)) - lse_ref[0])
            if masked:
                place = lax.broadcasted_iota(jnp.int32, (cut, 1), 0) + k * cut
                probs = jnp.where(place % frames < rest, probs, 0.0)
            back_probs = dot32(pair, grad_cols[...], (1, 0))
            back_scores = (probs * (back_probs - delta[...])).astype(BF16)
            back_pair = dot32(probs.astype(BF16), grad_rows[...], (1, 0)) + dot32(back_scores, q_rows[...], (1, 0))
            back_q[...] += dot32(pair, back_scores, (0, 0))
            low = (back_pair * factor).astype(BF16)
            if cut >= part_rows:
                for f in range(cut // part_rows):
                    low_part = low[f * part_rows : (f + 1) * part_rows]
                    back_kv_ref[k * (cut // part_rows) + f, early, late, 0] = low_part
            else:
                start = k * cut % part_rows
                back_kv_ref[k * cut // part_rows, early, late, 0, start : start + cut] = low
        return 0

    @pl.when(rest > 0)
    def _():
        step(full, True)

    lax.fori_loop(0, full, lambda block, _: step(block, False), 0)

    def clear(block, _):
        for f in range(freqs):
            back_kv_ref[f, block % times, block // times, 0] = jnp.zeros((part_rows, PAIR), BF16)
        return 0

    lax.fori_loop(full + (rest > 0).astype(jnp.int32), times * lates, clear, 0)
    for p in range(pieces):
        back_q_ref[p] = (back_q[:HEAD_DIM, p * width : (p + 1) * width] * SCALE).astype(BF16)


def attend_back(full, rest, kv, q, grad, out, lse, head, frames):
    freqs, times, lates, clips, part_rows, _ = kv.shape
    pieces, _, width = q.shape
    width //= clips
    queries = pieces * width
    rows = freqs * part_rows
    pairs = clips * rows * times * lates * queries
    kv_spec = pl.BlockSpec((freqs, times, lates, 1, part_rows, PAIR), lambda c, *_: (0, 0, 0, c, 0, 0))
    q_spec = pl.BlockSpec((pieces, HEAD_DIM, width), lambda c, *_: (0, head, c))
    return pl.pallas_call(
        functools.partial(attend_back_kernel, frames, 2),
        grid_spec=pltpu.PrefetchScalarGridSpec(
            num_scalar_prefetch=2,
            grid=(clips,),
            in_specs=[
                kv_spec,
                q_spec,
                q_spec,
                pl.BlockSpec((1, HEAD_DIM, queries), lambda c, *_: (c, 0, 0)),
                pl.BlockSpec((1, 1, queries), lambda c, *_: (c, 0, 0)),
            ],
            out_specs=[kv_spec, pl.BlockSpec((pieces, HEAD_DIM, width), lambda c, *_: (0, 0, c))],
            scratch_shapes=[
                pltpu.VMEM((PAIR, queries), F32),
                pltpu.VMEM((PAIR, queries), BF16),
                pltpu.VMEM((PAIR, queries), BF16),
                pltpu.VMEM((queries, PAIR), BF16),
                pltpu.VMEM((queries, PAIR), BF16),
                pltpu.VMEM((1, queries), F32),
            ],
        ),
        out_shape=[
            jax.ShapeDtypeStruct(kv.shape, BF16),
            jax.ShapeDtypeStruct((pieces, HEAD_DIM, clips * width), BF16),
        ],
        compiler_params=pltpu.CompilerParams(vmem_limit_bytes=VMEM_LIMIT),
        cost_estimate=pl.CostEstimate(flops=2560 * pairs, bytes_accessed=4 * kv.size, transcendentals=pairs),
    )(full, rest, kv, q, grad, out, lse)


def layer_norm(values, scaling, offset):
    row_mean = jnp.mean(values, axis=-1, keepdims=True)
    centred = values - row_mean
    spread = jnp.mean(centred * centred, axis=-1, keepdims=True)
    return centred * lax.rsqrt(spread + EPSILON) * scaling + offset


def gelu_exact(values):
    return jax.nn.gelu(values, approximate=False)


def to_groups(values):
    return lax.all_to_all(values, "g", 0, 0, tiled=True)


def per_device(
    tokens,
    out_grad,
    lengths,
    norm1_gain,
    norm1_shift,
    w_qkv,
    query_bias,
    value_bias,
    w_proj,
    proj_bias,
    norm2_gain,
    norm2_shift,
    w_fc1,
    fc1_bias,
    w_fc2,
    fc2_bias,
    moment,
    ema_decay,
):
    clips, freq_rows, frames, width = tokens.shape
    part = freq_rows * frames
    rows = clips * part
    freqs, times = lax.axis_size("f"), lax.axis_size("t")
    lates = GROUPS
    plane = ("f", "t")
    devices = freqs * times * lates
    time_index = lax.axis_index("g") * times + lax.axis_index("t")
    frame = time_index * frames + lax.broadcasted_iota(jnp.int32, (1, freq_rows, frames), 2)
    keep_rows = (frame < lengths[:, None, None]).astype(F32).reshape(rows, 1)
    full, rest = lengths // frames, lengths % frames

    def pack(values):
        if part % 128 == 0:
            return values
        values = values.reshape(lates, -1, clips, part).transpose(1, 2, 0, 3)
        return values.reshape(1, -1, clips * lates * part)

    def unpack(values):
        if part % 128 == 0:
            return values
        values = values.reshape(-1, clips, lates, part).transpose(2, 0, 1, 3)
        return values.reshape(lates, -1, rows)

    inputs = tokens.astype(F32).reshape(rows, width)
    normed, norm1_pull = jax.vjp(layer_norm, inputs, norm1_gain, norm1_shift)
    normed_low = normed.astype(BF16)
    w_q = w_qkv[:, :width]
    head_dims = (width, GROUPS, GROUP_HEADS, HEAD_DIM)
    w_kv = jnp.stack([w_qkv[:, width : 2 * width].reshape(head_dims), w_qkv[:, 2 * width :].reshape(head_dims)], axis=3)
    w_kv = w_kv.reshape(width, 2 * width)
    kv_bias = jnp.stack([jnp.zeros((HEADS, HEAD_DIM), F32), value_bias.reshape(HEADS, HEAD_DIM)], axis=1).reshape(2 * width)
    queries = ((dot32(w_q, normed_low, (0, 1)) + query_bias[:, None]) * (SCALE * LOG2E)).astype(BF16)
    pairs = (dot32(normed_low, w_kv, (1, 0)) + kv_bias).astype(BF16)
    pairs = pairs.reshape(rows, GROUPS, GROUP_HEADS, PAIR).transpose(2, 1, 0, 3)
    pairs = pairs.reshape(GROUP_HEADS, GROUPS, clips, part, PAIR)
    q = pack(to_groups(queries.reshape(GROUPS, -1, rows)))
    kv, attended, kept = [], [], []
    for head in range(GROUP_HEADS):
        mine = to_groups(pairs[head])
        mine = lax.all_gather(mine, plane, axis=0, tiled=False).reshape(freqs, times, lates, clips, part, PAIR)
        kv.append(mine)
    for head in range(GROUP_HEADS):
        low, out, lse = attend(full, rest, kv[head], q, head, frames)
        attended.append(low)
        kept.append((out, lse))
    attended_low = to_groups(unpack(jnp.concatenate(attended, axis=1))).reshape(width, rows)
    branch = dot32(attended_low, w_proj, (0, 0)) + proj_bias
    hidden = inputs + branch
    normed2, norm2_pull = jax.vjp(layer_norm, hidden, norm2_gain, norm2_shift)
    normed2_low = normed2.astype(BF16)
    preactive = dot32(normed2_low, w_fc1, (1, 0)) + fc1_bias
    activated, gelu_pull = jax.vjp(gelu_exact, preactive)
    activated_low = activated.astype(BF16)
    branch2 = dot32(activated_low, w_fc2, (1, 0)) + fc2_bias
    block_out = ((hidden + branch2) * keep_rows).astype(BF16).reshape(tokens.shape)
    grad_out = out_grad.astype(F32).reshape(rows, width) * keep_rows
    back_branch2 = grad_out.astype(BF16)
    grad_fc2_bias = jnp.sum(back_branch2.astype(F32), axis=0)
    grad_fc2 = dot32(activated_low, back_branch2, (0, 0))
    back_activated = dot32(back_branch2, w_fc2, (1, 1))
    back_preactive = gelu_pull(back_activated)[0].astype(BF16)
    grad_fc1_bias = jnp.sum(back_preactive.astype(F32), axis=0)
    grad_fc1 = dot32(normed2_low, back_preactive, (0, 0))
    back_normed2 = dot32(back_preactive, w_fc1, (1, 1))
    back_hidden_norm, grad_norm2_gain, grad_norm2_shift = norm2_pull(back_normed2)
    back_hidden = grad_out + back_hidden_norm
    back_branch = back_hidden.astype(BF16)
    grad_proj_bias = jnp.sum(back_branch.astype(F32), axis=0)
    grad_proj = dot32(attended_low, back_branch, (1, 0))
    back_attended = dot32(w_proj, back_branch, (1, 1)).astype(BF16)
    grad = pack(to_groups(back_attended.reshape(GROUPS, -1, rows)))
    back_pairs, back_queries = [], []
    for head in range(GROUP_HEADS):
        out, lse = kept[head]
        back_kv, back_q = attend_back(full, rest, kv[head], q, grad, out, lse, head, frames)
        back_queries.append(back_q)
        back_kv = back_kv.reshape(freqs * times, lates, clips, part, PAIR)
        back_kv = lax.psum_scatter(back_kv, plane, scatter_dimension=0, tiled=False)
        back_pairs.append(to_groups(back_kv))
    back_q = to_groups(unpack(jnp.concatenate(back_queries, axis=1))).reshape(width, rows)
    back_kv = jnp.stack(back_pairs).transpose(2, 3, 1, 0, 4).reshape(rows, 2 * width)
    grad_query_bias = jnp.sum(back_q.astype(F32), axis=1)
    grad_kv_bias = jnp.sum(back_kv.astype(F32), axis=0)
    grad_value_bias = grad_kv_bias.reshape(HEADS, 2, HEAD_DIM)[:, 1].reshape(width)
    grad_q = dot32(normed_low, back_q, (0, 1))
    grad_kv = dot32(normed_low, back_kv, (0, 0)).reshape(width, HEADS, 2, HEAD_DIM)
    grad_qkv = jnp.concatenate([grad_q, grad_kv[:, :, 0].reshape(width, width), grad_kv[:, :, 1].reshape(width, width)], axis=1)
    back_normed = dot32(back_q, w_q, (0, 1)) + dot32(back_kv, w_kv, (1, 1))
    back_input_norm, grad_norm1_gain, grad_norm1_shift = norm1_pull(back_normed)
    input_grad = (back_hidden + back_input_norm).astype(BF16).reshape(tokens.shape)
    joined = jnp.concatenate(
        [
            grad_norm1_gain,
            grad_norm1_shift,
            grad_qkv.reshape(-1),
            grad_query_bias,
            grad_value_bias,
            grad_proj.reshape(-1),
            grad_proj_bias,
            grad_norm2_gain,
            grad_norm2_shift,
            grad_fc1.reshape(-1),
            grad_fc1_bias,
            grad_fc2.reshape(-1),
            grad_fc2_bias,
        ]
    ).astype(BF16)
    padding = moment.shape[0] * devices - joined.shape[0]
    joined = jnp.concatenate([joined, jnp.zeros((padding,), BF16)])
    weight_grad = lax.psum_scatter(joined, ("f", "g", "t"), scatter_dimension=0, tiled=True).astype(F32)
    new_moment = ema_decay[0] * moment + (1.0 - ema_decay[0]) * weight_grad
    return (block_out, input_grad, weight_grad, new_moment)


def solution(mesh):
    freqs, times = mesh.shape["freq"], mesh.shape["tm"]
    fine = Mesh(mesh.devices.reshape(freqs, GROUPS, times // GROUPS), ("f", "g", "t"))
    patches = P(None, "f", ("g", "t"), None)
    flat = P(("f", "g", "t"))
    return jax.shard_map(
        per_device,
        mesh=fine,
        in_specs=(patches, patches) + (P(),) * 14 + (flat, P()),
        out_specs=(patches, patches, flat, flat),
        check_vma=False,
    )
```

```python
import functools
import math

import jax
import jax.numpy as jnp
from jax import lax
from jax.experimental import pallas as pl
from jax.experimental.pallas import tpu as pltpu
from jax.sharding import Mesh
from jax.sharding import PartitionSpec as P

HEADS = 12
HEAD_DIM = 64
GROUPS = 4
GROUP_HEADS = HEADS // GROUPS
PAIR = 2 * HEAD_DIM
LANES = 128
OUT_ROWS = HEAD_DIM + 8
GRAD_ROWS = HEAD_DIM + 16
EPSILON = 1e-06
NEGATIVE = -1e30
LOG2E = math.log2(math.e)
LN2 = math.log(2.0)
SCALE = HEAD_DIM**-0.5
VMEM_LIMIT = 60 * 2**20
BF16 = jnp.bfloat16
F32 = jnp.float32


def dot32(left, right, contract):
    return lax.dot_general(left, right, ((contract[:1], contract[1:]), ((), ())), preferred_element_type=F32)


def work(info_ref, clip, times):
    t, full, rest = info_ref[1], info_ref[2 + 2 * clip], info_ref[3 + 2 * clip]
    live = full + (rest > 0).astype(jnp.int32)
    query_blocks = (live + times - 1) // times
    key_blocks = jnp.maximum(full - t + times - 1, 0) // times
    partial = (rest > 0) & (full % times == t)
    return query_blocks, key_blocks, partial, rest


def joined(ref, late):
    tiles = [ref[late, j] for j in range(ref.shape[1])]
    return tiles[0] if len(tiles) == 1 else jnp.concatenate(tiles, axis=1)


def load_pairs(kv_refs, slot):
    return [ref[f, slot, 0] for ref in kv_refs for f in range(ref.shape[0])]


def attend_kernel(clip, times, frames, n_kv, n_q, n_out, info_ref, *refs):
    kv_refs, q_refs, refs = refs[:n_kv], refs[n_kv : n_kv + n_q], refs[n_kv + n_q :]
    refs = refs[-n_out - 5 :]
    out_refs, (acc, top, q_pad, scores, tops) = refs[:n_out], refs[n_out:]
    query_blocks, key_blocks, partial, rest = work(info_ref, clip, times)
    width = q_refs[0].shape[1] * q_refs[0].shape[3]
    rows = scores.shape[1]
    for late in range(GROUPS):
        for p, ref in enumerate(q_refs):
            q_pad[late, :HEAD_DIM, p * width : (p + 1) * width] = joined(ref, late)
        q_pad[late, HEAD_DIM:, :] = jnp.zeros((HEAD_DIM, q_pad.shape[2]), BF16)
    acc[...] = jnp.zeros_like(acc)
    top[...] = jnp.full_like(top, NEGATIVE)
    ones = jnp.ones((16, rows), BF16)

    def load(block):
        return jnp.concatenate(load_pairs(kv_refs, block), axis=0)

    def consume(u, pair, block_scores, block_top):
        old = top[u]
        new = jnp.maximum(old, block_top)
        probs = jnp.exp2(block_scores - new).astype(BF16)
        top[u] = new
        values = jnp.concatenate([pair.T[HEAD_DIM:], ones], axis=0)
        acc[u] = acc[u] * jnp.exp2(old - new) + dot32(values, probs, (1, 0))

    def masked(u, _):
        pair = load(key_blocks)
        alive = lax.broadcasted_iota(jnp.int32, (rows, 1), 0) % frames < rest
        block_scores = jnp.where(alive, dot32(pair, q_pad[u], (1, 0)), NEGATIVE)
        consume(u, pair, block_scores, jnp.max(block_scores, axis=0, keepdims=True))
        return 0

    lax.fori_loop(0, jnp.where(partial, query_blocks, 0), masked, 0)
    total = query_blocks * key_blocks
    per = jnp.maximum(key_blocks, 1)

    def score(step, slot):
        block_scores = dot32(load(step % per), q_pad[step // per], (1, 0))
        scores[slot] = block_scores
        tops[slot] = jnp.max(block_scores, axis=0, keepdims=True)

    @pl.when(total > 0)
    def _():
        score(0, 0)

    def two_steps(double, _):
        for slot in range(2):
            step = 2 * double + slot
            score(jnp.minimum(step + 1, total - 1), 1 - slot)
            consume(step // per, load(step % per), scores[slot], tops[slot])
        return 0

    lax.fori_loop(0, total // 2, two_steps, 0)

    @pl.when(total % 2 == 1)
    def _():
        consume((total - 1) // per, load((total - 1) % per), scores[0], tops[0])

    for late in range(GROUPS):
        norm = acc[late, HEAD_DIM : HEAD_DIM + 1, :]
        some = norm > 0.0
        safe = jnp.where(some, norm, 1.0)
        out = acc[late, :HEAD_DIM, :] / safe
        lse = jnp.where(some, top[late] + jnp.log2(safe), NEGATIVE)
        p = 0
        for ref in out_refs:
            for part in range(ref.shape[0]):
                cols = slice(p * width, (p + 1) * width)
                ref[part, late, :HEAD_DIM, :] = out[:, cols]
                ref[part, late, HEAD_DIM:, :] = jnp.broadcast_to(lse[:, cols], (OUT_ROWS - HEAD_DIM, width))
                p += 1


def specs_of(kv, q, clip, clips):
    kv_specs = [pl.BlockSpec((a.shape[0], GROUPS, 1, *a.shape[3:]), lambda i, *_: (0, 0, clip, 0, 0)) for a in kv]
    _, tiles, _, lanes = q[0].shape
    q_specs = [pl.BlockSpec((GROUPS, tiles // clips, HEAD_DIM, lanes), lambda i, *_: (0, clip, 0, 0)) for a in q]
    return kv_specs, q_specs, tiles * lanes // clips


def attend(info, kv, q, clip, clips, times, frames, parts, before, after):
    kv_specs, q_specs, width = specs_of(kv, q, clip, clips)
    queries = len(q) * width
    rows = sum(a.shape[0] for a in kv) * kv[0].shape[3]
    pairs = GROUPS * rows * GROUPS * queries
    out_specs = [pl.BlockSpec((n, GROUPS, OUT_ROWS, width), lambda i, *_: (0, 0, 0, clip)) for n in parts]
    n_in = 1 + len(kv) + len(q)
    return pl.pallas_call(
        functools.partial(attend_kernel, clip, times, frames, len(kv), len(q), len(parts)),
        grid_spec=pltpu.PrefetchScalarGridSpec(
            num_scalar_prefetch=1,
            grid=(1,),
            in_specs=kv_specs + q_specs + [pl.BlockSpec(memory_space=pl.ANY)] * (len(before) + len(after)),
            out_specs=out_specs,
            scratch_shapes=[
                pltpu.VMEM((GROUPS, GRAD_ROWS, queries), F32),
                pltpu.VMEM((GROUPS, 1, queries), F32),
                pltpu.VMEM((GROUPS, PAIR, queries), BF16),
                pltpu.VMEM((2, rows, queries), F32),
                pltpu.VMEM((2, 1, queries), F32),
            ],
        ),
        out_shape=[jax.ShapeDtypeStruct((n, GROUPS, OUT_ROWS, clips * width), F32) for n in parts],
        input_output_aliases={n_in + i: i for i in range(len(before))},
        compiler_params=pltpu.CompilerParams(vmem_limit_bytes=VMEM_LIMIT),
        cost_estimate=pl.CostEstimate(flops=256 * pairs, bytes_accessed=pairs // 16, transcendentals=pairs),
    )(info, *kv, *q, *before, *after)


def attend_back_kernel(clip, times, frames, cuts, n_kv, n_q, n_out, info_ref, *refs):
    kv_refs, q_refs, grad_refs = refs[:n_kv], refs[n_kv : n_kv + n_q], refs[n_kv + n_q : n_kv + 2 * n_q]
    refs = refs[-n_out - n_kv - 8 :]
    back_q_refs, back_kv_refs, refs = refs[:n_out], refs[n_out : n_out + n_kv], refs[n_out + n_kv :]
    back_q, back_kv, q_cols, grad_cols, q_rows, grad_rows, lse, delta = refs
    query_blocks, key_blocks, partial, rest = work(info_ref, clip, times)
    width = grad_refs[0].shape[-1]
    part_rows = kv_refs[0].shape[3]
    rows = back_kv.shape[1]
    cut = rows // cuts
    zero = jnp.zeros((HEAD_DIM, width), BF16)

    def prepare(late, _):
        for p, (q_ref, grad_ref) in enumerate(zip(q_refs, grad_refs)):
            cols = slice(p * width, (p + 1) * width)
            query = jnp.concatenate([joined(q_ref, late), zero], axis=0)
            grad = jnp.concatenate([zero, grad_ref[late, :HEAD_DIM]], axis=0)
            q_cols[late, :, cols] = query
            grad_cols[late, :, cols] = grad
            q_rows[late, cols, :] = query.T
            grad_rows[late, cols, :] = grad.T
            extra = grad_ref[late, HEAD_DIM:].astype(F32)
            lse[late, :, cols] = extra[0:1] + extra[1:2] + extra[2:3]
            delta[late, :, cols] = extra[3:4] + extra[4:5] + extra[5:6]
        return 0

    lax.fori_loop(0, query_blocks, prepare, 0)
    back_q[...] = jnp.zeros_like(back_q)
    back_kv[...] = jnp.zeros_like(back_kv)

    def step(u, block, masked):
        pairs = load_pairs(kv_refs, block)
        for k in range(cuts):
            part = pairs[k * len(pairs) // cuts : (k + 1) * len(pairs) // cuts]
            pair = part[0] if len(part) == 1 else jnp.concatenate(part, axis=0)
            probs = jnp.exp2(dot32(pair, q_cols[u], (1, 0)) - lse[u])
            if masked:
                row = lax.broadcasted_iota(jnp.int32, (cut, 1), 0)
                probs = jnp.where(row % frames < rest, probs, 0.0)
            back_probs = dot32(pair, grad_cols[u], (1, 0))
            back_scores = (probs * (back_probs - delta[u])).astype(BF16)
            back_pair = dot32(probs.astype(BF16), grad_rows[u], (1, 0)) + dot32(back_scores, q_rows[u], (1, 0))
            back_q[u] += dot32(pair, back_scores, (0, 0))
            back_kv[block, k * cut : (k + 1) * cut, :] += back_pair
        return 0

    lax.fori_loop(0, jnp.where(partial, query_blocks, 0), lambda u, _: step(u, key_blocks, True), 0)
    per = jnp.maximum(key_blocks, 1)
    lax.fori_loop(0, query_blocks * key_blocks, lambda i, _: step(i // per, i % per, False), 0)
    is_key = lax.broadcasted_iota(jnp.int32, (1, PAIR), 1) < HEAD_DIM
    factor = jnp.where(is_key, jnp.float32(LN2), jnp.float32(1.0))
    for late in range(GROUPS):
        p = 0
        for ref in back_q_refs:
            for part in range(ref.shape[0]):
                cols = slice(p * width, (p + 1) * width)
                ref[part, late] = (back_q[late, :HEAD_DIM, cols] * SCALE).astype(BF16)
                p += 1
        p = 0
        for ref in back_kv_refs:
            for f in range(ref.shape[0]):
                ref[f, late, 0] = (back_kv[late, p * part_rows : (p + 1) * part_rows, :] * factor).astype(BF16)
                p += 1


def attend_back(info, kv, q, grad, clip, clips, times, frames, parts, before, after):
    kv_specs, q_specs, width = specs_of(kv, q, clip, clips)
    queries = len(q) * width
    rows = sum(a.shape[0] for a in kv) * kv[0].shape[3]
    pairs = GROUPS * rows * GROUPS * queries
    grad_specs = [pl.BlockSpec((GROUPS, GRAD_ROWS, width), lambda i, *_: (0, 0, clip)) for a in grad]
    q_out = [pl.BlockSpec((n, GROUPS, HEAD_DIM, width), lambda i, *_: (0, 0, 0, clip)) for n in parts]
    n_in = 1 + len(kv) + len(q) + len(grad)
    return pl.pallas_call(
        functools.partial(attend_back_kernel, clip, times, frames, 2, len(kv), len(q), len(parts)),
        grid_spec=pltpu.PrefetchScalarGridSpec(
            num_scalar_prefetch=1,
            grid=(1,),
            in_specs=kv_specs + q_specs + grad_specs + [pl.BlockSpec(memory_space=pl.ANY)] * (len(before) + len(after)),
            out_specs=q_out + kv_specs,
            scratch_shapes=[
                pltpu.VMEM((GROUPS, PAIR, queries), F32),
                pltpu.VMEM((GROUPS, rows, PAIR), F32),
                pltpu.VMEM((GROUPS, PAIR, queries), BF16),
                pltpu.VMEM((GROUPS, PAIR, queries), BF16),
                pltpu.VMEM((GROUPS, queries, PAIR), BF16),
                pltpu.VMEM((GROUPS, queries, PAIR), BF16),
                pltpu.VMEM((GROUPS, 1, queries), F32),
                pltpu.VMEM((GROUPS, 1, queries), F32),
            ],
        ),
        out_shape=[jax.ShapeDtypeStruct((n, GROUPS, HEAD_DIM, clips * width), BF16) for n in parts]
        + [jax.ShapeDtypeStruct(a.shape, BF16) for a in kv],
        input_output_aliases={n_in + i: i for i in range(len(before))},
        compiler_params=pltpu.CompilerParams(vmem_limit_bytes=VMEM_LIMIT),
        cost_estimate=pl.CostEstimate(flops=640 * pairs, bytes_accessed=pairs // 8, transcendentals=pairs),
    )(info, *kv, *q, *grad, *before, *after)


def thirds(values):
    high = values.astype(BF16).astype(F32)
    middle = (values - high).astype(BF16).astype(F32)
    return jnp.concatenate([high, middle, values - high - middle], axis=0)


def blend(left, left_lse, right, right_lse):
    most = jnp.maximum(left_lse, right_lse)
    left_part, right_part = jnp.exp2(left_lse - most), jnp.exp2(right_lse - most)
    total = left_part + right_part
    return (left * left_part + right * right_part) / total, most + jnp.log2(total)


def merge_cores_kernel(kept_ref, came_ref, mine_ref, sent_ref):
    for n in range(GROUPS):
        for part in range(2):
            left, right = kept_ref[part, n], came_ref[part, n]
            out, lse = blend(left[:HEAD_DIM], left[HEAD_DIM : HEAD_DIM + 1], right[:HEAD_DIM], right[HEAD_DIM : HEAD_DIM + 1])
            if part == 0:
                mine_ref[n, :HEAD_DIM] = out
                mine_ref[n, HEAD_DIM:] = jnp.broadcast_to(lse, (OUT_ROWS - HEAD_DIM, out.shape[1]))
            else:
                fill = jnp.zeros((GRAD_ROWS - HEAD_DIM - 3, out.shape[1]), F32)
                sent_ref[n] = jnp.concatenate([out, thirds(lse), fill], axis=0).astype(BF16)


def merge_cores(kept, came):
    _, _, _, width = kept.shape
    return pl.pallas_call(
        merge_cores_kernel,
        out_shape=[jax.ShapeDtypeStruct((GROUPS, OUT_ROWS, width), F32), jax.ShapeDtypeStruct((GROUPS, GRAD_ROWS, width), BF16)],
        compiler_params=pltpu.CompilerParams(vmem_limit_bytes=VMEM_LIMIT),
    )(kept, came)


def merge_chips_kernel(mine_ref, came_ref, out_ref, low_ref):
    for n in range(GROUPS):
        left, right = mine_ref[n], came_ref[n].astype(F32)
        right_lse = right[HEAD_DIM : HEAD_DIM + 1] + right[HEAD_DIM + 1 : HEAD_DIM + 2] + right[HEAD_DIM + 2 : HEAD_DIM + 3]
        out, lse = blend(left[:HEAD_DIM], left[HEAD_DIM : HEAD_DIM + 1], right[:HEAD_DIM], right_lse)
        low_ref[n] = out.astype(BF16)
        out_ref[n, :HEAD_DIM] = out
        out_ref[n, HEAD_DIM:] = jnp.broadcast_to(lse, (OUT_ROWS - HEAD_DIM, out.shape[1]))


def merge_chips(mine, came):
    _, _, width = mine.shape
    return pl.pallas_call(
        merge_chips_kernel,
        out_shape=[jax.ShapeDtypeStruct((GROUPS, OUT_ROWS, width), F32)] + [jax.ShapeDtypeStruct((GROUPS, HEAD_DIM, width), BF16)],
        compiler_params=pltpu.CompilerParams(vmem_limit_bytes=VMEM_LIMIT),
    )(mine, came)


def grad_rows_kernel(grad_ref, *refs):
    out_refs, ready_refs = refs[:GROUP_HEADS], refs[-GROUP_HEADS:]
    for head in range(GROUP_HEADS):
        for n in range(GROUPS):
            grad = grad_ref[n, head * HEAD_DIM : (head + 1) * HEAD_DIM].astype(F32)
            out = out_refs[head][n]
            delta = jnp.sum(grad * out[:HEAD_DIM], axis=0, keepdims=True)
            fill = jnp.zeros((GRAD_ROWS - HEAD_DIM - 6, grad.shape[1]), F32)
            rows = jnp.concatenate([grad, thirds(out[HEAD_DIM : HEAD_DIM + 1]), thirds(delta), fill], axis=0)
            ready_refs[head][n] = rows.astype(BF16)


def grad_rows_of(grad, outs, after):
    width = grad.shape[-1]
    whole = pl.BlockSpec(memory_space=pltpu.VMEM)
    return pl.pallas_call(
        grad_rows_kernel,
        in_specs=[whole] * (1 + len(outs)) + [pl.BlockSpec(memory_space=pl.ANY)],
        out_shape=[jax.ShapeDtypeStruct((GROUPS, GRAD_ROWS, width), BF16)] * GROUP_HEADS,
        compiler_params=pltpu.CompilerParams(vmem_limit_bytes=VMEM_LIMIT),
    )(grad, *outs, after)


def sum_back_kernel(kept_ref, came_ref, q_kept_ref, q_came_ref, ready_ref):
    rows = kept_ref.shape[1]
    for n in range(GROUPS):
        ready_ref[n, :rows] = (kept_ref[n].astype(F32) + came_ref[n].astype(F32)).astype(BF16)
        query = (q_kept_ref[n].astype(F32) + q_came_ref[n].astype(F32)).astype(BF16)
        for j in range(rows // LANES):
            at = rows + j * HEAD_DIM
            ready_ref[n, at : at + HEAD_DIM] = query[:, j * LANES : (j + 1) * LANES]


def sum_back(kept, came, q_kept, q_came):
    groups, rows, _ = kept.shape
    return pl.pallas_call(
        sum_back_kernel,
        out_shape=jax.ShapeDtypeStruct((groups, rows + rows // LANES * HEAD_DIM, LANES), BF16),
        compiler_params=pltpu.CompilerParams(vmem_limit_bytes=VMEM_LIMIT),
    )(kept, came, q_kept, q_came)


def spread(lines, at, stride, values):
    rows, width = values.shape
    for piece in range(width // LANES):
        lines[pl.ds(at + piece, rows, stride=stride), :] = values[:, piece * LANES : (piece + 1) * LANES]


def write_window(start, lines, ref, at=0):
    skip = start % 8
    rows = ref.shape[1]
    base = pl.multiple_of(start - skip, 8)
    for s in range(8):

        @pl.when(skip == s)
        def _():
            ref[at] = lines[pl.ds(base, rows + 8), :][s : s + rows].astype(BF16)


def pack_early_kernel(size, first, att_ref, branch_ref, normed_ref, pre_ref, act_ref, out_ref, vec_ref, window_ref, lines):
    step = pl.program_id(0)

    @pl.when(step == 0)
    def _():
        width = branch_ref.shape[1]
        blocks = pre_ref.shape[1] // width
        per = width // LANES
        spread(lines, 0, per, dot32(att_ref[...], branch_ref[...], (1, 0)))
        at = width * per
        lines[at : at + 3 * per, :] = vec_ref[0 : 3 * per]
        at += 3 * per
        for b in range(blocks):
            cols = slice(b * width, (b + 1) * width)
            spread(lines, at + b * per, blocks * per, dot32(normed_ref[...], pre_ref[:, cols], (0, 0)))
        at += blocks * width * per
        lines[at : at + blocks * per, :] = vec_ref[3 * per : (3 + blocks) * per]
        at += blocks * per
        for b in range(blocks):
            cols = slice(b * width, (b + 1) * width)
            spread(lines, at + b * width * per, per, dot32(act_ref[:, cols], out_ref[...], (0, 0)))
        at += blocks * width * per
        lines[at : at + per, :] = vec_ref[(3 + blocks) * per :]
        lines[at + per :, :] = jnp.zeros((lines.shape[0] - at - per, LANES), F32)

    @pl.when(step < first)
    def _():
        window_ref[...] = jnp.zeros_like(window_ref)

    @pl.when(step >= first)
    def _():
        write_window((step - first) * size, lines, window_ref)


def pack_early(devices, size, *operands):
    chunks = devices - LATE_CHUNKS
    whole = [pl.BlockSpec(a.shape, lambda j: (0, 0)) for a in operands]
    entries = chunks * size * LANES
    return pl.pallas_call(
        functools.partial(pack_early_kernel, size, LATE_CHUNKS),
        grid=(devices,),
        in_specs=whole,
        out_specs=pl.BlockSpec((1, EARLY_WINDOW, LANES), lambda j: (j, 0, 0)),
        scratch_shapes=[pltpu.VMEM((-(-(chunks - 1) * size // 8) * 8 + EARLY_WINDOW + 8, LANES), F32)],
        out_shape=jax.ShapeDtypeStruct((devices, EARLY_WINDOW, LANES), BF16),
        compiler_params=pltpu.CompilerParams(vmem_limit_bytes=VMEM_LIMIT),
        cost_estimate=pl.CostEstimate(flops=1024 * entries, bytes_accessed=4 * entries, transcendentals=0),
    )(*operands)


SWAP = [(0, 1), (1, 0)]


def swap(values, axis):
    return lax.ppermute(values, axis, SWAP)


def add(left, right):
    return (left.astype(F32) + right.astype(F32)).astype(BF16)


def trade(values, dim, keep, axis):
    sent = lax.dynamic_index_in_dim(values, 1 - keep, dim, keepdims=False)
    kept = lax.dynamic_index_in_dim(values, keep, dim, keepdims=False)
    return add(kept, swap(sent, axis))


EARLY_WINDOW = 1744
LATE_CHUNKS = 8
LATE_WINDOW = 1792


def reduce_late(send, keep):
    f, g, x = lax.axis_index("f"), lax.axis_index("g"), lax.axis_index("x")
    pairs = add(keep, swap(send, "c")).reshape(2, 2, 4, -1, LANES)
    first = trade(trade(pairs[:, :, :2], 1, x, "x"), 1, f, "f")
    second = trade(trade(pairs[:, :, 2:], 2, f, "f"), 1, x, "x")
    mine = jnp.concatenate([first, second], axis=1)
    low = jnp.minimum(g, 1)
    near = add(mine, lax.ppermute(mine, "g", [(3, 2)]))
    far = lax.ppermute(near, "g", [(2, 1)])
    mine = jnp.where(g == 1, add(mine, far), mine)
    sent = lax.dynamic_index_in_dim(mine, 1 - low, 0, keepdims=False)
    mine = lax.dynamic_index_in_dim(mine, low, 0, keepdims=False)
    mine = add(mine, lax.ppermute(sent, "g", SWAP))
    far = swap(mine, "f")
    part = LATE_WINDOW // 4
    return jnp.concatenate([mine[:part], far[:part], mine[part:], far[part:]], axis=0).astype(F32)


def own_chunk(early, late, size):
    is_late = (lax.axis_index("f") == 0) & (lax.axis_index("g") < 2)
    return jnp.where(is_late, late[: size // LANES], early[: size // LANES]).reshape(size)


def centre(values):
    centred = values - jnp.mean(values, axis=-1, keepdims=True)
    scale = lax.rsqrt(jnp.mean(centred * centred, axis=-1, keepdims=True) + EPSILON)
    return centred * scale, scale


def centre_back(grad, unit, scale):
    mean = jnp.mean(grad, axis=-1, keepdims=True)
    along = jnp.mean(grad * unit, axis=-1, keepdims=True)
    return scale * (grad - mean - unit * along)


def row(ref):
    return ref[...].reshape(1, -1)


def swap_halves(values):
    return pltpu.roll(values, HEAD_DIM, axis=1)


def start_kernel(info_ref, x_ref, gain_ref, shift_ref, w_ref, query_bias_ref, value_bias_ref, *refs):
    rows, width = x_ref.shape

    def put(head, values):
        refs[head % GROUP_HEADS][head // GROUP_HEADS, :rows] = values.astype(BF16)

    unit, _ = centre(x_ref[...].astype(F32))
    normed = (unit * row(gain_ref) + row(shift_ref)).astype(BF16)
    keys = dot32(normed, w_ref[:, width : 2 * width], (1, 0))
    values = dot32(normed, w_ref[:, 2 * width :], (1, 0)) + row(value_bias_ref)
    is_key = lax.broadcasted_iota(jnp.int32, (1, PAIR), 1) < HEAD_DIM
    for j in range(HEADS // 2):
        key, value = keys[:, j * PAIR : (j + 1) * PAIR], values[:, j * PAIR : (j + 1) * PAIR]
        put(2 * j, jnp.where(is_key, key, swap_halves(value)))
        put(2 * j + 1, jnp.where(is_key, swap_halves(key), value))
    query = (dot32(normed, w_ref[:, :width], (1, 0)) + row(query_bias_ref)) * (SCALE * LOG2E)
    query = query.astype(BF16).T
    for head in range(HEADS):
        part = query[head * HEAD_DIM : (head + 1) * HEAD_DIM]
        for tile in range(rows // LANES):
            at = rows + tile * HEAD_DIM
            refs[head % GROUP_HEADS][head // GROUP_HEADS, at : at + HEAD_DIM] = part[:, tile * LANES : (tile + 1) * LANES]


def one_step(kernel, info, operands, shapes, scratch, flops):
    return pl.pallas_call(
        kernel,
        grid_spec=pltpu.PrefetchScalarGridSpec(
            num_scalar_prefetch=1,
            grid=(1,),
            in_specs=[pl.BlockSpec(a.shape, lambda i, *_, n=a.ndim: (0,) * n) for a in operands],
            out_specs=[pl.BlockSpec(a.shape, lambda i, *_, n=len(a.shape): (0,) * n) for a in shapes],
            scratch_shapes=scratch,
        ),
        out_shape=shapes,
        compiler_params=pltpu.CompilerParams(vmem_limit_bytes=VMEM_LIMIT),
        cost_estimate=pl.CostEstimate(flops=flops, bytes_accessed=flops // 500, transcendentals=0),
    )(info, *operands)


def start(info, x, gain, shift, w_qkv, query_bias, value_bias):
    rows, width = x.shape
    shapes = [jax.ShapeDtypeStruct((GROUPS, rows + rows // LANES * HEAD_DIM, LANES), BF16)] * GROUP_HEADS
    operands = (x, gain, shift, w_qkv, query_bias, value_bias)
    return one_step(start_kernel, info, operands, shapes, [], 2 * rows * width * 3 * width)


def middle_kernel(
    info_ref, x_ref, out_grad_ref, keep_ref, w_proj_ref, proj_bias_ref, gain_ref, shift_ref, w_fc1_ref, fc1_bias_ref, w_fc2_ref,
    fc2_bias_ref, *refs,
):
    attended_refs, refs = refs[:GROUP_HEADS], refs[GROUP_HEADS:]
    mixed_ref, back_hidden_ref, att_ref, branch_ref, normed_ref, pre_ref, act_ref, out_ref, vec_ref = refs[:9]
    grad_ref, heads = refs[9:]
    width = x_ref.shape[1]
    rows = x_ref.shape[0]
    per = width // LANES
    for head in range(HEADS):
        heads[head] = attended_refs[head % GROUP_HEADS][head // GROUP_HEADS]
    attended = heads[...].reshape(width, rows)
    att_ref[...] = attended
    keep = keep_ref[...]
    hidden = x_ref[...].astype(F32) + (dot32(attended, w_proj_ref[...], (0, 0)) + row(proj_bias_ref))
    unit, scale = centre(hidden)
    normed = (unit * row(gain_ref) + row(shift_ref)).astype(BF16)
    normed_ref[...] = normed
    grad_out = out_grad_ref[...].astype(F32) * keep
    low_out = grad_out.astype(BF16)
    out_ref[...] = low_out
    branch2 = jnp.zeros((rows, width), F32)
    back_normed = jnp.zeros((rows, width), F32)

    def put(at, line):
        for piece in range(line.shape[1] // LANES):
            vec_ref[at + piece : at + piece + 1, :] = line[:, piece * LANES : (piece + 1) * LANES]

    blocks = pre_ref.shape[1] // width
    for b in range(blocks):
        cols = slice(b * width, (b + 1) * width)
        pre = dot32(normed, w_fc1_ref[:, cols], (1, 0)) + row(fc1_bias_ref)[:, cols]
        share = 0.5 * (1.0 + lax.erf(pre * (0.5**0.5)))
        low_act = (pre * share).astype(BF16)
        act_ref[:, cols] = low_act
        branch2 += dot32(low_act, w_fc2_ref[cols, :], (1, 0))
        slope = share + pre * jnp.exp(-0.5 * pre * pre) * ((2.0 * math.pi) ** -0.5)
        back_pre = (dot32(low_out, w_fc2_ref[cols, :], (1, 1)) * slope).astype(BF16)
        pre_ref[:, cols] = back_pre
        put((3 + b) * per, jnp.sum(back_pre.astype(F32), axis=0, keepdims=True))
        back_normed += dot32(back_pre, w_fc1_ref[:, cols], (1, 1))
    mixed_ref[...] = ((hidden + (branch2 + row(fc2_bias_ref))) * keep).astype(BF16)
    put((3 + blocks) * per, jnp.sum(low_out.astype(F32), axis=0, keepdims=True))
    put(per, jnp.sum(back_normed * unit, axis=0, keepdims=True))
    put(2 * per, jnp.sum(back_normed, axis=0, keepdims=True))
    back_hidden = grad_out + centre_back(back_normed * row(gain_ref), unit, scale)
    back_hidden_ref[...] = back_hidden
    branch = back_hidden.astype(BF16)
    branch_ref[...] = branch
    put(0, jnp.sum(branch.astype(F32), axis=0, keepdims=True))
    back_attended = dot32(w_proj_ref[...], branch, (1, 1)).astype(BF16)
    grad_ref[...] = back_attended.reshape(grad_ref.shape)


def middle(info, x, out_grad, keep, w_proj, proj_bias, gain, shift, w_fc1, fc1_bias, w_fc2, fc2_bias, attended):
    rows, width = x.shape
    ff = w_fc1.shape[1]
    low = lambda *shape: jax.ShapeDtypeStruct(shape, BF16)
    shapes = [
        low(rows, width), jax.ShapeDtypeStruct((rows, width), F32), low(width, rows), low(rows, width), low(rows, width),
        low(rows, ff), low(rows, ff), low(rows, width), jax.ShapeDtypeStruct(((4 * width + ff) // LANES, LANES), F32),
        low(GROUPS, width // GROUPS, rows),
    ]
    operands = [x, out_grad, keep, w_proj, proj_bias, gain, shift, w_fc1, fc1_bias, w_fc2, fc2_bias]
    operands += attended
    scratch = [pltpu.VMEM((HEADS, HEAD_DIM, rows), BF16)]
    outs = one_step(middle_kernel, info, operands, shapes, scratch, 2 * rows * width * (2 * width + 4 * ff))
    return outs[0], outs[1], outs[2:9], outs[9]


def finish_kernel(size, info_ref, x_ref, gain_ref, shift_ref, w_ref, back_hidden_ref, *refs):
    back_refs, (input_ref, send_ref, keep_ref, queries, flat, lines) = refs[:GROUP_HEADS], refs[GROUP_HEADS:]
    rows, width = x_ref.shape
    per = width // LANES

    def pair(head):
        return back_refs[head % GROUP_HEADS][head // GROUP_HEADS, :rows].astype(F32)

    for head in range(HEADS):
        ref = back_refs[head % GROUP_HEADS]
        for tile in range(rows // LANES):
            at = rows + tile * HEAD_DIM
            queries[head, :, tile * LANES : (tile + 1) * LANES] = ref[head // GROUP_HEADS, at : at + HEAD_DIM]
    is_key = lax.broadcasted_iota(jnp.int32, (1, PAIR), 1) < HEAD_DIM
    for j in range(HEADS // 2):
        first, second = pair(2 * j), pair(2 * j + 1)
        flat[:, j * PAIR : (j + 1) * PAIR] = jnp.where(is_key, first, swap_halves(second)).astype(BF16)
        flat[:, width + j * PAIR : width + (j + 1) * PAIR] = jnp.where(is_key, swap_halves(first), second).astype(BF16)
    query = queries[...].reshape(width, rows)
    unit, scale = centre(x_ref[...].astype(F32))
    normed = (unit * row(gain_ref) + row(shift_ref)).astype(BF16)
    spread(lines, 2 * per, 3 * per, dot32(normed, query, (0, 1)))
    for b in range(2):
        spread(lines, (3 + b) * per, 3 * per, dot32(normed, flat[:, b * width : (b + 1) * width], (0, 0)))
    back_normed = dot32(query, w_ref[:, :width], (0, 1)) + dot32(flat[...], w_ref[:, width:], (1, 1))
    input_ref[...] = (back_hidden_ref[...] + centre_back(back_normed * row(gain_ref), unit, scale)).astype(BF16)

    def put(at, line):
        for piece in range(per):
            lines[at + piece : at + piece + 1, :] = line[:, piece * LANES : (piece + 1) * LANES]

    put(0, jnp.sum(back_normed * unit, axis=0, keepdims=True))
    put(per, jnp.sum(back_normed, axis=0, keepdims=True))
    at = (2 + 3 * width) * per
    put(at, dot32(jnp.ones((8, rows), BF16), query, (1, 1))[0:1])
    put(at + per, jnp.sum(flat[:, width:].astype(F32), axis=0, keepdims=True))
    lines[at + 2 * per :, :] = jnp.zeros((lines.shape[0] - at - 2 * per, LANES), F32)
    core = info_ref[1] % 2

    def window(step, _):
        for ref, which in ((send_ref, 1 - core), (keep_ref, core)):
            write_window((2 * step + which) * size, lines, ref, step)
        return 0

    lax.fori_loop(0, LATE_CHUNKS // 2, window, 0)


def finish(size, info, x, gain, shift, w_qkv, back_hidden, back):
    rows, width = x.shape
    window = jax.ShapeDtypeStruct((LATE_CHUNKS // 2, LATE_WINDOW, LANES), BF16)
    shapes = [jax.ShapeDtypeStruct((rows, width), BF16), window, window]
    operands = [x, gain, shift, w_qkv, back_hidden, *back]
    scratch = [
        pltpu.VMEM((HEADS, HEAD_DIM, rows), BF16),
        pltpu.VMEM((rows, 2 * width), BF16),
        pltpu.VMEM((-(-(LATE_CHUNKS - 1) * size // 8) * 8 + LATE_WINDOW + 8, LANES), F32),
    ]
    kernel = functools.partial(finish_kernel, size)
    return one_step(kernel, info, operands, shapes, scratch, 4 * rows * width * 3 * width)


def along_g(values):
    return lax.all_to_all(values, "g", 0, 0, tiled=True)


def hold(values, after):
    return lax.optimization_barrier((values, list(after)))[0] if len(after) > 0 else values


class Plane:
    parts = (2, 2)

    def gather_keys(self, kv):
        return [kv[None], swap(kv, "f")[None]]

    def gather_queries(self, q):
        over = swap(q, "x")
        return [q, over, swap(q, "c"), swap(over, "c")]

    gather_grads = gather_queries

    def merge(self, outs):
        mine, sent = merge_cores(outs[0], swap(outs[1], "c"))
        yield [sent]
        yield merge_chips(mine, swap(sent, "x"))

    def sum_back(self, outs):
        q_sent, q_kept, sent, kept = outs[1], outs[0], outs[3][0], outs[2][0]
        both = add(q_kept, swap(q_sent, "c"))
        groups, clips, rows, _ = kept.shape
        came = swap(sent, "f").reshape(groups, clips * rows, PAIR)
        return sum_back(kept.reshape(groups, clips * rows, PAIR), came, both[0], swap(both[1], "x"))


class AnyPlane:
    parts = (1,)

    def __init__(self, clips, times):
        self.clips, self.times = clips, times

    def split(self, values):
        groups, rows, width = values.shape
        values = values.reshape(groups, rows, self.clips, self.times, -1).transpose(3, 0, 1, 2, 4)
        return values.reshape(self.times, groups, rows, width // self.times)

    def gather_keys(self, kv):
        return [lax.all_gather(kv, "f")]

    def gather_queries(self, q):
        groups, tiles, rows, lanes = q.shape
        q = lax.all_gather(q.transpose(0, 2, 1, 3).reshape(groups, rows, self.clips, -1), "t")
        return [q.transpose(1, 3, 2, 0, 4).reshape(groups, self.clips, rows, -1)]

    def gather_grads(self, values):
        groups, rows, _ = values.shape
        values = lax.all_gather(values.reshape(groups, rows, self.clips, -1), "t")
        return [values.transpose(1, 2, 3, 0, 4).reshape(groups, rows, -1)]

    def merge(self, outs):
        came = lax.all_to_all(self.split(outs[0][0]), "t", 0, 0, tiled=True)
        out, lse = came[:, :, :HEAD_DIM], came[:, :, HEAD_DIM : HEAD_DIM + 1]
        most = jnp.max(lse, axis=0)
        share = jnp.exp2(lse - most)
        total = jnp.sum(share, axis=0)
        out = jnp.sum(out * share, axis=0) / total
        lse = jnp.broadcast_to(most + jnp.log2(total), (GROUPS, OUT_ROWS - HEAD_DIM, out.shape[-1]))
        yield [out]
        yield jnp.concatenate([out, lse], axis=1), out.astype(BF16)

    def sum_back(self, outs):
        back_q = lax.psum_scatter(self.split(outs[0][0]), "t", scatter_dimension=0, tiled=False)
        back_kv = lax.psum_scatter(outs[1], "f", scatter_dimension=0, tiled=False).reshape(GROUPS, -1, PAIR)
        back_q = back_q.reshape(GROUPS, HEAD_DIM, -1, LANES).transpose(0, 2, 1, 3).reshape(GROUPS, -1, LANES)
        return jnp.concatenate([back_kv, back_q], axis=1)


def layer_norm(values, scaling, offset):
    row_mean = jnp.mean(values, axis=-1, keepdims=True)
    centred = values - row_mean
    spread = jnp.mean(centred * centred, axis=-1, keepdims=True)
    return centred * lax.rsqrt(spread + EPSILON) * scaling + offset


def gelu_exact(values):
    return jax.nn.gelu(values, approximate=False)


def per_device(
    time_axes,
    tokens,
    out_grad,
    lengths,
    norm1_gain,
    norm1_shift,
    w_qkv,
    query_bias,
    value_bias,
    w_proj,
    proj_bias,
    norm2_gain,
    norm2_shift,
    w_fc1,
    fc1_bias,
    w_fc2,
    fc2_bias,
    moment,
    ema_decay,
):
    clips, freq_rows, frames, width = tokens.shape
    part = freq_rows * frames
    rows = clips * part
    times = lax.axis_size(time_axes)
    devices = lax.axis_size("f") * GROUPS * times
    early_index = lax.axis_index(time_axes)
    fast = time_axes == ("x", "c")
    plane = Plane() if fast else AnyPlane(clips, times)
    core = lax.axis_index(time_axes[-1]).reshape(1)
    first_frame = (lax.axis_index("g") * times + early_index) * frames
    frame = first_frame + lax.broadcasted_iota(jnp.int32, (1, freq_rows, frames), 2)
    keep_rows = (frame < lengths[:, None, None]).astype(F32).reshape(rows, 1)
    info = [lax.axis_index("g"), early_index]
    for clip in range(clips):
        info += [lengths[clip] // frames, lengths[clip] % frames]
    info = jnp.stack(info).astype(jnp.int32)

    x = tokens.reshape(rows, width)
    packs = start(info, x, norm1_gain, norm1_shift, w_qkv, query_bias, value_bias)
    kv, q, attended, kept, merges, outs = [], [], [], [], [], ()

    def fetch(head, after):
        got = along_g(packs[head])
        pairs, queries = hold((got[:, :rows], got[:, rows:]), after)
        kv.append(plane.gather_keys(pairs.reshape(GROUPS, clips, part, PAIR)))
        q.append(plane.gather_queries(queries.reshape(GROUPS, -1, HEAD_DIM, LANES)))

    def merged(merge):
        out, low = next(merge)
        kept.append(out)
        attended.append(along_g(low))
        return low

    for head in range(GROUP_HEADS):
        for later in {0: (0, 1), 1: (2,)}.get(head, ()):
            fetch(later, [outs[0]] if later > 1 else [])
        for clip in range(clips):
            after = []
            if clip == 0 and head > 0:
                merges.append(plane.merge(outs))
                after = [outs[0]]
                outs = ()
                if head > 1:
                    after.append(merged(merges[-2]))
            if clip == clips - 1:
                if head > 0:
                    after = next(merges[-1])
                if fast and head + 1 < GROUP_HEADS:
                    after += [q[head + 1][1]]
            outs = attend(info, kv[head], q[head], clip, clips, times, frames, plane.parts, outs, after)
    merges.append(plane.merge(outs))
    next(merges[-1])
    for merge in merges[len(attended) :]:
        merged(merge)
    if fast:
        size = moment.shape[0] // LANES
        block_out, back_hidden, early, grad = middle(
            info, x, out_grad.reshape(rows, width), keep_rows, w_proj, proj_bias, norm2_gain, norm2_shift, w_fc1, fc1_bias,
            w_fc2, fc2_bias, attended,
        )
        block_out = block_out.reshape(tokens.shape)
        early_windows = pack_early(devices, size, *early)
    else:
        attended_low = jnp.concatenate(attended, axis=1).reshape(width, rows)
        branch = dot32(attended_low, w_proj, (0, 0)) + proj_bias
        hidden = x.astype(F32) + branch
        normed2, norm2_pull = jax.vjp(layer_norm, hidden, norm2_gain, norm2_shift)
        normed2_low = normed2.astype(BF16)
        preactive = dot32(normed2_low, w_fc1, (1, 0)) + fc1_bias
        activated, gelu_pull = jax.vjp(gelu_exact, preactive)
        activated_low = activated.astype(BF16)
        branch2 = dot32(activated_low, w_fc2, (1, 0)) + fc2_bias
        block_out = ((hidden + branch2) * keep_rows).astype(BF16).reshape(tokens.shape)
        grad_out = out_grad.astype(F32).reshape(rows, width) * keep_rows
        back_branch2 = grad_out.astype(BF16)
        grad_fc2_bias = jnp.sum(back_branch2.astype(F32), axis=0)
        back_activated = dot32(back_branch2, w_fc2, (1, 1))
        back_preactive = gelu_pull(back_activated)[0].astype(BF16)
        grad_fc1_bias = jnp.sum(back_preactive.astype(F32), axis=0)
        back_normed2 = dot32(back_preactive, w_fc1, (1, 1))
        back_hidden_norm, grad_norm2_gain, grad_norm2_shift = norm2_pull(back_normed2)
        back_hidden = grad_out + back_hidden_norm
        back_branch = back_hidden.astype(BF16)
        grad_proj_bias = jnp.sum(back_branch.astype(F32), axis=0)
        back_attended = dot32(w_proj, back_branch, (1, 1)).astype(BF16)
        early_windows = info
        grad = back_attended.reshape(GROUPS, -1, rows)
    ready = grad_rows_of(along_g(grad), kept, early_windows)
    back, outs = [], ()
    for head in range(GROUP_HEADS):
        grads = plane.gather_grads(hold(ready[head], one) if head > 0 else ready[head])
        if fast and head == 0:
            early_sum = hold(early_windows, grads)
            early_sum = lax.psum_scatter(early_sum, ("f", "g") + time_axes, scatter_dimension=0, tiled=False)
        before, outs = outs, ()
        for clip in range(clips):
            after = []
            if head > 0 and clip == 0:
                after = [before[0]]
            elif head > 0:
                after = [plane.sum_back(before)]
                back.append(along_g(after[0]))
            outs = attend_back(info, kv[head], q[head], grads, clip, clips, times, frames, plane.parts, outs, after)
            one = [outs[0]] if clip == 0 else one
    back.append(along_g(plane.sum_back(outs)))
    if fast:
        input_grad, *late_windows = finish(
            size, info, x, norm1_gain, norm1_shift, w_qkv, back_hidden, back
        )
        input_grad = input_grad.reshape(tokens.shape)
        late_sum = reduce_late(*late_windows)
        weight_grad = own_chunk(lax.optimization_barrier(early_sum.astype(F32)), late_sum, moment.shape[0])
    else:
        back = jnp.stack(back, axis=1)
        back_kv = back[:, :, :rows].transpose(2, 0, 1, 3).reshape(rows, 2 * width)
        back_q = back[:, :, rows:].reshape(GROUPS, GROUP_HEADS, -1, HEAD_DIM, LANES).transpose(0, 1, 3, 2, 4).reshape(width, rows)
        grad_query_bias = jnp.sum(back_q.astype(F32), axis=1)
        grad_kv_bias = jnp.sum(back_kv.astype(F32), axis=0)
        grad_value_bias = grad_kv_bias.reshape(HEADS, 2, HEAD_DIM)[:, 1].reshape(width)
        normed, norm1_pull = jax.vjp(layer_norm, x.astype(F32), norm1_gain, norm1_shift)
        normed_low = normed.astype(BF16)
        head_dims = (width, GROUPS, GROUP_HEADS, HEAD_DIM)
        w_q = w_qkv[:, :width]
        w_kv = [w_qkv[:, width : 2 * width].reshape(head_dims), w_qkv[:, 2 * width :].reshape(head_dims)]
        w_kv = jnp.stack(w_kv, axis=3).reshape(width, 2 * width)
        back_normed = dot32(back_q, w_q, (0, 1)) + dot32(back_kv, w_kv, (1, 1))
        back_input_norm, grad_norm1_gain, grad_norm1_shift = norm1_pull(back_normed)
        input_grad = (back_hidden + back_input_norm).astype(BF16).reshape(tokens.shape)
        grad_proj = dot32(attended_low, back_branch, (1, 0))
        grad_fc1 = dot32(normed2_low, back_preactive, (0, 0))
        grad_fc2 = dot32(activated_low, back_branch2, (0, 0))
        grad_q = dot32(normed_low, back_q, (0, 1))
        grad_kv = dot32(normed_low, back_kv, (0, 0)).reshape(width, HEADS, 2, HEAD_DIM)
        grad_qkv = jnp.concatenate([grad_q, grad_kv[:, :, 0].reshape(width, width), grad_kv[:, :, 1].reshape(width, width)], axis=1)
        joined = jnp.concatenate(
            [
                grad_norm1_gain,
                grad_norm1_shift,
                grad_qkv.reshape(-1),
                grad_query_bias,
                grad_value_bias,
                grad_proj.reshape(-1),
                grad_proj_bias,
                grad_norm2_gain,
                grad_norm2_shift,
                grad_fc1.reshape(-1),
                grad_fc1_bias,
                grad_fc2.reshape(-1),
                grad_fc2_bias,
            ]
        ).astype(BF16)
        padding = moment.shape[0] * devices - joined.shape[0]
        joined = jnp.concatenate([joined, jnp.zeros((padding,), BF16)])
        weight_grad = lax.psum_scatter(joined, ("f", "g") + time_axes, scatter_dimension=0, tiled=True).astype(F32)
    new_moment = ema_decay[0] * moment + (1.0 - ema_decay[0]) * weight_grad
    return (block_out, input_grad, weight_grad, new_moment)


def solution(mesh):
    freqs, times = mesh.shape["freq"], mesh.shape["tm"]
    if (freqs, times) == (2, 16):
        time_sizes, time_axes = (2, 2), ("x", "c")
    else:
        time_sizes, time_axes = (times // GROUPS,), ("t",)
    fine = Mesh(mesh.devices.reshape(freqs, GROUPS, *time_sizes), ("f", "g") + time_axes)
    patches = P(None, "f", ("g",) + time_axes, None)
    flat = P(("f", "g") + time_axes)
    return jax.shard_map(
        functools.partial(per_device, time_axes),
        mesh=fine,
        in_specs=(patches, patches) + (P(),) * 14 + (flat, P()),
        out_specs=(patches, patches, flat, flat),
        check_vma=False,
    )
```

```python
import functools
import math

import jax
import jax.numpy as jnp
from jax import lax
from jax.experimental import pallas as pl
from jax.experimental.pallas import tpu as pltpu
from jax.sharding import Mesh
from jax.sharding import PartitionSpec as P

HEADS = 12
HEAD_DIM = 64
GROUPS = 4
GROUP_HEADS = HEADS // GROUPS
PAIR = 2 * HEAD_DIM
LANES = 128
OUT_ROWS = HEAD_DIM + 8
GRAD_ROWS = HEAD_DIM + 16
EPSILON = 1e-06
NEGATIVE = -1e30
LOG2E = math.log2(math.e)
LN2 = math.log(2.0)
SCALE = HEAD_DIM**-0.5
VMEM_LIMIT = 60 * 2**20
BF16 = jnp.bfloat16
F32 = jnp.float32


TOKEN = jax.ShapeDtypeStruct((8, LANES), F32)
TOKEN_SPEC = pl.BlockSpec((8, LANES), lambda i, *_: (0, 0))


def dot32(left, right, contract):
    return lax.dot_general(left, right, ((contract[:1], contract[1:]), ((), ())), preferred_element_type=F32)


def work(info_ref, clip, times, frames):
    t, full, rest = info_ref[0], info_ref[1 + clip] // frames, info_ref[1 + clip] % frames
    live = full + (rest > 0).astype(jnp.int32)
    query_blocks = (live + times - 1) // times
    key_blocks = jnp.maximum(full - t + times - 1, 0) // times
    partial = (rest > 0) & (full % times == t)
    return query_blocks, key_blocks, partial, rest


def joined(ref, late):
    tiles = [ref[late, j] for j in range(ref.shape[1])]
    return tiles[0] if len(tiles) == 1 else jnp.concatenate(tiles, axis=1)


def load_pairs(kv_refs, slot):
    return [ref[f, slot, 0] for ref in kv_refs for f in range(ref.shape[0])]


def attend_kernel(clip, times, frames, n_kv, n_q, n_out, info_ref, *refs):
    kv_refs, q_refs, refs = refs[:n_kv], refs[n_kv : n_kv + n_q], refs[n_kv + n_q :]
    refs = refs[-n_out - 6 :]
    out_refs, (token_ref, acc, top, q_pad, scores, tops) = refs[:n_out], refs[n_out:]
    token_ref[...] = jnp.zeros_like(token_ref)
    query_blocks, key_blocks, partial, rest = work(info_ref, clip, times, frames)
    width = q_refs[0].shape[1] * q_refs[0].shape[3]
    rows = scores.shape[1]
    for late in range(GROUPS):
        for p, ref in enumerate(q_refs):
            q_pad[late, :HEAD_DIM, p * width : (p + 1) * width] = joined(ref, late)
        q_pad[late, HEAD_DIM:, :] = jnp.zeros((HEAD_DIM, q_pad.shape[2]), BF16)
    acc[...] = jnp.zeros_like(acc)
    top[...] = jnp.full_like(top, NEGATIVE)
    ones = jnp.ones((16, rows), BF16)

    def load(block):
        return jnp.concatenate(load_pairs(kv_refs, block), axis=0)

    def consume(u, pair, block_scores, block_top):
        old = top[u]
        new = jnp.maximum(old, block_top)
        probs = jnp.exp2(block_scores - new).astype(BF16)
        top[u] = new
        values = jnp.concatenate([pair.T[HEAD_DIM:], ones], axis=0)
        acc[u] = acc[u] * jnp.exp2(old - new) + dot32(values, probs, (1, 0))

    def masked(u, _):
        pair = load(key_blocks)
        alive = lax.broadcasted_iota(jnp.int32, (rows, 1), 0) % frames < rest
        block_scores = jnp.where(alive, dot32(pair, q_pad[u], (1, 0)), NEGATIVE)
        consume(u, pair, block_scores, jnp.max(block_scores, axis=0, keepdims=True))
        return 0

    lax.fori_loop(0, jnp.where(partial, query_blocks, 0), masked, 0)
    total = query_blocks * key_blocks
    per = jnp.maximum(key_blocks, 1)

    def score(step, slot):
        block_scores = dot32(load(step % per), q_pad[step // per], (1, 0))
        scores[slot] = block_scores
        tops[slot] = jnp.max(block_scores, axis=0, keepdims=True)

    @pl.when(total > 0)
    def _():
        score(0, 0)

    def two_steps(double, _):
        for slot in range(2):
            step = 2 * double + slot
            score(jnp.minimum(step + 1, total - 1), 1 - slot)
            consume(step // per, load(step % per), scores[slot], tops[slot])
        return 0

    lax.fori_loop(0, total // 2, two_steps, 0)

    @pl.when(total % 2 == 1)
    def _():
        consume((total - 1) // per, load((total - 1) % per), scores[0], tops[0])

    for late in range(GROUPS):
        norm = acc[late, HEAD_DIM : HEAD_DIM + 1, :]
        some = norm > 0.0
        safe = jnp.where(some, norm, 1.0)
        out = acc[late, :HEAD_DIM, :] / safe
        lse = jnp.where(some, top[late] + jnp.log2(safe), NEGATIVE)
        fill = jnp.zeros((GRAD_ROWS - HEAD_DIM - 3, out.shape[1]), F32)
        full = jnp.concatenate([out, thirds(lse), fill], axis=0).astype(BF16)
        for p, ref in enumerate(out_refs):
            ref[late] = full[:, p * width : (p + 1) * width]


def specs_of(kv, q, place, places):
    kv_specs = [pl.BlockSpec((a.shape[0], GROUPS, 1, *a.shape[3:]), lambda i, *_: (0, 0, place, 0, 0)) for a in kv]
    _, tiles, _, lanes = q[0].shape
    q_specs = [pl.BlockSpec((GROUPS, tiles // places, HEAD_DIM, lanes), lambda i, *_: (0, place, 0, 0)) for a in q]
    return kv_specs, q_specs, tiles * lanes // places


def attend(info, kv, q, place, clip, clips, times, frames, before, after):
    kv_specs, q_specs, width = specs_of(kv, q, place, kv[0].shape[2])
    queries = len(q) * width
    rows = sum(a.shape[0] for a in kv) * kv[0].shape[3]
    pairs = GROUPS * rows * GROUPS * queries
    out_specs = [pl.BlockSpec((GROUPS, GRAD_ROWS, width), lambda i, *_: (0, 0, clip))] * len(q) + [TOKEN_SPEC]
    n_in = 1 + len(kv) + len(q)
    return pl.pallas_call(
        functools.partial(attend_kernel, clip, times, frames, len(kv), len(q), len(q)),
        grid_spec=pltpu.PrefetchScalarGridSpec(
            num_scalar_prefetch=1,
            grid=(1,),
            in_specs=kv_specs + q_specs + [pl.BlockSpec(memory_space=pl.ANY)] * (len(before) + len(after)),
            out_specs=out_specs,
            scratch_shapes=[
                pltpu.VMEM((GROUPS, GRAD_ROWS, queries), F32),
                pltpu.VMEM((GROUPS, 1, queries), F32),
                pltpu.VMEM((GROUPS, PAIR, queries), BF16),
                pltpu.VMEM((2, rows, queries), F32),
                pltpu.VMEM((2, 1, queries), F32),
            ],
        ),
        out_shape=[jax.ShapeDtypeStruct((GROUPS, GRAD_ROWS, clips * width), BF16)] * len(q) + [TOKEN],
        input_output_aliases={n_in + i: i for i in range(len(before))},
        compiler_params=pltpu.CompilerParams(vmem_limit_bytes=VMEM_LIMIT),
        cost_estimate=pl.CostEstimate(flops=256 * pairs, bytes_accessed=pairs // 16, transcendentals=pairs),
    )(info, *kv, *q, *before, *after)


def attend_back_kernel(clip, times, frames, cuts, n_kv, n_q, n_out, info_ref, *refs):
    kv_refs, q_refs, grad_refs = refs[:n_kv], refs[n_kv : n_kv + n_q], refs[n_kv + n_q : n_kv + 2 * n_q]
    refs = refs[-n_out - n_kv - 9 :]
    back_q_refs, back_kv_refs, refs = refs[:n_out], refs[n_out : n_out + n_kv], refs[n_out + n_kv :]
    refs[0][...] = jnp.zeros_like(refs[0])
    _, back_q, back_kv, q_cols, grad_cols, q_rows, grad_rows, lse, delta = refs
    query_blocks, key_blocks, partial, rest = work(info_ref, clip, times, frames)
    width = grad_refs[0].shape[-1]
    part_rows = kv_refs[0].shape[3]
    rows = back_kv.shape[1]
    cut = rows // cuts
    zero = jnp.zeros((HEAD_DIM, width), BF16)

    def prepare(late, _):
        for p, (q_ref, grad_ref) in enumerate(zip(q_refs, grad_refs)):
            cols = slice(p * width, (p + 1) * width)
            query = jnp.concatenate([joined(q_ref, late), zero], axis=0)
            grad = jnp.concatenate([zero, grad_ref[late, :HEAD_DIM]], axis=0)
            q_cols[late, :, cols] = query
            grad_cols[late, :, cols] = grad
            q_rows[late, cols, :] = query.T
            grad_rows[late, cols, :] = grad.T
            extra = grad_ref[late, HEAD_DIM:].astype(F32)
            lse[late, :, cols] = extra[0:1] + extra[1:2] + extra[2:3]
            delta[late, :, cols] = extra[3:4] + extra[4:5] + extra[5:6]
        return 0

    lax.fori_loop(0, query_blocks, prepare, 0)
    back_q[...] = jnp.zeros_like(back_q)
    back_kv[...] = jnp.zeros_like(back_kv)

    def step(u, block, masked):
        pairs = load_pairs(kv_refs, block)
        for k in range(cuts):
            part = pairs[k * len(pairs) // cuts : (k + 1) * len(pairs) // cuts]
            pair = part[0] if len(part) == 1 else jnp.concatenate(part, axis=0)
            probs = jnp.exp2(dot32(pair, q_cols[u], (1, 0)) - lse[u])
            if masked:
                row = lax.broadcasted_iota(jnp.int32, (cut, 1), 0)
                probs = jnp.where(row % frames < rest, probs, 0.0)
            back_probs = dot32(pair, grad_cols[u], (1, 0))
            back_scores = (probs * (back_probs - delta[u])).astype(BF16)
            back_pair = dot32(probs.astype(BF16), grad_rows[u], (1, 0)) + dot32(back_scores, q_rows[u], (1, 0))
            back_q[u] += dot32(pair, back_scores, (0, 0))
            back_kv[block, k * cut : (k + 1) * cut, :] += back_pair
        return 0

    lax.fori_loop(0, jnp.where(partial, query_blocks, 0), lambda u, _: step(u, key_blocks, True), 0)
    per = jnp.maximum(key_blocks, 1)
    lax.fori_loop(0, query_blocks * key_blocks, lambda i, _: step(i // per, i % per, False), 0)
    is_key = lax.broadcasted_iota(jnp.int32, (1, PAIR), 1) < HEAD_DIM
    factor = jnp.where(is_key, jnp.float32(LN2), jnp.float32(1.0))
    for late in range(GROUPS):
        for p, ref in enumerate(back_q_refs):
            ref[late] = (back_q[late, :HEAD_DIM, p * width : (p + 1) * width] * SCALE).astype(BF16)
        p = 0
        for ref in back_kv_refs:
            for f in range(ref.shape[0]):
                ref[f, late, 0] = (back_kv[late, p * part_rows : (p + 1) * part_rows, :] * factor).astype(BF16)
                p += 1


def attend_back(info, kv, q, grad, place, clip, clips, times, frames, before, after):
    kv_specs, q_specs, width = specs_of(kv, q, place, kv[0].shape[2])
    queries = len(q) * width
    rows = sum(a.shape[0] for a in kv) * kv[0].shape[3]
    pairs = GROUPS * rows * GROUPS * queries
    grad_specs = [pl.BlockSpec((GROUPS, GRAD_ROWS, width), lambda i, *_: (0, 0, clip)) for a in grad]
    q_out = [pl.BlockSpec((GROUPS, HEAD_DIM, width), lambda i, *_: (0, 0, clip))] * len(q)
    kv_out = [pl.BlockSpec((a.shape[0], GROUPS, 1, *a.shape[3:]), lambda i, *_: (0, 0, clip, 0, 0)) for a in kv]
    n_in = 1 + len(kv) + len(q) + len(grad)
    return pl.pallas_call(
        functools.partial(attend_back_kernel, clip, times, frames, 2, len(kv), len(q), len(q)),
        grid_spec=pltpu.PrefetchScalarGridSpec(
            num_scalar_prefetch=1,
            grid=(1,),
            in_specs=kv_specs + q_specs + grad_specs + [pl.BlockSpec(memory_space=pl.ANY)] * (len(before) + len(after)),
            out_specs=q_out + kv_out + [TOKEN_SPEC],
            scratch_shapes=[
                pltpu.VMEM((GROUPS, PAIR, queries), F32),
                pltpu.VMEM((GROUPS, rows, PAIR), F32),
                pltpu.VMEM((GROUPS, PAIR, queries), BF16),
                pltpu.VMEM((GROUPS, PAIR, queries), BF16),
                pltpu.VMEM((GROUPS, queries, PAIR), BF16),
                pltpu.VMEM((GROUPS, queries, PAIR), BF16),
                pltpu.VMEM((GROUPS, 1, queries), F32),
                pltpu.VMEM((GROUPS, 1, queries), F32),
            ],
        ),
        out_shape=[jax.ShapeDtypeStruct((GROUPS, HEAD_DIM, clips * width), BF16)] * len(q)
        + [jax.ShapeDtypeStruct((a.shape[0], GROUPS, clips, *a.shape[3:]), BF16) for a in kv]
        + [TOKEN],
        input_output_aliases={n_in + i: i for i in range(len(before))},
        compiler_params=pltpu.CompilerParams(vmem_limit_bytes=VMEM_LIMIT),
        cost_estimate=pl.CostEstimate(flops=640 * pairs, bytes_accessed=pairs // 8, transcendentals=pairs),
    )(info, *kv, *q, *grad, *before, *after)


def thirds(values):
    high = values.astype(BF16).astype(F32)
    middle = (values - high).astype(BF16).astype(F32)
    return jnp.concatenate([high, middle, values - high - middle], axis=0)


def merge_kernel(_, *refs):
    part_refs, (out_ref, low_ref) = refs[:-2], refs[-2:]
    for n in range(GROUPS):
        parts = [ref[n].astype(F32) for ref in part_refs]
        lses = [p[HEAD_DIM : HEAD_DIM + 1] + p[HEAD_DIM + 1 : HEAD_DIM + 2] + p[HEAD_DIM + 2 : HEAD_DIM + 3] for p in parts]
        most = functools.reduce(jnp.maximum, lses)
        shares = [jnp.exp2(lse - most) for lse in lses]
        total = sum(shares)
        out = sum(p[:HEAD_DIM] * share for p, share in zip(parts, shares)) / total
        low_ref[n] = out.astype(BF16)
        out_ref[n, :HEAD_DIM] = out
        out_ref[n, HEAD_DIM:] = jnp.broadcast_to(most + jnp.log2(total), (OUT_ROWS - HEAD_DIM, out.shape[1]))


def merge(parts, after):
    _, _, width = parts[0].shape
    return pl.pallas_call(
        merge_kernel,
        in_specs=[pl.BlockSpec(memory_space=pl.ANY)] + [pl.BlockSpec(memory_space=pltpu.VMEM)] * len(parts),
        out_shape=[jax.ShapeDtypeStruct((GROUPS, OUT_ROWS, width), F32), jax.ShapeDtypeStruct((GROUPS, HEAD_DIM, width), BF16)],
        compiler_params=pltpu.CompilerParams(vmem_limit_bytes=VMEM_LIMIT),
    )(after, *parts)


def grad_rows_kernel(grad_ref, *refs):
    out_refs, ready_refs = refs[:GROUP_HEADS], refs[-GROUP_HEADS:]
    for head in range(GROUP_HEADS):
        for n in range(GROUPS):
            grad = grad_ref[n, head * HEAD_DIM : (head + 1) * HEAD_DIM].astype(F32)
            out = out_refs[head][n]
            delta = jnp.sum(grad * out[:HEAD_DIM], axis=0, keepdims=True)
            fill = jnp.zeros((GRAD_ROWS - HEAD_DIM - 6, grad.shape[1]), F32)
            rows = jnp.concatenate([grad, thirds(out[HEAD_DIM : HEAD_DIM + 1]), thirds(delta), fill], axis=0)
            ready_refs[head][n] = rows.astype(BF16)


def grad_rows_of(grad, outs, after):
    width = grad.shape[-1]
    whole = pl.BlockSpec(memory_space=pltpu.VMEM)
    return pl.pallas_call(
        grad_rows_kernel,
        in_specs=[whole] * (1 + len(outs)) + [pl.BlockSpec(memory_space=pl.ANY)],
        out_shape=[jax.ShapeDtypeStruct((GROUPS, GRAD_ROWS, width), BF16)] * GROUP_HEADS,
        compiler_params=pltpu.CompilerParams(vmem_limit_bytes=VMEM_LIMIT),
    )(grad, *outs, after)


def sum_back_kernel(_, kept_ref, came_ref, *refs):
    q_refs, ready_ref = refs[:-1], refs[-1]
    rows = kept_ref.shape[1]
    for n in range(GROUPS):
        ready_ref[n, :rows] = (kept_ref[n].astype(F32) + came_ref[n].astype(F32)).astype(BF16)
        query = sum(ref[n].astype(F32) for ref in q_refs).astype(BF16)
        for j in range(rows // LANES):
            at = rows + j * HEAD_DIM
            ready_ref[n, at : at + HEAD_DIM] = query[:, j * LANES : (j + 1) * LANES]


def sum_back(after, kept, came, queries):
    groups, rows, _ = kept.shape
    return pl.pallas_call(
        sum_back_kernel,
        in_specs=[pl.BlockSpec(memory_space=pl.ANY)] + [pl.BlockSpec(memory_space=pltpu.VMEM)] * (2 + len(queries)),
        out_shape=jax.ShapeDtypeStruct((groups, rows + rows // LANES * HEAD_DIM, LANES), BF16),
        compiler_params=pltpu.CompilerParams(vmem_limit_bytes=VMEM_LIMIT),
    )(after, kept, came, *queries)


def spread(lines, at, stride, values):
    rows, width = values.shape
    for piece in range(width // LANES):
        lines[pl.ds(at + piece, rows, stride=stride), :] = values[:, piece * LANES : (piece + 1) * LANES]


def write_window(start, lines, ref, at=0):
    skip = start % 8
    rows = ref.shape[1]
    base = pl.multiple_of(start - skip, 8)
    for s in range(8):

        @pl.when(skip == s)
        def _():
            ref[at] = lines[pl.ds(base, rows + 8), :][s : s + rows].astype(BF16)


def pack_early_kernel(size, first, att_ref, branch_ref, normed_ref, pre_ref, act_ref, out_ref, vec_ref, window_ref, lines):
    step = pl.program_id(0)

    @pl.when(step == 0)
    def _():
        width = branch_ref.shape[1]
        blocks = pre_ref.shape[1] // width
        per = width // LANES
        spread(lines, 0, per, dot32(att_ref[...], branch_ref[...], (1, 0)))
        at = width * per
        lines[at : at + 3 * per, :] = vec_ref[0 : 3 * per]
        at += 3 * per
        for b in range(blocks):
            cols = slice(b * width, (b + 1) * width)
            spread(lines, at + b * per, blocks * per, dot32(normed_ref[...], pre_ref[:, cols], (0, 0)))
        at += blocks * width * per
        lines[at : at + blocks * per, :] = vec_ref[3 * per : (3 + blocks) * per]
        at += blocks * per
        for b in range(blocks):
            cols = slice(b * width, (b + 1) * width)
            spread(lines, at + b * width * per, per, dot32(act_ref[:, cols], out_ref[...], (0, 0)))
        at += blocks * width * per
        lines[at : at + per, :] = vec_ref[(3 + blocks) * per :]
        lines[at + per :, :] = jnp.zeros((lines.shape[0] - at - per, LANES), F32)

    @pl.when(step < first)
    def _():
        window_ref[...] = jnp.zeros_like(window_ref)

    @pl.when(step >= first)
    def _():
        write_window((step - first) * size, lines, window_ref)


def early_order(chunk):
    f, g, x, c = chunk // 16, chunk // 4 % 4, chunk // 2 % 2, chunk % 2
    return ((c * 2 + x) * 2 + f) * 4 + g


def pack_early(devices, size, *operands):
    chunks = devices - LATE_CHUNKS
    whole = [pl.BlockSpec(a.shape, lambda j: (0, 0)) for a in operands]
    entries = chunks * size * LANES
    return pl.pallas_call(
        functools.partial(pack_early_kernel, size, LATE_CHUNKS),
        grid=(devices,),
        in_specs=whole,
        out_specs=pl.BlockSpec((1, EARLY_WINDOW, LANES), lambda j: (early_order(j), 0, 0)),
        scratch_shapes=[pltpu.VMEM((-(-(chunks - 1) * size // 8) * 8 + EARLY_WINDOW + 8, LANES), F32)],
        out_shape=jax.ShapeDtypeStruct((devices, EARLY_WINDOW, LANES), BF16),
        compiler_params=pltpu.CompilerParams(vmem_limit_bytes=VMEM_LIMIT),
        cost_estimate=pl.CostEstimate(flops=1024 * entries, bytes_accessed=4 * entries, transcendentals=0),
    )(*operands)


SWAP = [(0, 1), (1, 0)]


def swap(values, axis):
    return lax.ppermute(values, axis, SWAP)


def add(left, right):
    return (left.astype(F32) + right.astype(F32)).astype(BF16)


def trade(values, dim, keep, axis):
    sent = lax.dynamic_index_in_dim(values, 1 - keep, dim, keepdims=False)
    kept = lax.dynamic_index_in_dim(values, keep, dim, keepdims=False)
    return add(kept, swap(sent, axis))


EARLY_WINDOW = 1744
LATE_CHUNKS = 8
LATE_WINDOW = 1792


def reduce_late(send, keep, after):
    f, x = lax.axis_index("f"), lax.axis_index("x")
    pairs = add(keep, swap(send, "c")).reshape(2, 2, 4, -1, LANES)
    first = trade(trade(pairs[:, :, :2], 1, x, "x"), 1, f, "f")
    second = trade(trade(pairs[:, :, 2:], 2, f, "f"), 1, x, "x")
    parts = along_g(hold(jnp.stack([first[0], first[1], second[1], second[0]]), [after]))
    mine = sum(parts[n].astype(F32) for n in range(GROUPS)).astype(BF16)
    mine = jnp.concatenate([mine, lax.ppermute(mine, "g", [(2, 1), (3, 0)])], axis=0)
    far = swap(mine, "f")
    part = LATE_WINDOW // 4
    return jnp.concatenate([mine[:part], far[:part], mine[part:], far[part:]], axis=0).astype(F32)


def own_chunk(early, late, size):
    is_late = (lax.axis_index("f") == 0) & (lax.axis_index("g") < 2)
    return jnp.where(is_late, late[: size // LANES], early[: size // LANES]).reshape(size)


def centre(values):
    centred = values - jnp.mean(values, axis=-1, keepdims=True)
    scale = lax.rsqrt(jnp.mean(centred * centred, axis=-1, keepdims=True) + EPSILON)
    return centred * scale, scale


def centre_back(grad, unit, scale):
    mean = jnp.mean(grad, axis=-1, keepdims=True)
    along = jnp.mean(grad * unit, axis=-1, keepdims=True)
    return scale * (grad - mean - unit * along)


def row(ref):
    return ref[...].reshape(1, -1)


def swap_halves(values):
    return pltpu.roll(values, HEAD_DIM, axis=1)


def start_kernel(x_ref, gain_ref, shift_ref, w_ref, query_bias_ref, value_bias_ref, *refs):
    rows, width = x_ref.shape

    def put(head, values):
        at = max(head % GROUP_HEADS - 1, 0) * rows
        refs[min(head % GROUP_HEADS, 1)][head // GROUP_HEADS, at : at + rows] = values.astype(BF16)

    unit, _ = centre(x_ref[...].astype(F32))
    normed = (unit * row(gain_ref) + row(shift_ref)).astype(BF16)
    keys = dot32(normed, w_ref[:, width : 2 * width], (1, 0))
    values = dot32(normed, w_ref[:, 2 * width :], (1, 0)) + row(value_bias_ref)
    is_key = lax.broadcasted_iota(jnp.int32, (1, PAIR), 1) < HEAD_DIM
    for j in range(HEADS // 2):
        key, value = keys[:, j * PAIR : (j + 1) * PAIR], values[:, j * PAIR : (j + 1) * PAIR]
        put(2 * j, jnp.where(is_key, key, swap_halves(value)))
        put(2 * j + 1, jnp.where(is_key, swap_halves(key), value))
    query = (dot32(normed, w_ref[:, :width], (1, 0)) + row(query_bias_ref)) * (SCALE * LOG2E)
    query = query.astype(BF16).T
    for head in range(HEADS):
        part = query[head * HEAD_DIM : (head + 1) * HEAD_DIM]
        ref = refs[min(head % GROUP_HEADS, 1)]
        first = ref.shape[1] // (rows + rows // LANES * HEAD_DIM) * rows
        first += max(head % GROUP_HEADS - 1, 0) * rows // LANES * HEAD_DIM
        for tile in range(rows // LANES):
            at = first + tile * HEAD_DIM
            ref[head // GROUP_HEADS, at : at + HEAD_DIM] = part[:, tile * LANES : (tile + 1) * LANES]


def one_step(kernel, info, operands, shapes, scratch, flops):
    scalars = [] if info is None else [info]
    return pl.pallas_call(
        kernel,
        grid_spec=pltpu.PrefetchScalarGridSpec(
            num_scalar_prefetch=len(scalars),
            grid=(1,),
            in_specs=[pl.BlockSpec(a.shape, lambda i, *_, n=a.ndim: (0,) * n) for a in operands],
            out_specs=[pl.BlockSpec(a.shape, lambda i, *_, n=len(a.shape): (0,) * n) for a in shapes],
            scratch_shapes=scratch,
        ),
        out_shape=shapes,
        compiler_params=pltpu.CompilerParams(vmem_limit_bytes=VMEM_LIMIT),
        cost_estimate=pl.CostEstimate(flops=flops, bytes_accessed=flops // 500, transcendentals=0),
    )(*scalars, *operands)


def start(x, gain, shift, w_qkv, query_bias, value_bias):
    rows, width = x.shape
    height = rows + rows // LANES * HEAD_DIM
    shapes = [jax.ShapeDtypeStruct((GROUPS, n * height, LANES), BF16) for n in (1, GROUP_HEADS - 1)]
    operands = (x, gain, shift, w_qkv, query_bias, value_bias)
    return one_step(start_kernel, None, operands, shapes, [], 2 * rows * width * 3 * width)


def middle_kernel(
    x_ref, out_grad_ref, keep_ref, w_proj_ref, proj_bias_ref, gain_ref, shift_ref, w_fc1_ref, fc1_bias_ref, w_fc2_ref,
    fc2_bias_ref, *refs,
):
    attended_refs, refs = refs[:GROUP_HEADS], refs[GROUP_HEADS:]
    mixed_ref, back_hidden_ref, att_ref, branch_ref, normed_ref, pre_ref, act_ref, out_ref, vec_ref = refs[:9]
    grad_ref, heads = refs[9:]
    width = x_ref.shape[1]
    rows = x_ref.shape[0]
    per = width // LANES
    for head in range(HEADS):
        heads[head] = attended_refs[head % GROUP_HEADS][head // GROUP_HEADS]
    attended = heads[...].reshape(width, rows)
    att_ref[...] = attended
    keep = keep_ref[...]
    hidden = x_ref[...].astype(F32) + (dot32(attended, w_proj_ref[...], (0, 0)) + row(proj_bias_ref))
    unit, scale = centre(hidden)
    normed = (unit * row(gain_ref) + row(shift_ref)).astype(BF16)
    normed_ref[...] = normed
    grad_out = out_grad_ref[...].astype(F32) * keep
    low_out = grad_out.astype(BF16)
    out_ref[...] = low_out
    branch2 = jnp.zeros((rows, width), F32)
    back_normed = jnp.zeros((rows, width), F32)

    def put(at, line):
        for piece in range(line.shape[1] // LANES):
            vec_ref[at + piece : at + piece + 1, :] = line[:, piece * LANES : (piece + 1) * LANES]

    blocks = pre_ref.shape[1] // width
    for b in range(blocks):
        cols = slice(b * width, (b + 1) * width)
        pre = dot32(normed, w_fc1_ref[:, cols], (1, 0)) + row(fc1_bias_ref)[:, cols]
        share = 0.5 * (1.0 + lax.erf(pre * (0.5**0.5)))
        low_act = (pre * share).astype(BF16)
        act_ref[:, cols] = low_act
        branch2 += dot32(low_act, w_fc2_ref[cols, :], (1, 0))
        slope = share + pre * jnp.exp(-0.5 * pre * pre) * ((2.0 * math.pi) ** -0.5)
        back_pre = (dot32(low_out, w_fc2_ref[cols, :], (1, 1)) * slope).astype(BF16)
        pre_ref[:, cols] = back_pre
        put((3 + b) * per, jnp.sum(back_pre.astype(F32), axis=0, keepdims=True))
        back_normed += dot32(back_pre, w_fc1_ref[:, cols], (1, 1))
    mixed_ref[...] = ((hidden + (branch2 + row(fc2_bias_ref))) * keep).astype(BF16)
    put((3 + blocks) * per, jnp.sum(low_out.astype(F32), axis=0, keepdims=True))
    put(per, jnp.sum(back_normed * unit, axis=0, keepdims=True))
    put(2 * per, jnp.sum(back_normed, axis=0, keepdims=True))
    back_hidden = grad_out + centre_back(back_normed * row(gain_ref), unit, scale)
    back_hidden_ref[...] = back_hidden
    branch = back_hidden.astype(BF16)
    branch_ref[...] = branch
    put(0, jnp.sum(branch.astype(F32), axis=0, keepdims=True))
    back_attended = dot32(w_proj_ref[...], branch, (1, 1)).astype(BF16)
    grad_ref[...] = back_attended.reshape(grad_ref.shape)


def middle(x, out_grad, keep, w_proj, proj_bias, gain, shift, w_fc1, fc1_bias, w_fc2, fc2_bias, attended):
    rows, width = x.shape
    ff = w_fc1.shape[1]
    low = lambda *shape: jax.ShapeDtypeStruct(shape, BF16)
    shapes = [
        low(rows, width), jax.ShapeDtypeStruct((rows, width), F32), low(width, rows), low(rows, width), low(rows, width),
        low(rows, ff), low(rows, ff), low(rows, width), jax.ShapeDtypeStruct(((4 * width + ff) // LANES, LANES), F32),
        low(GROUPS, width // GROUPS, rows),
    ]
    operands = [x, out_grad, keep, w_proj, proj_bias, gain, shift, w_fc1, fc1_bias, w_fc2, fc2_bias]
    operands += attended
    scratch = [pltpu.VMEM((HEADS, HEAD_DIM, rows), BF16)]
    outs = one_step(middle_kernel, None, operands, shapes, scratch, 2 * rows * width * (2 * width + 4 * ff))
    return outs[0], outs[1], outs[2:9], outs[9]


def finish_kernel(size, info_ref, x_ref, gain_ref, shift_ref, w_ref, back_hidden_ref, *refs):
    back_refs, (input_ref, send_ref, keep_ref, queries, flat, lines) = refs[:GROUP_HEADS], refs[GROUP_HEADS:]
    rows, width = x_ref.shape
    per = width // LANES

    def pair(head):
        return back_refs[head % GROUP_HEADS][head // GROUP_HEADS, :rows].astype(F32)

    for head in range(HEADS):
        ref = back_refs[head % GROUP_HEADS]
        for tile in range(rows // LANES):
            at = rows + tile * HEAD_DIM
            queries[head, :, tile * LANES : (tile + 1) * LANES] = ref[head // GROUP_HEADS, at : at + HEAD_DIM]
    is_key = lax.broadcasted_iota(jnp.int32, (1, PAIR), 1) < HEAD_DIM
    for j in range(HEADS // 2):
        first, second = pair(2 * j), pair(2 * j + 1)
        flat[:, j * PAIR : (j + 1) * PAIR] = jnp.where(is_key, first, swap_halves(second)).astype(BF16)
        flat[:, width + j * PAIR : width + (j + 1) * PAIR] = jnp.where(is_key, swap_halves(first), second).astype(BF16)
    query = queries[...].reshape(width, rows)
    unit, scale = centre(x_ref[...].astype(F32))
    normed = (unit * row(gain_ref) + row(shift_ref)).astype(BF16)
    spread(lines, 2 * per, 3 * per, dot32(normed, query, (0, 1)))
    for b in range(2):
        spread(lines, (3 + b) * per, 3 * per, dot32(normed, flat[:, b * width : (b + 1) * width], (0, 0)))
    back_normed = dot32(query, w_ref[:, :width], (0, 1)) + dot32(flat[...], w_ref[:, width:], (1, 1))
    input_ref[...] = (back_hidden_ref[...] + centre_back(back_normed * row(gain_ref), unit, scale)).astype(BF16)

    def put(at, line):
        for piece in range(per):
            lines[at + piece : at + piece + 1, :] = line[:, piece * LANES : (piece + 1) * LANES]

    put(0, jnp.sum(back_normed * unit, axis=0, keepdims=True))
    put(per, jnp.sum(back_normed, axis=0, keepdims=True))
    at = (2 + 3 * width) * per
    put(at, dot32(jnp.ones((8, rows), BF16), query, (1, 1))[0:1])
    put(at + per, jnp.sum(flat[:, width:].astype(F32), axis=0, keepdims=True))
    lines[at + 2 * per :, :] = jnp.zeros((lines.shape[0] - at - 2 * per, LANES), F32)
    core = info_ref[0] % 2

    def window(step, _):
        for ref, which in ((send_ref, 1 - core), (keep_ref, core)):
            write_window((2 * step + which) * size, lines, ref, step)
        return 0

    lax.fori_loop(0, LATE_CHUNKS // 2, window, 0)


def finish(size, info, x, gain, shift, w_qkv, back_hidden, back):
    rows, width = x.shape
    window = jax.ShapeDtypeStruct((LATE_CHUNKS // 2, LATE_WINDOW, LANES), BF16)
    shapes = [jax.ShapeDtypeStruct((rows, width), BF16), window, window]
    operands = [x, gain, shift, w_qkv, back_hidden, *back]
    scratch = [
        pltpu.VMEM((HEADS, HEAD_DIM, rows), BF16),
        pltpu.VMEM((rows, 2 * width), BF16),
        pltpu.VMEM((-(-(LATE_CHUNKS - 1) * size // 8) * 8 + LATE_WINDOW + 8, LANES), F32),
    ]
    kernel = functools.partial(finish_kernel, size)
    return one_step(kernel, info, operands, shapes, scratch, 4 * rows * width * 3 * width)


def along_g(values):
    return lax.all_to_all(values, "g", 0, 0, tiled=True)


def hold(values, after):
    return lax.optimization_barrier((values, list(after)))[0] if len(after) > 0 else values


def exchange(parts):
    return [lax.ppermute(part, ("x", "c"), [(i, i ^ n) for i in range(4)]) for part, n in zip(parts, (2, 1, 3))]


class Plane:
    def gather_keys(self, kv):
        return [kv[None], swap(kv, "f")[None]]

    def gather_queries(self, q):
        return [q] + exchange([q] * 3)

    gather_grads = gather_queries

    def gather_first(self, values):
        over = swap(values, "x")
        return [values, over, swap(values, "c"), swap(over, "c")]

    def gather_parts(self, outs):
        return [outs[0]] + exchange(outs[1:4])

    def gather_back(self, outs):
        kept, sent = outs[4][0], outs[5][0]
        shape = (kept.shape[0], -1, PAIR)
        return kept.reshape(shape), swap(sent, "f").reshape(shape), self.gather_parts(outs)

    def sum_back(self, after, parts):
        return sum_back(after, *parts)


class AnyPlane:
    def __init__(self, clips, times, part):
        self.clips, self.times, self.part = clips, times, part

    def split(self, values):
        groups, rows, width = values.shape
        values = values.reshape(groups, rows, self.clips, self.times, -1).transpose(3, 0, 1, 2, 4)
        return values.reshape(self.times, groups, rows, width // self.times)

    def gather_keys(self, kv):
        return [lax.all_gather(kv, "f")]

    def gather_queries(self, q):
        groups, tiles, rows, lanes = q.shape
        q = lax.all_gather(q.transpose(0, 2, 1, 3).reshape(groups, rows, -1, self.part), "t")
        return [q.transpose(1, 3, 2, 0, 4).reshape(groups, -1, rows, self.times * self.part)]

    def gather_grads(self, values):
        groups, rows, _ = values.shape
        values = lax.all_gather(values.reshape(groups, rows, -1, self.part), "t")
        return [values.transpose(1, 2, 3, 0, 4).reshape(groups, rows, -1)]

    gather_first = gather_grads

    def gather_parts(self, outs):
        return list(lax.all_to_all(self.split(outs[0]), "t", 0, 0, tiled=True))

    def gather_back(self, outs):
        return outs

    def sum_back(self, after, outs):
        back_q = lax.psum_scatter(self.split(outs[0]), "t", scatter_dimension=0, tiled=False)
        back_kv = lax.psum_scatter(outs[1], "f", scatter_dimension=0, tiled=False).reshape(GROUPS, -1, PAIR)
        back_q = back_q.reshape(GROUPS, HEAD_DIM, -1, LANES).transpose(0, 2, 1, 3).reshape(GROUPS, -1, LANES)
        return jnp.concatenate([back_kv, back_q], axis=1)


def layer_norm(values, scaling, offset):
    row_mean = jnp.mean(values, axis=-1, keepdims=True)
    centred = values - row_mean
    spread = jnp.mean(centred * centred, axis=-1, keepdims=True)
    return centred * lax.rsqrt(spread + EPSILON) * scaling + offset


def gelu_exact(values):
    return jax.nn.gelu(values, approximate=False)


def per_device(
    time_axes,
    tokens,
    out_grad,
    lengths,
    norm1_gain,
    norm1_shift,
    w_qkv,
    query_bias,
    value_bias,
    w_proj,
    proj_bias,
    norm2_gain,
    norm2_shift,
    w_fc1,
    fc1_bias,
    w_fc2,
    fc2_bias,
    moment,
    ema_decay,
):
    clips, freq_rows, frames, width = tokens.shape
    part = freq_rows * frames
    rows = clips * part
    times = lax.axis_size(time_axes)
    devices = lax.axis_size("f") * GROUPS * times
    early_index = lax.axis_index(time_axes)
    fast = time_axes == ("x", "c")
    plane = Plane() if fast else AnyPlane(clips, times, part)
    first_frame = (lax.axis_index("g") * times + early_index) * frames
    frame = first_frame + lax.broadcasted_iota(jnp.int32, (1, freq_rows, frames), 2)
    keep_rows = (frame < lengths[:, None, None]).astype(F32).reshape(rows, 1)
    info = jnp.concatenate([early_index.astype(jnp.int32).reshape(1), lengths])

    x = tokens.reshape(rows, width)
    packs = start(x, norm1_gain, norm1_shift, w_qkv, query_bias, value_bias)
    attended, kept = [], []

    def fetch(values, heads, after):
        got = along_g(values)
        pairs, queries = hold((got[:, : heads * rows], got[:, heads * rows :]), after)
        kv = plane.gather_keys(pairs.reshape(GROUPS, heads * clips, part, PAIR))
        return kv, plane.gather_queries(queries.reshape(GROUPS, -1, HEAD_DIM, LANES))

    def merged(after, parts):
        out, low = merge(parts, after)
        kept.append(out)
        attended.append(along_g(low))
        return low

    def run(head, clip, outs, after):
        kv, q = fetched[min(head, 1)]
        place = max(head - 1, 0) * clips + clip
        *outs, token = attend(info, kv, q, place, clip, clips, times, frames, outs, after)
        return outs, token

    fetched = [fetch(packs[0], 1, [])]
    fetched.append(fetch(packs[1], GROUP_HEADS - 1, fetched[0][0][1:] + fetched[0][1][1:]))
    parts = None
    for head in range(GROUP_HEADS):
        outs, token = run(head, 0, (), [] if head == 0 else [token])
        after = [token]
        if head > 0:
            after.append(merged(token, parts))
        for clip in range(1, clips):
            outs, token = run(head, clip, outs, after)
        come = fetched[1][0][1:] + fetched[1][1][1:] if head == 0 else []
        parts = plane.gather_parts(hold(outs, come))
    merged(token, parts)
    if fast:
        size = moment.shape[0] // LANES
        block_out, back_hidden, early, grad = middle(
            x, out_grad.reshape(rows, width), keep_rows, w_proj, proj_bias, norm2_gain, norm2_shift, w_fc1, fc1_bias,
            w_fc2, fc2_bias, attended,
        )
        block_out = block_out.reshape(tokens.shape)
        early_windows = pack_early(devices, size, *early)
    else:
        attended_low = jnp.concatenate(attended, axis=1).reshape(width, rows)
        branch = dot32(attended_low, w_proj, (0, 0)) + proj_bias
        hidden = x.astype(F32) + branch
        normed2, norm2_pull = jax.vjp(layer_norm, hidden, norm2_gain, norm2_shift)
        normed2_low = normed2.astype(BF16)
        preactive = dot32(normed2_low, w_fc1, (1, 0)) + fc1_bias
        activated, gelu_pull = jax.vjp(gelu_exact, preactive)
        activated_low = activated.astype(BF16)
        branch2 = dot32(activated_low, w_fc2, (1, 0)) + fc2_bias
        block_out = ((hidden + branch2) * keep_rows).astype(BF16).reshape(tokens.shape)
        grad_out = out_grad.astype(F32).reshape(rows, width) * keep_rows
        back_branch2 = grad_out.astype(BF16)
        grad_fc2_bias = jnp.sum(back_branch2.astype(F32), axis=0)
        back_activated = dot32(back_branch2, w_fc2, (1, 1))
        back_preactive = gelu_pull(back_activated)[0].astype(BF16)
        grad_fc1_bias = jnp.sum(back_preactive.astype(F32), axis=0)
        back_normed2 = dot32(back_preactive, w_fc1, (1, 1))
        back_hidden_norm, grad_norm2_gain, grad_norm2_shift = norm2_pull(back_normed2)
        back_hidden = grad_out + back_hidden_norm
        back_branch = back_hidden.astype(BF16)
        grad_proj_bias = jnp.sum(back_branch.astype(F32), axis=0)
        back_attended = dot32(w_proj, back_branch, (1, 1)).astype(BF16)
        early_windows = info
        grad = back_attended.reshape(GROUPS, -1, rows)
    ready = grad_rows_of(along_g(grad), kept, early_windows)
    back, parts, token = [], None, None
    grads = plane.gather_first(ready[0])
    if fast:
        early_sum = hold(early_windows, grads[:1]).reshape(2, 2, 2, GROUPS, EARLY_WINDOW, LANES)
        early_sum = lax.psum_scatter(early_sum, "c", scatter_dimension=0, tiled=False)

    def run_back(head, clip, outs, after):
        kv, q = fetched[min(head, 1)]
        place = max(head - 1, 0) * clips + clip
        *outs, token = attend_back(info, kv, q, grads, place, clip, clips, times, frames, outs, after)
        return outs, token

    for head in range(GROUP_HEADS):
        outs, token = run_back(head, 0, (), [] if head == 0 else [token])
        after = [token]
        if head > 0:
            after.append(plane.sum_back(token, parts))
            back.append(along_g(after[-1]))
        if fast and head == 0:
            early_sum = hold(early_sum, [token])
            after.append(early_sum)
            early_sum = early_sum.reshape(4, GROUPS, EARLY_WINDOW, LANES)
            early_sum = lax.psum_scatter(early_sum, ("x", "f"), scatter_dimension=0, tiled=False)
        if head + 1 < GROUP_HEADS:
            later = plane.gather_grads(hold(ready[head + 1], after))
        for clip in range(1, clips):
            outs, token = run_back(head, clip, outs, after)
        if head + 1 < GROUP_HEADS:
            outs = hold(outs, later[1:])
            grads = later
        parts = plane.gather_back(outs)
    back.append(along_g(plane.sum_back(token, parts)))
    if fast:
        input_grad, *late_windows = finish(
            size, info, x, norm1_gain, norm1_shift, w_qkv, back_hidden, back
        )
        input_grad = input_grad.reshape(tokens.shape)
        early_sum = lax.psum_scatter(hold(early_sum, [back[-1]]), "g", scatter_dimension=0, tiled=False).astype(F32)
        late_sum = reduce_late(*late_windows, early_sum)
        weight_grad = own_chunk(lax.optimization_barrier(early_sum), late_sum, moment.shape[0])
    else:
        back = jnp.stack(back, axis=1)
        back_kv = back[:, :, :rows].transpose(2, 0, 1, 3).reshape(rows, 2 * width)
        back_q = back[:, :, rows:].reshape(GROUPS, GROUP_HEADS, -1, HEAD_DIM, LANES).transpose(0, 1, 3, 2, 4).reshape(width, rows)
        grad_query_bias = jnp.sum(back_q.astype(F32), axis=1)
        grad_kv_bias = jnp.sum(back_kv.astype(F32), axis=0)
        grad_value_bias = grad_kv_bias.reshape(HEADS, 2, HEAD_DIM)[:, 1].reshape(width)
        normed, norm1_pull = jax.vjp(layer_norm, x.astype(F32), norm1_gain, norm1_shift)
        normed_low = normed.astype(BF16)
        head_dims = (width, GROUPS, GROUP_HEADS, HEAD_DIM)
        w_q = w_qkv[:, :width]
        w_kv = [w_qkv[:, width : 2 * width].reshape(head_dims), w_qkv[:, 2 * width :].reshape(head_dims)]
        w_kv = jnp.stack(w_kv, axis=3).reshape(width, 2 * width)
        back_normed = dot32(back_q, w_q, (0, 1)) + dot32(back_kv, w_kv, (1, 1))
        back_input_norm, grad_norm1_gain, grad_norm1_shift = norm1_pull(back_normed)
        input_grad = (back_hidden + back_input_norm).astype(BF16).reshape(tokens.shape)
        grad_proj = dot32(attended_low, back_branch, (1, 0))
        grad_fc1 = dot32(normed2_low, back_preactive, (0, 0))
        grad_fc2 = dot32(activated_low, back_branch2, (0, 0))
        grad_q = dot32(normed_low, back_q, (0, 1))
        grad_kv = dot32(normed_low, back_kv, (0, 0)).reshape(width, HEADS, 2, HEAD_DIM)
        grad_qkv = jnp.concatenate([grad_q, grad_kv[:, :, 0].reshape(width, width), grad_kv[:, :, 1].reshape(width, width)], axis=1)
        joined = jnp.concatenate(
            [
                grad_norm1_gain,
                grad_norm1_shift,
                grad_qkv.reshape(-1),
                grad_query_bias,
                grad_value_bias,
                grad_proj.reshape(-1),
                grad_proj_bias,
                grad_norm2_gain,
                grad_norm2_shift,
                grad_fc1.reshape(-1),
                grad_fc1_bias,
                grad_fc2.reshape(-1),
                grad_fc2_bias,
            ]
        ).astype(BF16)
        padding = moment.shape[0] * devices - joined.shape[0]
        joined = jnp.concatenate([joined, jnp.zeros((padding,), BF16)])
        weight_grad = lax.psum_scatter(joined, ("f", "g") + time_axes, scatter_dimension=0, tiled=True).astype(F32)
    new_moment = ema_decay[0] * moment + (1.0 - ema_decay[0]) * weight_grad
    return (block_out, input_grad, weight_grad, new_moment)


def solution(mesh):
    freqs, times = mesh.shape["freq"], mesh.shape["tm"]
    if (freqs, times) == (2, 16):
        time_sizes, time_axes = (2, 2), ("x", "c")
    else:
        time_sizes, time_axes = (times // GROUPS,), ("t",)
    fine = Mesh(mesh.devices.reshape(freqs, GROUPS, *time_sizes), ("f", "g") + time_axes)
    patches = P(None, "f", ("g",) + time_axes, None)
    flat = P(("f", "g") + time_axes)
    return jax.shard_map(
        functools.partial(per_device, time_axes),
        mesh=fine,
        in_specs=(patches, patches) + (P(),) * 14 + (flat, P()),
        out_specs=(patches, patches, flat, flat),
        check_vma=False,
    )
```

```python
import functools
import math

import jax
import jax.numpy as jnp
from jax import lax
from jax.experimental import pallas as pl
from jax.experimental.pallas import tpu as pltpu
from jax.sharding import Mesh
from jax.sharding import PartitionSpec as P

HEADS = 12
HEAD_DIM = 64
GROUPS = 4
GROUP_HEADS = HEADS // GROUPS
PAIR = 2 * HEAD_DIM
LANES = 128
OUT_ROWS = HEAD_DIM + 8
GRAD_ROWS = HEAD_DIM + 16
EPSILON = 1e-06
NEGATIVE = -1e30
LOG2E = math.log2(math.e)
LN2 = math.log(2.0)
SCALE = HEAD_DIM**-0.5
VMEM_LIMIT = 60 * 2**20
BF16 = jnp.bfloat16
F32 = jnp.float32


TOKEN = jax.ShapeDtypeStruct((8, LANES), F32)
TOKEN_SPEC = pl.BlockSpec((8, LANES), lambda i, *_: (0, 0))


def dot32(left, right, contract):
    return lax.dot_general(left, right, ((contract[:1], contract[1:]), ((), ())), preferred_element_type=F32)


def work(info_ref, clip, times, frames):
    t, full, rest = info_ref[0], info_ref[1 + clip] // frames, info_ref[1 + clip] % frames
    live = full + (rest > 0).astype(jnp.int32)
    query_blocks = (live + times - 1) // times
    key_blocks = jnp.maximum(full - t + times - 1, 0) // times
    partial = (rest > 0) & (full % times == t)
    return query_blocks, key_blocks, partial, rest


def joined(ref, late):
    tiles = [ref[late, j] for j in range(ref.shape[1])]
    return tiles[0] if len(tiles) == 1 else jnp.concatenate(tiles, axis=1)


def load_pairs(kv_refs, slot):
    return [ref[f, slot, 0] for ref in kv_refs for f in range(ref.shape[0])]


def attend_kernel(clip, times, frames, n_kv, n_q, n_out, info_ref, *refs):
    kv_refs, q_refs, refs = refs[:n_kv], refs[n_kv : n_kv + n_q], refs[n_kv + n_q :]
    refs = refs[-n_out - 6 :]
    out_refs, (token_ref, acc, top, q_pad, scores, tops) = refs[:n_out], refs[n_out:]
    token_ref[...] = jnp.zeros_like(token_ref)
    query_blocks, key_blocks, partial, rest = work(info_ref, clip, times, frames)
    width = q_refs[0].shape[1] * q_refs[0].shape[3]
    rows = scores.shape[1]
    for late in range(GROUPS):
        for p, ref in enumerate(q_refs):
            q_pad[late, :HEAD_DIM, p * width : (p + 1) * width] = joined(ref, late)
        q_pad[late, HEAD_DIM:, :] = jnp.zeros((HEAD_DIM, q_pad.shape[2]), BF16)
    acc[...] = jnp.zeros_like(acc)
    top[...] = jnp.full_like(top, NEGATIVE)
    ones = jnp.ones((16, rows), BF16)

    def load(block):
        return jnp.concatenate(load_pairs(kv_refs, block), axis=0)

    def consume(u, pair, block_scores, block_top):
        old = top[u]
        new = jnp.maximum(old, block_top)
        probs = jnp.exp2(block_scores - new).astype(BF16)
        top[u] = new
        values = jnp.concatenate([pair.T[HEAD_DIM:], ones], axis=0)
        acc[u] = acc[u] * jnp.exp2(old - new) + dot32(values, probs, (1, 0))

    def masked(u, _):
        pair = load(key_blocks)
        alive = lax.broadcasted_iota(jnp.int32, (rows, 1), 0) % frames < rest
        block_scores = jnp.where(alive, dot32(pair, q_pad[u], (1, 0)), NEGATIVE)
        consume(u, pair, block_scores, jnp.max(block_scores, axis=0, keepdims=True))
        return 0

    lax.fori_loop(0, jnp.where(partial, query_blocks, 0), masked, 0)
    total = query_blocks * key_blocks
    per = jnp.maximum(key_blocks, 1)

    def score(step, slot):
        block_scores = dot32(load(step % per), q_pad[step // per], (1, 0))
        scores[slot] = block_scores
        tops[slot] = jnp.max(block_scores, axis=0, keepdims=True)

    @pl.when(total > 0)
    def _():
        score(0, 0)

    def two_steps(double, _):
        for slot in range(2):
            step = 2 * double + slot
            score(jnp.minimum(step + 1, total - 1), 1 - slot)
            consume(step // per, load(step % per), scores[slot], tops[slot])
        return 0

    lax.fori_loop(0, total // 2, two_steps, 0)

    @pl.when(total % 2 == 1)
    def _():
        consume((total - 1) // per, load((total - 1) % per), scores[0], tops[0])

    for late in range(GROUPS):
        norm = acc[late, HEAD_DIM : HEAD_DIM + 1, :]
        some = norm > 0.0
        safe = jnp.where(some, norm, 1.0)
        out = acc[late, :HEAD_DIM, :] / safe
        lse = jnp.where(some, top[late] + jnp.log2(safe), NEGATIVE)
        fill = jnp.zeros((GRAD_ROWS - HEAD_DIM - 3, out.shape[1]), F32)
        full = jnp.concatenate([out, thirds(lse), fill], axis=0).astype(BF16)
        for p, ref in enumerate(out_refs):
            ref[late] = full[:, p * width : (p + 1) * width]


def specs_of(kv, q, place, places):
    kv_specs = [pl.BlockSpec((a.shape[0], GROUPS, 1, *a.shape[3:]), lambda i, *_: (0, 0, place, 0, 0)) for a in kv]
    _, tiles, _, lanes = q[0].shape
    q_specs = [pl.BlockSpec((GROUPS, tiles // places, HEAD_DIM, lanes), lambda i, *_: (0, place, 0, 0)) for a in q]
    return kv_specs, q_specs, tiles * lanes // places


def attend(info, kv, q, place, clip, clips, times, frames, before, after):
    kv_specs, q_specs, width = specs_of(kv, q, place, kv[0].shape[2])
    queries = len(q) * width
    rows = sum(a.shape[0] for a in kv) * kv[0].shape[3]
    pairs = GROUPS * rows * GROUPS * queries
    out_specs = [pl.BlockSpec((GROUPS, GRAD_ROWS, width), lambda i, *_: (0, 0, clip % clips))] * len(q) + [TOKEN_SPEC]
    n_in = 1 + len(kv) + len(q)
    return pl.pallas_call(
        functools.partial(attend_kernel, clip, times, frames, len(kv), len(q), len(q)),
        grid_spec=pltpu.PrefetchScalarGridSpec(
            num_scalar_prefetch=1,
            grid=(1,),
            in_specs=kv_specs + q_specs + [pl.BlockSpec(memory_space=pl.ANY)] * (len(before) + len(after)),
            out_specs=out_specs,
            scratch_shapes=[
                pltpu.VMEM((GROUPS, GRAD_ROWS, queries), F32),
                pltpu.VMEM((GROUPS, 1, queries), F32),
                pltpu.VMEM((GROUPS, PAIR, queries), BF16),
                pltpu.VMEM((2, rows, queries), F32),
                pltpu.VMEM((2, 1, queries), F32),
            ],
        ),
        out_shape=[jax.ShapeDtypeStruct((GROUPS, GRAD_ROWS, clips * width), BF16)] * len(q) + [TOKEN],
        input_output_aliases={n_in + i: i for i in range(len(before))},
        compiler_params=pltpu.CompilerParams(vmem_limit_bytes=VMEM_LIMIT),
        cost_estimate=pl.CostEstimate(flops=256 * pairs, bytes_accessed=pairs // 16, transcendentals=pairs),
    )(info, *kv, *q, *before, *after)


def attend_back_kernel(clip, times, frames, cuts, n_kv, n_q, n_out, info_ref, *refs):
    kv_refs, q_refs, grad_refs = refs[:n_kv], refs[n_kv : n_kv + n_q], refs[n_kv + n_q : n_kv + 2 * n_q]
    refs = refs[-n_out - n_kv - 7 :]
    back_q_refs, back_kv_refs, refs = refs[:n_out], refs[n_out : n_out + n_kv], refs[n_out + n_kv :]
    refs[0][...] = jnp.zeros_like(refs[0])
    _, back_q, back_kv, q_cols, grad_cols, lse, delta = refs
    query_blocks, key_blocks, partial, rest = work(info_ref, clip, times, frames)
    width = grad_refs[0].shape[-1]
    part_rows = kv_refs[0].shape[3]
    rows = back_kv.shape[1]
    cut = rows // cuts
    zero = jnp.zeros((HEAD_DIM, width), BF16)

    def prepare(late, _):
        for p, (q_ref, grad_ref) in enumerate(zip(q_refs, grad_refs)):
            cols = slice(p * width, (p + 1) * width)
            q_cols[late, :, cols] = jnp.concatenate([joined(q_ref, late), zero], axis=0)
            grad_cols[late, :, cols] = jnp.concatenate([zero, grad_ref[late, :HEAD_DIM]], axis=0)
            extra = grad_ref[late, HEAD_DIM:].astype(F32)
            lse[late, :, cols] = extra[0:1] + extra[1:2] + extra[2:3]
            delta[late, :, cols] = extra[3:4] + extra[4:5] + extra[5:6]
        return 0

    lax.fori_loop(0, query_blocks, prepare, 0)
    back_q[...] = jnp.zeros_like(back_q)
    back_kv[...] = jnp.zeros_like(back_kv)

    def step(u, block, masked):
        pairs = load_pairs(kv_refs, block)
        for k in range(cuts):
            part = pairs[k * len(pairs) // cuts : (k + 1) * len(pairs) // cuts]
            pair = part[0] if len(part) == 1 else jnp.concatenate(part, axis=0)
            probs = jnp.exp2(dot32(pair, q_cols[u], (1, 0)) - lse[u])
            if masked:
                row = lax.broadcasted_iota(jnp.int32, (cut, 1), 0)
                probs = jnp.where(row % frames < rest, probs, 0.0)
            back_probs = dot32(pair, grad_cols[u], (1, 0))
            back_scores = (probs * (back_probs - delta[u])).astype(BF16)
            back_pair = dot32(probs.astype(BF16), grad_cols[u], (1, 1)) + dot32(back_scores, q_cols[u], (1, 1))
            back_q[u] += dot32(pair, back_scores, (0, 0))
            back_kv[block, k * cut : (k + 1) * cut, :] += back_pair
        return 0

    lax.fori_loop(0, jnp.where(partial, query_blocks, 0), lambda u, _: step(u, key_blocks, True), 0)
    per = jnp.maximum(key_blocks, 1)
    lax.fori_loop(0, query_blocks * key_blocks, lambda i, _: step(i // per, i % per, False), 0)
    is_key = lax.broadcasted_iota(jnp.int32, (1, PAIR), 1) < HEAD_DIM
    factor = jnp.where(is_key, jnp.float32(LN2), jnp.float32(1.0))
    for late in range(GROUPS):
        for p, ref in enumerate(back_q_refs):
            ref[late] = (back_q[late, :HEAD_DIM, p * width : (p + 1) * width] * SCALE).astype(BF16)
        p = 0
        for ref in back_kv_refs:
            for f in range(ref.shape[0]):
                ref[f, late, 0] = (back_kv[late, p * part_rows : (p + 1) * part_rows, :] * factor).astype(BF16)
                p += 1


def attend_back(info, kv, q, grad, place, clip, clips, times, frames, before, after):
    kv_specs, q_specs, width = specs_of(kv, q, place, kv[0].shape[2])
    queries = len(q) * width
    rows = sum(a.shape[0] for a in kv) * kv[0].shape[3]
    pairs = GROUPS * rows * GROUPS * queries
    grad_specs = [pl.BlockSpec((GROUPS, GRAD_ROWS, width), lambda i, *_: (0, 0, clip)) for a in grad]
    q_out = [pl.BlockSpec((GROUPS, HEAD_DIM, width), lambda i, *_: (0, 0, clip % clips))] * len(q)
    kv_out = [pl.BlockSpec((a.shape[0], GROUPS, 1, *a.shape[3:]), lambda i, *_: (0, 0, clip % clips, 0, 0)) for a in kv]
    n_in = 1 + len(kv) + len(q) + len(grad)
    return pl.pallas_call(
        functools.partial(attend_back_kernel, clip, times, frames, 2, len(kv), len(q), len(q)),
        grid_spec=pltpu.PrefetchScalarGridSpec(
            num_scalar_prefetch=1,
            grid=(1,),
            in_specs=kv_specs + q_specs + grad_specs + [pl.BlockSpec(memory_space=pl.ANY)] * (len(before) + len(after)),
            out_specs=q_out + kv_out + [TOKEN_SPEC],
            scratch_shapes=[
                pltpu.VMEM((GROUPS, PAIR, queries), F32),
                pltpu.VMEM((GROUPS, rows, PAIR), F32),
                pltpu.VMEM((GROUPS, PAIR, queries), BF16),
                pltpu.VMEM((GROUPS, PAIR, queries), BF16),
                pltpu.VMEM((GROUPS, 1, queries), F32),
                pltpu.VMEM((GROUPS, 1, queries), F32),
            ],
        ),
        out_shape=[jax.ShapeDtypeStruct((GROUPS, HEAD_DIM, clips * width), BF16)] * len(q)
        + [jax.ShapeDtypeStruct((a.shape[0], GROUPS, clips, *a.shape[3:]), BF16) for a in kv]
        + [TOKEN],
        input_output_aliases={n_in + i: i for i in range(len(before))},
        compiler_params=pltpu.CompilerParams(vmem_limit_bytes=VMEM_LIMIT),
        cost_estimate=pl.CostEstimate(flops=640 * pairs, bytes_accessed=pairs // 8, transcendentals=pairs),
    )(info, *kv, *q, *grad, *before, *after)


def thirds(values):
    high = values.astype(BF16).astype(F32)
    middle = (values - high).astype(BF16).astype(F32)
    return jnp.concatenate([high, middle, values - high - middle], axis=0)


def merge_kernel(_, *refs):
    part_refs, (out_ref, low_ref) = refs[:-2], refs[-2:]
    for n in range(GROUPS):
        parts = [ref[n].astype(F32) for ref in part_refs]
        lses = [p[HEAD_DIM : HEAD_DIM + 1] + p[HEAD_DIM + 1 : HEAD_DIM + 2] + p[HEAD_DIM + 2 : HEAD_DIM + 3] for p in parts]
        most = functools.reduce(jnp.maximum, lses)
        shares = [jnp.exp2(lse - most) for lse in lses]
        total = sum(shares)
        out = sum(p[:HEAD_DIM] * share for p, share in zip(parts, shares)) / total
        low_ref[n] = out.astype(BF16)
        out_ref[n, :HEAD_DIM] = out
        out_ref[n, HEAD_DIM:] = jnp.broadcast_to(most + jnp.log2(total), (OUT_ROWS - HEAD_DIM, out.shape[1]))


def merge(parts, after):
    _, _, width = parts[0].shape
    return pl.pallas_call(
        merge_kernel,
        in_specs=[pl.BlockSpec(memory_space=pl.ANY)] + [pl.BlockSpec(memory_space=pltpu.VMEM)] * len(parts),
        out_shape=[jax.ShapeDtypeStruct((GROUPS, OUT_ROWS, width), F32), jax.ShapeDtypeStruct((GROUPS, HEAD_DIM, width), BF16)],
        compiler_params=pltpu.CompilerParams(vmem_limit_bytes=VMEM_LIMIT),
    )(after, *parts)


def grad_rows_kernel(n_out, grad_ref, *refs):
    out_refs, ready_refs = refs[:n_out], refs[-GROUP_HEADS:]
    for head in range(GROUP_HEADS):
        for n in range(GROUPS):
            grad = grad_ref[n, head * HEAD_DIM : (head + 1) * HEAD_DIM].astype(F32)
            out = out_refs[head][n]
            if head == GROUP_HEADS - 1 and n_out > GROUP_HEADS:
                out = jnp.concatenate([ref[n] for ref in out_refs[head:]], axis=1)
            delta = jnp.sum(grad * out[:HEAD_DIM], axis=0, keepdims=True)
            fill = jnp.zeros((GRAD_ROWS - HEAD_DIM - 6, grad.shape[1]), F32)
            rows = jnp.concatenate([grad, thirds(out[HEAD_DIM : HEAD_DIM + 1]), thirds(delta), fill], axis=0)
            ready_refs[head][n] = rows.astype(BF16)


def grad_rows_of(grad, outs, after):
    width = grad.shape[-1]
    whole = pl.BlockSpec(memory_space=pltpu.VMEM)
    return pl.pallas_call(
        functools.partial(grad_rows_kernel, len(outs)),
        in_specs=[whole] * (1 + len(outs)) + [pl.BlockSpec(memory_space=pl.ANY)],
        out_shape=[jax.ShapeDtypeStruct((GROUPS, GRAD_ROWS, width), BF16)] * GROUP_HEADS,
        compiler_params=pltpu.CompilerParams(vmem_limit_bytes=VMEM_LIMIT),
    )(grad, *outs, after)


def sum_back_kernel(_, kept_ref, came_ref, *refs):
    q_refs, ready_ref = refs[:-1], refs[-1]
    rows = kept_ref.shape[1]
    for n in range(GROUPS):
        ready_ref[n, :rows] = (kept_ref[n].astype(F32) + came_ref[n].astype(F32)).astype(BF16)
        query = sum(ref[n].astype(F32) for ref in q_refs).astype(BF16)
        for j in range(rows // LANES):
            at = rows + j * HEAD_DIM
            ready_ref[n, at : at + HEAD_DIM] = query[:, j * LANES : (j + 1) * LANES]


def sum_back(after, kept, came, queries):
    groups, rows, _ = kept.shape
    return pl.pallas_call(
        sum_back_kernel,
        in_specs=[pl.BlockSpec(memory_space=pl.ANY)] + [pl.BlockSpec(memory_space=pltpu.VMEM)] * (2 + len(queries)),
        out_shape=jax.ShapeDtypeStruct((groups, rows + rows // LANES * HEAD_DIM, LANES), BF16),
        compiler_params=pltpu.CompilerParams(vmem_limit_bytes=VMEM_LIMIT),
    )(after, kept, came, *queries)


def spread(lines, at, stride, values):
    rows, width = values.shape
    for piece in range(width // LANES):
        lines[pl.ds(at + piece, rows, stride=stride), :] = values[:, piece * LANES : (piece + 1) * LANES]


def write_window(start, lines, ref, at=0):
    skip = start % 8
    rows = ref.shape[1]
    base = pl.multiple_of(start - skip, 8)
    for s in range(8):

        @pl.when(skip == s)
        def _():
            ref[at] = lines[pl.ds(base, rows + 8), :][s : s + rows].astype(BF16)


def pack_early_kernel(size, first, att_ref, branch_ref, normed_ref, pre_ref, act_ref, out_ref, vec_ref, window_ref, lines):
    step = pl.program_id(0)

    @pl.when(step == 0)
    def _():
        width = branch_ref.shape[1]
        blocks = pre_ref.shape[1] // width
        per = width // LANES
        spread(lines, 0, per, dot32(att_ref[...], branch_ref[...], (1, 0)))
        at = width * per
        lines[at : at + 3 * per, :] = vec_ref[0 : 3 * per]
        at += 3 * per
        for b in range(blocks):
            cols = slice(b * width, (b + 1) * width)
            spread(lines, at + b * per, blocks * per, dot32(normed_ref[...], pre_ref[:, cols], (0, 0)))
        at += blocks * width * per
        lines[at : at + blocks * per, :] = vec_ref[3 * per : (3 + blocks) * per]
        at += blocks * per
        for b in range(blocks):
            cols = slice(b * width, (b + 1) * width)
            spread(lines, at + b * width * per, per, dot32(act_ref[:, cols], out_ref[...], (0, 0)))
        at += blocks * width * per
        lines[at : at + per, :] = vec_ref[(3 + blocks) * per :]
        lines[at + per :, :] = jnp.zeros((lines.shape[0] - at - per, LANES), F32)

    @pl.when(step < first)
    def _():
        window_ref[...] = jnp.zeros_like(window_ref)

    @pl.when(step >= first)
    def _():
        write_window((step - first) * size, lines, window_ref)


def early_order(chunk):
    f, g, x, c = chunk // 16, chunk // 4 % 4, chunk // 2 % 2, chunk % 2
    return ((c * 2 + x) * 2 + f) * 4 + g


def pack_early(devices, size, *operands):
    chunks = devices - LATE_CHUNKS
    whole = [pl.BlockSpec(a.shape, lambda j: (0, 0)) for a in operands]
    entries = chunks * size * LANES
    return pl.pallas_call(
        functools.partial(pack_early_kernel, size, LATE_CHUNKS),
        grid=(devices,),
        in_specs=whole,
        out_specs=pl.BlockSpec((1, EARLY_WINDOW, LANES), lambda j: (early_order(j), 0, 0)),
        scratch_shapes=[pltpu.VMEM((-(-(chunks - 1) * size // 8) * 8 + EARLY_WINDOW + 8, LANES), F32)],
        out_shape=jax.ShapeDtypeStruct((devices, EARLY_WINDOW, LANES), BF16),
        compiler_params=pltpu.CompilerParams(vmem_limit_bytes=VMEM_LIMIT),
        cost_estimate=pl.CostEstimate(flops=1024 * entries, bytes_accessed=4 * entries, transcendentals=0),
    )(*operands)


SWAP = [(0, 1), (1, 0)]


def swap(values, axis):
    return lax.ppermute(values, axis, SWAP)


def add(left, right):
    return (left.astype(F32) + right.astype(F32)).astype(BF16)


def trade(values, dim, keep, axis):
    sent = lax.dynamic_index_in_dim(values, 1 - keep, dim, keepdims=False)
    kept = lax.dynamic_index_in_dim(values, keep, dim, keepdims=False)
    return add(kept, swap(sent, axis))


EARLY_WINDOW = 1744
LATE_CHUNKS = 8
LATE_WINDOW = 1792


def reduce_late(send, keep, after):
    f, x = lax.axis_index("f"), lax.axis_index("x")
    pairs = add(keep, swap(send, "c")).reshape(2, 2, 4, -1, LANES)
    first = trade(trade(pairs[:, :, :2], 1, x, "x"), 1, f, "f")
    second = trade(trade(pairs[:, :, 2:], 2, f, "f"), 1, x, "x")
    parts = along_g(hold(jnp.stack([first[0], first[1], second[1], second[0]]), [after]))
    mine = sum(parts[n].astype(F32) for n in range(GROUPS)).astype(BF16)
    routes = ([(4, 0), (5, 1)], [(2, 1), (3, 0)], [(6, 1), (7, 0)])
    came = [lax.ppermute(mine, ("f", "g"), route) for route in routes]
    return jnp.concatenate([mine] + came, axis=0).astype(F32)


def own_chunk(early, late, size):
    is_late = (lax.axis_index("f") == 0) & (lax.axis_index("g") < 2)
    return jnp.where(is_late, late[: size // LANES], early[: size // LANES]).reshape(size)


def centre(values):
    centred = values - jnp.mean(values, axis=-1, keepdims=True)
    scale = lax.rsqrt(jnp.mean(centred * centred, axis=-1, keepdims=True) + EPSILON)
    return centred * scale, scale


def centre_back(grad, unit, scale):
    mean = jnp.mean(grad, axis=-1, keepdims=True)
    along = jnp.mean(grad * unit, axis=-1, keepdims=True)
    return scale * (grad - mean - unit * along)


def row(ref):
    return ref[...].reshape(1, -1)


def swap_halves(values):
    return pltpu.roll(values, HEAD_DIM, axis=1)


def start_kernel(x_ref, gain_ref, shift_ref, w_ref, query_bias_ref, value_bias_ref, *refs):
    rows, width = x_ref.shape

    def put(head, values):
        at = max(head % GROUP_HEADS - 1, 0) * rows
        refs[min(head % GROUP_HEADS, 1)][head // GROUP_HEADS, at : at + rows] = values.astype(BF16)

    unit, _ = centre(x_ref[...].astype(F32))
    normed = (unit * row(gain_ref) + row(shift_ref)).astype(BF16)
    keys = dot32(normed, w_ref[:, width : 2 * width], (1, 0))
    values = dot32(normed, w_ref[:, 2 * width :], (1, 0)) + row(value_bias_ref)
    is_key = lax.broadcasted_iota(jnp.int32, (1, PAIR), 1) < HEAD_DIM
    for j in range(HEADS // 2):
        key, value = keys[:, j * PAIR : (j + 1) * PAIR], values[:, j * PAIR : (j + 1) * PAIR]
        put(2 * j, jnp.where(is_key, key, swap_halves(value)))
        put(2 * j + 1, jnp.where(is_key, swap_halves(key), value))
    query = (dot32(normed, w_ref[:, :width], (1, 0)) + row(query_bias_ref)) * (SCALE * LOG2E)
    query = query.astype(BF16).T
    for head in range(HEADS):
        part = query[head * HEAD_DIM : (head + 1) * HEAD_DIM]
        ref = refs[min(head % GROUP_HEADS, 1)]
        first = ref.shape[1] // (rows + rows // LANES * HEAD_DIM) * rows
        first += max(head % GROUP_HEADS - 1, 0) * rows // LANES * HEAD_DIM
        for tile in range(rows // LANES):
            at = first + tile * HEAD_DIM
            ref[head // GROUP_HEADS, at : at + HEAD_DIM] = part[:, tile * LANES : (tile + 1) * LANES]


def one_step(kernel, info, operands, shapes, scratch, flops):
    scalars = [] if info is None else [info]
    return pl.pallas_call(
        kernel,
        grid_spec=pltpu.PrefetchScalarGridSpec(
            num_scalar_prefetch=len(scalars),
            grid=(1,),
            in_specs=[pl.BlockSpec(a.shape, lambda i, *_, n=a.ndim: (0,) * n) for a in operands],
            out_specs=[pl.BlockSpec(a.shape, lambda i, *_, n=len(a.shape): (0,) * n) for a in shapes],
            scratch_shapes=scratch,
        ),
        out_shape=shapes,
        compiler_params=pltpu.CompilerParams(vmem_limit_bytes=VMEM_LIMIT),
        cost_estimate=pl.CostEstimate(flops=flops, bytes_accessed=flops // 500, transcendentals=0),
    )(*scalars, *operands)


def start(x, gain, shift, w_qkv, query_bias, value_bias):
    rows, width = x.shape
    height = rows + rows // LANES * HEAD_DIM
    shapes = [jax.ShapeDtypeStruct((GROUPS, n * height, LANES), BF16) for n in (1, GROUP_HEADS - 1)]
    operands = (x, gain, shift, w_qkv, query_bias, value_bias)
    return one_step(start_kernel, None, operands, shapes, [], 2 * rows * width * 3 * width)


def middle_kernel(
    x_ref, out_grad_ref, keep_ref, w_proj_ref, proj_bias_ref, gain_ref, shift_ref, w_fc1_ref, fc1_bias_ref, w_fc2_ref,
    fc2_bias_ref, *refs,
):
    attended_refs, refs = refs[: GROUP_HEADS + 1], refs[GROUP_HEADS + 1 :]
    mixed_ref, back_hidden_ref, att_ref, branch_ref, normed_ref, pre_ref, act_ref, out_ref, vec_ref = refs[:9]
    grad_ref, heads = refs[9:]
    width = x_ref.shape[1]
    rows = x_ref.shape[0]
    per = width // LANES
    for head in range(HEADS):
        group, place = head // GROUP_HEADS, head % GROUP_HEADS
        if place < GROUP_HEADS - 1:
            heads[head] = attended_refs[place][group]
        else:
            heads[head, :, : rows // 2] = attended_refs[place][group]
            heads[head, :, rows // 2 :] = attended_refs[place + 1][group]
    attended = heads[...].reshape(width, rows)
    att_ref[...] = attended
    keep = keep_ref[...]
    hidden = x_ref[...].astype(F32) + (dot32(attended, w_proj_ref[...], (0, 0)) + row(proj_bias_ref))
    unit, scale = centre(hidden)
    normed = (unit * row(gain_ref) + row(shift_ref)).astype(BF16)
    normed_ref[...] = normed
    grad_out = out_grad_ref[...].astype(F32) * keep
    low_out = grad_out.astype(BF16)
    out_ref[...] = low_out
    branch2 = jnp.zeros((rows, width), F32)
    back_normed = jnp.zeros((rows, width), F32)

    def put(at, line):
        for piece in range(line.shape[1] // LANES):
            vec_ref[at + piece : at + piece + 1, :] = line[:, piece * LANES : (piece + 1) * LANES]

    blocks = pre_ref.shape[1] // width
    for b in range(blocks):
        cols = slice(b * width, (b + 1) * width)
        pre = dot32(normed, w_fc1_ref[:, cols], (1, 0)) + row(fc1_bias_ref)[:, cols]
        share = 0.5 * (1.0 + lax.erf(pre * (0.5**0.5)))
        low_act = (pre * share).astype(BF16)
        act_ref[:, cols] = low_act
        branch2 += dot32(low_act, w_fc2_ref[cols, :], (1, 0))
        slope = share + pre * jnp.exp(-0.5 * pre * pre) * ((2.0 * math.pi) ** -0.5)
        back_pre = (dot32(low_out, w_fc2_ref[cols, :], (1, 1)) * slope).astype(BF16)
        pre_ref[:, cols] = back_pre
        put((3 + b) * per, jnp.sum(back_pre.astype(F32), axis=0, keepdims=True))
        back_normed += dot32(back_pre, w_fc1_ref[:, cols], (1, 1))
    mixed_ref[...] = ((hidden + (branch2 + row(fc2_bias_ref))) * keep).astype(BF16)
    put((3 + blocks) * per, jnp.sum(low_out.astype(F32), axis=0, keepdims=True))
    put(per, jnp.sum(back_normed * unit, axis=0, keepdims=True))
    put(2 * per, jnp.sum(back_normed, axis=0, keepdims=True))
    back_hidden = grad_out + centre_back(back_normed * row(gain_ref), unit, scale)
    back_hidden_ref[...] = back_hidden
    branch = back_hidden.astype(BF16)
    branch_ref[...] = branch
    put(0, jnp.sum(branch.astype(F32), axis=0, keepdims=True))
    back_attended = dot32(w_proj_ref[...], branch, (1, 1)).astype(BF16)
    grad_ref[...] = back_attended.reshape(grad_ref.shape)


def middle(x, out_grad, keep, w_proj, proj_bias, gain, shift, w_fc1, fc1_bias, w_fc2, fc2_bias, attended):
    rows, width = x.shape
    ff = w_fc1.shape[1]
    low = lambda *shape: jax.ShapeDtypeStruct(shape, BF16)
    shapes = [
        low(rows, width), jax.ShapeDtypeStruct((rows, width), F32), low(width, rows), low(rows, width), low(rows, width),
        low(rows, ff), low(rows, ff), low(rows, width), jax.ShapeDtypeStruct(((4 * width + ff) // LANES, LANES), F32),
        low(GROUPS, width // GROUPS, rows),
    ]
    operands = [x, out_grad, keep, w_proj, proj_bias, gain, shift, w_fc1, fc1_bias, w_fc2, fc2_bias]
    operands += attended
    scratch = [pltpu.VMEM((HEADS, HEAD_DIM, rows), BF16)]
    outs = one_step(middle_kernel, None, operands, shapes, scratch, 2 * rows * width * (2 * width + 4 * ff))
    return outs[0], outs[1], outs[2:9], outs[9]


def finish_kernel(size, info_ref, x_ref, gain_ref, shift_ref, w_ref, back_hidden_ref, *refs):
    back_refs, (input_ref, send_ref, keep_ref, queries, flat, lines) = refs[: GROUP_HEADS + 1], refs[GROUP_HEADS + 1 :]
    rows, width = x_ref.shape
    per = width // LANES

    def parts_of(head):
        place = head % GROUP_HEADS
        return back_refs[place : place + 1] if place < GROUP_HEADS - 1 else back_refs[place:]

    def pair(head):
        refs = parts_of(head)
        parts = [ref[head // GROUP_HEADS, : rows // len(refs)] for ref in refs]
        return (parts[0] if len(refs) == 1 else jnp.concatenate(parts, axis=0)).astype(F32)

    for head in range(HEADS):
        refs = parts_of(head)
        tiles = rows // LANES // len(refs)
        for tile in range(rows // LANES):
            at = rows // len(refs) + tile % tiles * HEAD_DIM
            part = refs[tile // tiles][head // GROUP_HEADS, at : at + HEAD_DIM]
            queries[head, :, tile * LANES : (tile + 1) * LANES] = part
    is_key = lax.broadcasted_iota(jnp.int32, (1, PAIR), 1) < HEAD_DIM
    for j in range(HEADS // 2):
        first, second = pair(2 * j), pair(2 * j + 1)
        flat[:, j * PAIR : (j + 1) * PAIR] = jnp.where(is_key, first, swap_halves(second)).astype(BF16)
        flat[:, width + j * PAIR : width + (j + 1) * PAIR] = jnp.where(is_key, swap_halves(first), second).astype(BF16)
    query = queries[...].reshape(width, rows)
    unit, scale = centre(x_ref[...].astype(F32))
    normed = (unit * row(gain_ref) + row(shift_ref)).astype(BF16)
    spread(lines, 2 * per, 3 * per, dot32(normed, query, (0, 1)))
    for b in range(2):
        spread(lines, (3 + b) * per, 3 * per, dot32(normed, flat[:, b * width : (b + 1) * width], (0, 0)))
    back_normed = dot32(query, w_ref[:, :width], (0, 1)) + dot32(flat[...], w_ref[:, width:], (1, 1))
    input_ref[...] = (back_hidden_ref[...] + centre_back(back_normed * row(gain_ref), unit, scale)).astype(BF16)

    def put(at, line):
        for piece in range(per):
            lines[at + piece : at + piece + 1, :] = line[:, piece * LANES : (piece + 1) * LANES]

    put(0, jnp.sum(back_normed * unit, axis=0, keepdims=True))
    put(per, jnp.sum(back_normed, axis=0, keepdims=True))
    at = (2 + 3 * width) * per
    put(at, dot32(jnp.ones((8, rows), BF16), query, (1, 1))[0:1])
    put(at + per, jnp.sum(flat[:, width:].astype(F32), axis=0, keepdims=True))
    lines[at + 2 * per :, :] = jnp.zeros((lines.shape[0] - at - 2 * per, LANES), F32)
    core = info_ref[0] % 2

    def window(step, _):
        for ref, which in ((send_ref, 1 - core), (keep_ref, core)):
            write_window((2 * step + which) * size, lines, ref, step)
        return 0

    lax.fori_loop(0, LATE_CHUNKS // 2, window, 0)


def finish(size, info, x, gain, shift, w_qkv, back_hidden, back):
    rows, width = x.shape
    window = jax.ShapeDtypeStruct((LATE_CHUNKS // 2, LATE_WINDOW, LANES), BF16)
    shapes = [jax.ShapeDtypeStruct((rows, width), BF16), window, window]
    operands = [x, gain, shift, w_qkv, back_hidden, *back]
    scratch = [
        pltpu.VMEM((HEADS, HEAD_DIM, rows), BF16),
        pltpu.VMEM((rows, 2 * width), BF16),
        pltpu.VMEM((-(-(LATE_CHUNKS - 1) * size // 8) * 8 + LATE_WINDOW + 8, LANES), F32),
    ]
    kernel = functools.partial(finish_kernel, size)
    return one_step(kernel, info, operands, shapes, scratch, rows * width)


def along_g(values):
    return lax.all_to_all(values, "g", 0, 0, tiled=True)


def hold(values, after):
    return lax.optimization_barrier((values, list(after)))[0] if len(after) > 0 else values


def exchange(parts):
    return [lax.ppermute(part, ("x", "c"), [(i, i ^ n) for i in range(4)]) for part, n in zip(parts, (2, 1, 3))]


class Plane:
    def gather_keys(self, kv):
        return [kv[None], swap(kv, "f")[None]]

    def gather_queries(self, q):
        return [q] + exchange([q] * 3)

    gather_grads = gather_queries

    def gather_first(self, values):
        over = swap(values, "x")
        return [values, over, swap(values, "c"), swap(over, "c")]

    def gather_parts(self, outs):
        return [outs[0]] + exchange(outs[1:4])

    def gather_back(self, outs):
        kept, sent = outs[4][0], outs[5][0]
        shape = (kept.shape[0], -1, PAIR)
        return kept.reshape(shape), swap(sent, "f").reshape(shape), self.gather_parts(outs)

    def sum_back(self, after, parts):
        return sum_back(after, *parts)


class AnyPlane:
    def __init__(self, clips, times, part):
        self.clips, self.times, self.part = clips, times, part

    def split(self, values):
        groups, rows, width = values.shape
        values = values.reshape(groups, rows, self.clips, self.times, -1).transpose(3, 0, 1, 2, 4)
        return values.reshape(self.times, groups, rows, width // self.times)

    def gather_keys(self, kv):
        return [lax.all_gather(kv, "f")]

    def gather_queries(self, q):
        groups, tiles, rows, lanes = q.shape
        q = lax.all_gather(q.transpose(0, 2, 1, 3).reshape(groups, rows, -1, self.part), "t")
        return [q.transpose(1, 3, 2, 0, 4).reshape(groups, -1, rows, self.times * self.part)]

    def gather_grads(self, values):
        groups, rows, _ = values.shape
        values = lax.all_gather(values.reshape(groups, rows, -1, self.part), "t")
        return [values.transpose(1, 2, 3, 0, 4).reshape(groups, rows, -1)]

    gather_first = gather_grads

    def gather_parts(self, outs):
        return list(lax.all_to_all(self.split(outs[0]), "t", 0, 0, tiled=True))

    def gather_back(self, outs):
        return outs

    def sum_back(self, after, outs):
        back_q = lax.psum_scatter(self.split(outs[0]), "t", scatter_dimension=0, tiled=False)
        back_kv = lax.psum_scatter(outs[1], "f", scatter_dimension=0, tiled=False).reshape(GROUPS, -1, PAIR)
        back_q = back_q.reshape(GROUPS, HEAD_DIM, -1, LANES).transpose(0, 2, 1, 3).reshape(GROUPS, -1, LANES)
        return jnp.concatenate([back_kv, back_q], axis=1)


def layer_norm(values, scaling, offset):
    row_mean = jnp.mean(values, axis=-1, keepdims=True)
    centred = values - row_mean
    spread = jnp.mean(centred * centred, axis=-1, keepdims=True)
    return centred * lax.rsqrt(spread + EPSILON) * scaling + offset


def gelu_exact(values):
    return jax.nn.gelu(values, approximate=False)


def per_device(
    time_axes,
    tokens,
    out_grad,
    lengths,
    norm1_gain,
    norm1_shift,
    w_qkv,
    query_bias,
    value_bias,
    w_proj,
    proj_bias,
    norm2_gain,
    norm2_shift,
    w_fc1,
    fc1_bias,
    w_fc2,
    fc2_bias,
    moment,
    ema_decay,
):
    clips, freq_rows, frames, width = tokens.shape
    part = freq_rows * frames
    rows = clips * part
    times = lax.axis_size(time_axes)
    devices = lax.axis_size("f") * GROUPS * times
    early_index = lax.axis_index(time_axes)
    fast = time_axes == ("x", "c")
    plane = Plane() if fast else AnyPlane(clips, times, part)
    first_frame = (lax.axis_index("g") * times + early_index) * frames
    frame = first_frame + lax.broadcasted_iota(jnp.int32, (1, freq_rows, frames), 2)
    keep_rows = (frame < lengths[:, None, None]).astype(F32).reshape(rows, 1)
    info = jnp.concatenate([early_index.astype(jnp.int32).reshape(1), lengths])

    x = tokens.reshape(rows, width)
    packs = start(x, norm1_gain, norm1_shift, w_qkv, query_bias, value_bias)
    attended, kept = [], []

    def fetch(values, heads, after):
        got = along_g(values)
        pairs, queries = hold((got[:, : heads * rows], got[:, heads * rows :]), after)
        kv = plane.gather_keys(pairs.reshape(GROUPS, heads * clips, part, PAIR))
        return kv, plane.gather_queries(queries.reshape(GROUPS, -1, HEAD_DIM, LANES))

    def merged(after, parts):
        out, low = merge(parts, after)
        kept.append(out)
        attended.append(along_g(hold(low, attended[-1:])))
        return low

    def alone(head):
        return fast and head == GROUP_HEADS - 1

    def run(head, clip, outs, after):
        kv, q = fetched[min(head, 1)]
        place = max(head - 1, 0) * clips + clip
        outs, held = ((), 1) if alone(head) else (outs, clips)
        *outs, token = attend(info, kv, q, place, clip, held, times, frames, outs, after)
        return outs, token

    fetched = [fetch(packs[0], 1, [])]
    fetched.append(fetch(packs[1], GROUP_HEADS - 1, fetched[0][0][1:] + fetched[0][1][1:]))
    parts = None
    for head in range(GROUP_HEADS):
        outs, token = run(head, 0, (), [] if head == 0 else [token])
        after = [token]
        if head > 0:
            after.append(merged(token, parts))
        come = fetched[1][0][1:] + fetched[1][1][1:] if head == 0 else []
        if alone(head):
            half = plane.gather_parts(outs)
            come = half[1:]
        for clip in range(1, clips):
            outs, token = run(head, clip, outs, after)
        parts = plane.gather_parts(hold(outs, come))
    if fast:
        merged(token, half)
    merged(token, parts)
    if fast:
        size = moment.shape[0] // LANES
        block_out, back_hidden, early, grad = middle(
            x, out_grad.reshape(rows, width), keep_rows, w_proj, proj_bias, norm2_gain, norm2_shift, w_fc1, fc1_bias,
            w_fc2, fc2_bias, attended,
        )
        block_out = block_out.reshape(tokens.shape)
        early_windows = pack_early(devices, size, *early)
    else:
        attended_low = jnp.concatenate(attended, axis=1).reshape(width, rows)
        branch = dot32(attended_low, w_proj, (0, 0)) + proj_bias
        hidden = x.astype(F32) + branch
        normed2, norm2_pull = jax.vjp(layer_norm, hidden, norm2_gain, norm2_shift)
        normed2_low = normed2.astype(BF16)
        preactive = dot32(normed2_low, w_fc1, (1, 0)) + fc1_bias
        activated, gelu_pull = jax.vjp(gelu_exact, preactive)
        activated_low = activated.astype(BF16)
        branch2 = dot32(activated_low, w_fc2, (1, 0)) + fc2_bias
        block_out = ((hidden + branch2) * keep_rows).astype(BF16).reshape(tokens.shape)
        grad_out = out_grad.astype(F32).reshape(rows, width) * keep_rows
        back_branch2 = grad_out.astype(BF16)
        grad_fc2_bias = jnp.sum(back_branch2.astype(F32), axis=0)
        back_activated = dot32(back_branch2, w_fc2, (1, 1))
        back_preactive = gelu_pull(back_activated)[0].astype(BF16)
        grad_fc1_bias = jnp.sum(back_preactive.astype(F32), axis=0)
        back_normed2 = dot32(back_preactive, w_fc1, (1, 1))
        back_hidden_norm, grad_norm2_gain, grad_norm2_shift = norm2_pull(back_normed2)
        back_hidden = grad_out + back_hidden_norm
        back_branch = back_hidden.astype(BF16)
        grad_proj_bias = jnp.sum(back_branch.astype(F32), axis=0)
        back_attended = dot32(w_proj, back_branch, (1, 1)).astype(BF16)
        early_windows = info
        grad = back_attended.reshape(GROUPS, -1, rows)
    ready = grad_rows_of(along_g(grad), kept, early_windows)
    back, parts, token = [], None, None
    grads = plane.gather_first(ready[0])
    if fast:
        early_sum = hold(early_windows, grads[:1]).reshape(2, 2, 2, GROUPS, EARLY_WINDOW, LANES)
        early_sum = lax.psum_scatter(early_sum, "c", scatter_dimension=0, tiled=False)

    def run_back(head, clip, outs, after):
        kv, q = fetched[min(head, 1)]
        place = max(head - 1, 0) * clips + clip
        outs, held = ((), 1) if alone(head) else (outs, clips)
        *outs, token = attend_back(info, kv, q, grads, place, clip, held, times, frames, outs, after)
        return outs, token

    for head in range(GROUP_HEADS):
        outs, token = run_back(head, 0, (), [] if head == 0 else [token])
        after = [token]
        if head > 0:
            after += [plane.sum_back(token, parts)] + back
            back.append(along_g(hold(after[1], back)))
        if fast and head == 0:
            early_sum = hold(early_sum, [token])
            after.append(early_sum)
        come = []
        if head + 1 < GROUP_HEADS:
            later = plane.gather_grads(hold(ready[head + 1], after))
            come = later[1:]
        if alone(head):
            half = plane.gather_back(outs)
            come = [half[1]] + half[2][1:]
        for clip in range(1, clips):
            outs, token = run_back(head, clip, outs, after)
        outs = hold(outs, come)
        if fast and head == 0:
            early_sum = hold(early_sum, come + [token]).reshape(4, GROUPS, EARLY_WINDOW, LANES)
            early_sum = lax.psum_scatter(early_sum, ("x", "f"), scatter_dimension=0, tiled=False)
        if head + 1 < GROUP_HEADS:
            grads = later
        parts = plane.gather_back(outs)
    if fast:
        back.append(along_g(hold(plane.sum_back(token, half), back[-1:])))
    back.append(along_g(hold(plane.sum_back(token, parts), back[-1:])))
    if fast:
        input_grad, *late_windows = finish(
            size, info, x, norm1_gain, norm1_shift, w_qkv, back_hidden, back
        )
        input_grad = input_grad.reshape(tokens.shape)
        early_sum = lax.psum_scatter(hold(early_sum, [back[-1]]), "g", scatter_dimension=0, tiled=False).astype(F32)
        late_sum = reduce_late(*late_windows, early_sum)
        weight_grad = own_chunk(lax.optimization_barrier(early_sum), late_sum, moment.shape[0])
    else:
        back = jnp.stack(back, axis=1)
        back_kv = back[:, :, :rows].transpose(2, 0, 1, 3).reshape(rows, 2 * width)
        back_q = back[:, :, rows:].reshape(GROUPS, GROUP_HEADS, -1, HEAD_DIM, LANES).transpose(0, 1, 3, 2, 4).reshape(width, rows)
        grad_query_bias = jnp.sum(back_q.astype(F32), axis=1)
        grad_kv_bias = jnp.sum(back_kv.astype(F32), axis=0)
        grad_value_bias = grad_kv_bias.reshape(HEADS, 2, HEAD_DIM)[:, 1].reshape(width)
        normed, norm1_pull = jax.vjp(layer_norm, x.astype(F32), norm1_gain, norm1_shift)
        normed_low = normed.astype(BF16)
        head_dims = (width, GROUPS, GROUP_HEADS, HEAD_DIM)
        w_q = w_qkv[:, :width]
        w_kv = [w_qkv[:, width : 2 * width].reshape(head_dims), w_qkv[:, 2 * width :].reshape(head_dims)]
        w_kv = jnp.stack(w_kv, axis=3).reshape(width, 2 * width)
        back_normed = dot32(back_q, w_q, (0, 1)) + dot32(back_kv, w_kv, (1, 1))
        back_input_norm, grad_norm1_gain, grad_norm1_shift = norm1_pull(back_normed)
        input_grad = (back_hidden + back_input_norm).astype(BF16).reshape(tokens.shape)
        grad_proj = dot32(attended_low, back_branch, (1, 0))
        grad_fc1 = dot32(normed2_low, back_preactive, (0, 0))
        grad_fc2 = dot32(activated_low, back_branch2, (0, 0))
        grad_q = dot32(normed_low, back_q, (0, 1))
        grad_kv = dot32(normed_low, back_kv, (0, 0)).reshape(width, HEADS, 2, HEAD_DIM)
        grad_qkv = jnp.concatenate([grad_q, grad_kv[:, :, 0].reshape(width, width), grad_kv[:, :, 1].reshape(width, width)], axis=1)
        joined = jnp.concatenate(
            [
                grad_norm1_gain,
                grad_norm1_shift,
                grad_qkv.reshape(-1),
                grad_query_bias,
                grad_value_bias,
                grad_proj.reshape(-1),
                grad_proj_bias,
                grad_norm2_gain,
                grad_norm2_shift,
                grad_fc1.reshape(-1),
                grad_fc1_bias,
                grad_fc2.reshape(-1),
                grad_fc2_bias,
            ]
        ).astype(BF16)
        padding = moment.shape[0] * devices - joined.shape[0]
        joined = jnp.concatenate([joined, jnp.zeros((padding,), BF16)])
        weight_grad = lax.psum_scatter(joined, ("f", "g") + time_axes, scatter_dimension=0, tiled=True).astype(F32)
    new_moment = ema_decay[0] * moment + (1.0 - ema_decay[0]) * weight_grad
    return (block_out, input_grad, weight_grad, new_moment)


def solution(mesh):
    freqs, times = mesh.shape["freq"], mesh.shape["tm"]
    if (freqs, times) == (2, 16):
        time_sizes, time_axes = (2, 2), ("x", "c")
    else:
        time_sizes, time_axes = (times // GROUPS,), ("t",)
    fine = Mesh(mesh.devices.reshape(freqs, GROUPS, *time_sizes), ("f", "g") + time_axes)
    patches = P(None, "f", ("g",) + time_axes, None)
    flat = P(("f", "g") + time_axes)
    return jax.shard_map(
        functools.partial(per_device, time_axes),
        mesh=fine,
        in_specs=(patches, patches) + (P(),) * 14 + (flat, P()),
        out_specs=(patches, patches, flat, flat),
        check_vma=False,
    )
```

```python
import functools
import math

import jax
import jax.numpy as jnp
from jax import lax
from jax.experimental import pallas as pl
from jax.experimental.pallas import tpu as pltpu
from jax.sharding import Mesh
from jax.sharding import PartitionSpec as P

HEADS = 12
HEAD_DIM = 64
GROUPS = 4
GROUP_HEADS = HEADS // GROUPS
PAIR = 2 * HEAD_DIM
LANES = 128
OUT_ROWS = HEAD_DIM + 8
GRAD_ROWS = HEAD_DIM + 16
EPSILON = 1e-06
NEGATIVE = -1e30
LOG2E = math.log2(math.e)
LN2 = math.log(2.0)
SCALE = HEAD_DIM**-0.5
VMEM_LIMIT = 60 * 2**20
BF16 = jnp.bfloat16
F32 = jnp.float32


TOKEN = jax.ShapeDtypeStruct((8, LANES), F32)
TOKEN_SPEC = pl.BlockSpec((8, LANES), lambda i, *_: (0, 0))


def dot32(left, right, contract):
    return lax.dot_general(left, right, ((contract[:1], contract[1:]), ((), ())), preferred_element_type=F32)


def work(info_ref, clip, times, frames):
    t, full, rest = info_ref[0], info_ref[1 + clip] // frames, info_ref[1 + clip] % frames
    live = full + (rest > 0).astype(jnp.int32)
    query_blocks = (live + times - 1) // times
    key_blocks = jnp.maximum(full - t + times - 1, 0) // times
    partial = (rest > 0) & (full % times == t)
    return query_blocks, key_blocks, partial, rest


def joined(ref, late):
    tiles = [ref[late, j] for j in range(ref.shape[1])]
    return tiles[0] if len(tiles) == 1 else jnp.concatenate(tiles, axis=1)


def load_pairs(kv_refs, slot):
    return [ref[f, slot, 0] for ref in kv_refs for f in range(ref.shape[0])]


def attend_kernel(clip, times, frames, n_kv, n_q, n_out, info_ref, *refs):
    kv_refs, q_refs, refs = refs[:n_kv], refs[n_kv : n_kv + n_q], refs[n_kv + n_q :]
    refs = refs[-n_out - 6 :]
    out_refs, (token_ref, acc, top, q_pad, scores, tops) = refs[:n_out], refs[n_out:]
    token_ref[...] = jnp.zeros_like(token_ref)
    query_blocks, key_blocks, partial, rest = work(info_ref, clip, times, frames)
    width = q_refs[0].shape[1] * q_refs[0].shape[3]
    rows = scores.shape[1]
    for late in range(GROUPS):
        for p, ref in enumerate(q_refs):
            q_pad[late, :HEAD_DIM, p * width : (p + 1) * width] = joined(ref, late)
        q_pad[late, HEAD_DIM:, :] = jnp.zeros((HEAD_DIM, q_pad.shape[2]), BF16)
    acc[...] = jnp.zeros_like(acc)
    top[...] = jnp.full_like(top, NEGATIVE)
    ones = jnp.ones((16, rows), BF16)

    def load(block):
        return jnp.concatenate(load_pairs(kv_refs, block), axis=0)

    def consume(u, pair, block_scores, block_top):
        old = top[u]
        new = jnp.maximum(old, block_top)
        probs = jnp.exp2(block_scores - new).astype(BF16)
        top[u] = new
        values = jnp.concatenate([pair.T[HEAD_DIM:], ones], axis=0)
        acc[u] = acc[u] * jnp.exp2(old - new) + dot32(values, probs, (1, 0))

    def masked(u, _):
        pair = load(key_blocks)
        alive = lax.broadcasted_iota(jnp.int32, (rows, 1), 0) % frames < rest
        block_scores = jnp.where(alive, dot32(pair, q_pad[u], (1, 0)), NEGATIVE)
        consume(u, pair, block_scores, jnp.max(block_scores, axis=0, keepdims=True))
        return 0

    lax.fori_loop(0, jnp.where(partial, query_blocks, 0), masked, 0)
    total = query_blocks * key_blocks
    per = jnp.maximum(key_blocks, 1)

    def score(step, slot):
        block_scores = dot32(load(step % per), q_pad[step // per], (1, 0))
        scores[slot] = block_scores
        tops[slot] = jnp.max(block_scores, axis=0, keepdims=True)

    @pl.when(total > 0)
    def _():
        score(0, 0)

    def two_steps(double, _):
        for slot in range(2):
            step = 2 * double + slot
            score(jnp.minimum(step + 1, total - 1), 1 - slot)
            consume(step // per, load(step % per), scores[slot], tops[slot])
        return 0

    lax.fori_loop(0, total // 2, two_steps, 0)

    @pl.when(total % 2 == 1)
    def _():
        consume((total - 1) // per, load((total - 1) % per), scores[0], tops[0])

    for late in range(GROUPS):
        norm = acc[late, HEAD_DIM : HEAD_DIM + 1, :]
        some = norm > 0.0
        safe = jnp.where(some, norm, 1.0)
        out = acc[late, :HEAD_DIM, :] / safe
        lse = jnp.where(some, top[late] + jnp.log2(safe), NEGATIVE)
        fill = jnp.zeros((GRAD_ROWS - HEAD_DIM - 3, out.shape[1]), F32)
        full = jnp.concatenate([out, thirds(lse), fill], axis=0).astype(BF16)
        for p, ref in enumerate(out_refs):
            ref[late] = full[:, p * width : (p + 1) * width]


def specs_of(kv, q, place, places):
    kv_specs = [pl.BlockSpec((a.shape[0], GROUPS, 1, *a.shape[3:]), lambda i, *_: (0, 0, place, 0, 0)) for a in kv]
    _, tiles, _, lanes = q[0].shape
    q_specs = [pl.BlockSpec((GROUPS, tiles // places, HEAD_DIM, lanes), lambda i, *_: (0, place, 0, 0)) for a in q]
    return kv_specs, q_specs, tiles * lanes // places


def attend(info, kv, q, place, clip, clips, times, frames, before, after):
    kv_specs, q_specs, width = specs_of(kv, q, place, kv[0].shape[2])
    queries = len(q) * width
    rows = sum(a.shape[0] for a in kv) * kv[0].shape[3]
    pairs = GROUPS * rows * GROUPS * queries
    out_specs = [pl.BlockSpec((GROUPS, GRAD_ROWS, width), lambda i, *_: (0, 0, clip % clips))] * len(q) + [TOKEN_SPEC]
    n_in = 1 + len(kv) + len(q)
    return pl.pallas_call(
        functools.partial(attend_kernel, clip, times, frames, len(kv), len(q), len(q)),
        grid_spec=pltpu.PrefetchScalarGridSpec(
            num_scalar_prefetch=1,
            grid=(1,),
            in_specs=kv_specs + q_specs + [pl.BlockSpec(memory_space=pl.ANY)] * (len(before) + len(after)),
            out_specs=out_specs,
            scratch_shapes=[
                pltpu.VMEM((GROUPS, GRAD_ROWS, queries), F32),
                pltpu.VMEM((GROUPS, 1, queries), F32),
                pltpu.VMEM((GROUPS, PAIR, queries), BF16),
                pltpu.VMEM((2, rows, queries), F32),
                pltpu.VMEM((2, 1, queries), F32),
            ],
        ),
        out_shape=[jax.ShapeDtypeStruct((GROUPS, GRAD_ROWS, clips * width), BF16)] * len(q) + [TOKEN],
        input_output_aliases={n_in + i: i for i in range(len(before))},
        compiler_params=pltpu.CompilerParams(vmem_limit_bytes=VMEM_LIMIT),
        cost_estimate=pl.CostEstimate(flops=256 * pairs, bytes_accessed=pairs // 16, transcendentals=pairs),
    )(info, *kv, *q, *before, *after)


def attend_back_kernel(clip, times, frames, cuts, n_kv, n_q, n_out, info_ref, *refs):
    kv_refs, q_refs, grad_refs = refs[:n_kv], refs[n_kv : n_kv + n_q], refs[n_kv + n_q : n_kv + 2 * n_q]
    refs = refs[-n_out - n_kv - 7 :]
    back_q_refs, back_kv_refs, refs = refs[:n_out], refs[n_out : n_out + n_kv], refs[n_out + n_kv :]
    refs[0][...] = jnp.zeros_like(refs[0])
    _, back_q, back_kv, q_cols, grad_cols, lse, delta = refs
    query_blocks, key_blocks, partial, rest = work(info_ref, clip, times, frames)
    width = grad_refs[0].shape[-1]
    part_rows = kv_refs[0].shape[3]
    rows = back_kv.shape[1]
    cut = rows // cuts
    zero = jnp.zeros((HEAD_DIM, width), BF16)

    def prepare(late, _):
        for p, (q_ref, grad_ref) in enumerate(zip(q_refs, grad_refs)):
            cols = slice(p * width, (p + 1) * width)
            q_cols[late, :, cols] = jnp.concatenate([joined(q_ref, late), zero], axis=0)
            grad_cols[late, :, cols] = jnp.concatenate([zero, grad_ref[late, :HEAD_DIM]], axis=0)
            extra = grad_ref[late, HEAD_DIM:].astype(F32)
            lse[late, :, cols] = extra[0:1] + extra[1:2] + extra[2:3]
            delta[late, :, cols] = extra[3:4] + extra[4:5] + extra[5:6]
        return 0

    lax.fori_loop(0, query_blocks, prepare, 0)
    back_q[...] = jnp.zeros_like(back_q)
    back_kv[...] = jnp.zeros_like(back_kv)

    def step(u, block, masked):
        pairs = load_pairs(kv_refs, block)
        for k in range(cuts):
            part = pairs[k * len(pairs) // cuts : (k + 1) * len(pairs) // cuts]
            pair = part[0] if len(part) == 1 else jnp.concatenate(part, axis=0)
            probs = jnp.exp2(dot32(pair, q_cols[u], (1, 0)) - lse[u])
            if masked:
                row = lax.broadcasted_iota(jnp.int32, (cut, 1), 0)
                probs = jnp.where(row % frames < rest, probs, 0.0)
            back_probs = dot32(pair, grad_cols[u], (1, 0))
            back_scores = (probs * (back_probs - delta[u])).astype(BF16)
            back_pair = dot32(probs.astype(BF16), grad_cols[u], (1, 1)) + dot32(back_scores, q_cols[u], (1, 1))
            back_q[u] += dot32(pair, back_scores, (0, 0))
            back_kv[block, k * cut : (k + 1) * cut, :] += back_pair
        return 0

    lax.fori_loop(0, jnp.where(partial, query_blocks, 0), lambda u, _: step(u, key_blocks, True), 0)
    per = jnp.maximum(key_blocks, 1)
    lax.fori_loop(0, query_blocks * key_blocks, lambda i, _: step(i // per, i % per, False), 0)
    is_key = lax.broadcasted_iota(jnp.int32, (1, PAIR), 1) < HEAD_DIM
    factor = jnp.where(is_key, jnp.float32(LN2), jnp.float32(1.0))
    for late in range(GROUPS):
        for p, ref in enumerate(back_q_refs):
            ref[late] = (back_q[late, :HEAD_DIM, p * width : (p + 1) * width] * SCALE).astype(BF16)
        p = 0
        for ref in back_kv_refs:
            for f in range(ref.shape[0]):
                ref[f, late, 0] = (back_kv[late, p * part_rows : (p + 1) * part_rows, :] * factor).astype(BF16)
                p += 1


def attend_back(info, kv, q, grad, place, clip, clips, times, frames, before, after):
    kv_specs, q_specs, width = specs_of(kv, q, place, kv[0].shape[2])
    queries = len(q) * width
    rows = sum(a.shape[0] for a in kv) * kv[0].shape[3]
    pairs = GROUPS * rows * GROUPS * queries
    grad_specs = [pl.BlockSpec((GROUPS, GRAD_ROWS, width), lambda i, *_: (0, 0, clip)) for a in grad]
    q_out = [pl.BlockSpec((GROUPS, HEAD_DIM, width), lambda i, *_: (0, 0, clip % clips))] * len(q)
    kv_out = [pl.BlockSpec((a.shape[0], GROUPS, 1, *a.shape[3:]), lambda i, *_: (0, 0, clip % clips, 0, 0)) for a in kv]
    n_in = 1 + len(kv) + len(q) + len(grad)
    return pl.pallas_call(
        functools.partial(attend_back_kernel, clip, times, frames, 2, len(kv), len(q), len(q)),
        grid_spec=pltpu.PrefetchScalarGridSpec(
            num_scalar_prefetch=1,
            grid=(1,),
            in_specs=kv_specs + q_specs + grad_specs + [pl.BlockSpec(memory_space=pl.ANY)] * (len(before) + len(after)),
            out_specs=q_out + kv_out + [TOKEN_SPEC],
            scratch_shapes=[
                pltpu.VMEM((GROUPS, PAIR, queries), F32),
                pltpu.VMEM((GROUPS, rows, PAIR), F32),
                pltpu.VMEM((GROUPS, PAIR, queries), BF16),
                pltpu.VMEM((GROUPS, PAIR, queries), BF16),
                pltpu.VMEM((GROUPS, 1, queries), F32),
                pltpu.VMEM((GROUPS, 1, queries), F32),
            ],
        ),
        out_shape=[jax.ShapeDtypeStruct((GROUPS, HEAD_DIM, clips * width), BF16)] * len(q)
        + [jax.ShapeDtypeStruct((a.shape[0], GROUPS, clips, *a.shape[3:]), BF16) for a in kv]
        + [TOKEN],
        input_output_aliases={n_in + i: i for i in range(len(before))},
        compiler_params=pltpu.CompilerParams(vmem_limit_bytes=VMEM_LIMIT),
        cost_estimate=pl.CostEstimate(flops=640 * pairs, bytes_accessed=pairs // 8, transcendentals=pairs),
    )(info, *kv, *q, *grad, *before, *after)


def thirds(values):
    high = values.astype(BF16).astype(F32)
    middle = (values - high).astype(BF16).astype(F32)
    return jnp.concatenate([high, middle, values - high - middle], axis=0)


def merge_kernel(_, *refs):
    part_refs, (out_ref, low_ref) = refs[:-2], refs[-2:]
    for n in range(GROUPS):
        parts = [ref[n].astype(F32) for ref in part_refs]
        lses = [p[HEAD_DIM : HEAD_DIM + 1] + p[HEAD_DIM + 1 : HEAD_DIM + 2] + p[HEAD_DIM + 2 : HEAD_DIM + 3] for p in parts]
        most = functools.reduce(jnp.maximum, lses)
        shares = [jnp.exp2(lse - most) for lse in lses]
        total = sum(shares)
        out = sum(p[:HEAD_DIM] * share for p, share in zip(parts, shares)) / total
        low_ref[n] = out.astype(BF16)
        out_ref[n, :HEAD_DIM] = out
        out_ref[n, HEAD_DIM:] = jnp.broadcast_to(most + jnp.log2(total), (OUT_ROWS - HEAD_DIM, out.shape[1]))


def merge(parts, after):
    _, _, width = parts[0].shape
    return pl.pallas_call(
        merge_kernel,
        in_specs=[pl.BlockSpec(memory_space=pl.ANY)] + [pl.BlockSpec(memory_space=pltpu.VMEM)] * len(parts),
        out_shape=[jax.ShapeDtypeStruct((GROUPS, OUT_ROWS, width), F32), jax.ShapeDtypeStruct((GROUPS, HEAD_DIM, width), BF16)],
        compiler_params=pltpu.CompilerParams(vmem_limit_bytes=VMEM_LIMIT),
    )(after, *parts)


def grad_rows_kernel(n_out, grad_ref, *refs):
    out_refs, ready_refs = refs[:n_out], refs[-GROUP_HEADS:]
    for head in range(GROUP_HEADS):
        for n in range(GROUPS):
            grad = grad_ref[n, head * HEAD_DIM : (head + 1) * HEAD_DIM].astype(F32)
            out = out_refs[head][n]
            if head == GROUP_HEADS - 1 and n_out > GROUP_HEADS:
                out = jnp.concatenate([ref[n] for ref in out_refs[head:]], axis=1)
            delta = jnp.sum(grad * out[:HEAD_DIM], axis=0, keepdims=True)
            fill = jnp.zeros((GRAD_ROWS - HEAD_DIM - 6, grad.shape[1]), F32)
            rows = jnp.concatenate([grad, thirds(out[HEAD_DIM : HEAD_DIM + 1]), thirds(delta), fill], axis=0)
            ready_refs[head][n] = rows.astype(BF16)


def grad_rows_of(grad, outs, after):
    width = grad.shape[-1]
    whole = pl.BlockSpec(memory_space=pltpu.VMEM)
    return pl.pallas_call(
        functools.partial(grad_rows_kernel, len(outs)),
        in_specs=[whole] * (1 + len(outs)) + [pl.BlockSpec(memory_space=pl.ANY)],
        out_shape=[jax.ShapeDtypeStruct((GROUPS, GRAD_ROWS, width), BF16)] * GROUP_HEADS,
        compiler_params=pltpu.CompilerParams(vmem_limit_bytes=VMEM_LIMIT),
    )(grad, *outs, after)


def sum_back_kernel(_, kept_ref, came_ref, *refs):
    q_refs, ready_ref = refs[:-1], refs[-1]
    rows = kept_ref.shape[1]
    for n in range(GROUPS):
        ready_ref[n, :rows] = (kept_ref[n].astype(F32) + came_ref[n].astype(F32)).astype(BF16)
        query = sum(ref[n].astype(F32) for ref in q_refs).astype(BF16)
        for j in range(rows // LANES):
            at = rows + j * HEAD_DIM
            ready_ref[n, at : at + HEAD_DIM] = query[:, j * LANES : (j + 1) * LANES]


def sum_back(after, kept, came, queries):
    groups, rows, _ = kept.shape
    return pl.pallas_call(
        sum_back_kernel,
        in_specs=[pl.BlockSpec(memory_space=pl.ANY)] + [pl.BlockSpec(memory_space=pltpu.VMEM)] * (2 + len(queries)),
        out_shape=jax.ShapeDtypeStruct((groups, rows + rows // LANES * HEAD_DIM, LANES), BF16),
        compiler_params=pltpu.CompilerParams(vmem_limit_bytes=VMEM_LIMIT),
    )(after, kept, came, *queries)


def spread(lines, at, stride, values):
    rows, width = values.shape
    for piece in range(width // LANES):
        lines[pl.ds(at + piece, rows, stride=stride), :] = values[:, piece * LANES : (piece + 1) * LANES]


def write_window(start, lines, ref, at=0):
    skip = start % 8
    rows = ref.shape[1]
    base = pl.multiple_of(start - skip, 8)
    for s in range(8):

        @pl.when(skip == s)
        def _():
            ref[at] = lines[pl.ds(base, rows + 8), :][s : s + rows].astype(BF16)


def pack_early_kernel(size, first, att_ref, branch_ref, normed_ref, pre_ref, act_ref, out_ref, vec_ref, window_ref, lines):
    step = pl.program_id(0)

    @pl.when(step == 0)
    def _():
        width = branch_ref.shape[1]
        blocks = pre_ref.shape[1] // width
        per = width // LANES
        spread(lines, 0, per, dot32(att_ref[...], branch_ref[...], (1, 0)))
        at = width * per
        lines[at : at + 3 * per, :] = vec_ref[0 : 3 * per]
        at += 3 * per
        for b in range(blocks):
            cols = slice(b * width, (b + 1) * width)
            spread(lines, at + b * per, blocks * per, dot32(normed_ref[...], pre_ref[:, cols], (0, 0)))
        at += blocks * width * per
        lines[at : at + blocks * per, :] = vec_ref[3 * per : (3 + blocks) * per]
        at += blocks * per
        for b in range(blocks):
            cols = slice(b * width, (b + 1) * width)
            spread(lines, at + b * width * per, per, dot32(act_ref[:, cols], out_ref[...], (0, 0)))
        at += blocks * width * per
        lines[at : at + per, :] = vec_ref[(3 + blocks) * per :]
        lines[at + per :, :] = jnp.zeros((lines.shape[0] - at - per, LANES), F32)

    @pl.when(step < first)
    def _():
        window_ref[...] = jnp.zeros_like(window_ref)

    @pl.when(step >= first)
    def _():
        write_window((step - first) * size, lines, window_ref)


def early_order(chunk):
    f, g, x, c = chunk // 16, chunk // 4 % 4, chunk // 2 % 2, chunk % 2
    return ((c * 2 + x) * 2 + f) * 4 + g


def pack_early(devices, size, *operands):
    chunks = devices - LATE_CHUNKS
    whole = [pl.BlockSpec(a.shape, lambda j: (0, 0)) for a in operands]
    entries = chunks * size * LANES
    return pl.pallas_call(
        functools.partial(pack_early_kernel, size, LATE_CHUNKS),
        grid=(devices,),
        in_specs=whole,
        out_specs=pl.BlockSpec((1, EARLY_WINDOW, LANES), lambda j: (early_order(j), 0, 0)),
        scratch_shapes=[pltpu.VMEM((-(-(chunks - 1) * size // 8) * 8 + EARLY_WINDOW + 8, LANES), F32)],
        out_shape=jax.ShapeDtypeStruct((devices, EARLY_WINDOW, LANES), BF16),
        compiler_params=pltpu.CompilerParams(vmem_limit_bytes=VMEM_LIMIT),
        cost_estimate=pl.CostEstimate(flops=1024 * entries, bytes_accessed=4 * entries, transcendentals=0),
    )(*operands)


SWAP = [(0, 1), (1, 0)]


def swap(values, axis):
    return lax.ppermute(values, axis, SWAP)


def add(left, right):
    return (left.astype(F32) + right.astype(F32)).astype(BF16)


def trade(values, dim, keep, axis):
    sent = lax.dynamic_index_in_dim(values, 1 - keep, dim, keepdims=False)
    kept = lax.dynamic_index_in_dim(values, keep, dim, keepdims=False)
    return add(kept, swap(sent, axis))


EARLY_WINDOW = 1744
LATE_CHUNKS = 8
LATE_WINDOW = 1792


def reduce_late(send, keep, after):
    f, x = lax.axis_index("f"), lax.axis_index("x")
    pairs = add(keep, swap(send, "c")).reshape(2, 2, 4, -1, LANES)
    first = trade(trade(pairs[:, :, :2], 1, x, "x"), 1, f, "f")
    second = trade(trade(pairs[:, :, 2:], 2, f, "f"), 1, x, "x")
    parts = along_g(jnp.stack([first[0], first[1], second[1], second[0]]))
    mine = sum(parts[n].astype(F32) for n in range(GROUPS)).astype(BF16)
    mine = hold(mine, [after])
    routes = ([(4, 0), (5, 1)], [(2, 1), (3, 0)], [(6, 1), (7, 0)])
    came = [lax.ppermute(mine, ("f", "g"), route) for route in routes]
    return jnp.concatenate([mine] + came, axis=0).astype(F32)


def own_chunk(early, late, size):
    is_late = (lax.axis_index("f") == 0) & (lax.axis_index("g") < 2)
    return jnp.where(is_late, late[: size // LANES], early[: size // LANES]).reshape(size)


def centre(values):
    centred = values - jnp.mean(values, axis=-1, keepdims=True)
    scale = lax.rsqrt(jnp.mean(centred * centred, axis=-1, keepdims=True) + EPSILON)
    return centred * scale, scale


def centre_back(grad, unit, scale):
    mean = jnp.mean(grad, axis=-1, keepdims=True)
    along = jnp.mean(grad * unit, axis=-1, keepdims=True)
    return scale * (grad - mean - unit * along)


def row(ref):
    return ref[...].reshape(1, -1)


def swap_halves(values):
    return pltpu.roll(values, HEAD_DIM, axis=1)


def start_kernel(x_ref, gain_ref, shift_ref, w_ref, query_bias_ref, value_bias_ref, *refs):
    rows, width = x_ref.shape

    def put(head, values):
        at = max(head % GROUP_HEADS - 1, 0) * rows
        refs[min(head % GROUP_HEADS, 1)][head // GROUP_HEADS, at : at + rows] = values.astype(BF16)

    unit, _ = centre(x_ref[...].astype(F32))
    normed = (unit * row(gain_ref) + row(shift_ref)).astype(BF16)
    keys = dot32(normed, w_ref[:, width : 2 * width], (1, 0))
    values = dot32(normed, w_ref[:, 2 * width :], (1, 0)) + row(value_bias_ref)
    is_key = lax.broadcasted_iota(jnp.int32, (1, PAIR), 1) < HEAD_DIM
    for j in range(HEADS // 2):
        key, value = keys[:, j * PAIR : (j + 1) * PAIR], values[:, j * PAIR : (j + 1) * PAIR]
        put(2 * j, jnp.where(is_key, key, swap_halves(value)))
        put(2 * j + 1, jnp.where(is_key, swap_halves(key), value))
    query = (dot32(normed, w_ref[:, :width], (1, 0)) + row(query_bias_ref)) * (SCALE * LOG2E)
    query = query.astype(BF16).T
    for head in range(HEADS):
        part = query[head * HEAD_DIM : (head + 1) * HEAD_DIM]
        ref = refs[min(head % GROUP_HEADS, 1)]
        first = ref.shape[1] // (rows + rows // LANES * HEAD_DIM) * rows
        first += max(head % GROUP_HEADS - 1, 0) * rows // LANES * HEAD_DIM
        for tile in range(rows // LANES):
            at = first + tile * HEAD_DIM
            ref[head // GROUP_HEADS, at : at + HEAD_DIM] = part[:, tile * LANES : (tile + 1) * LANES]


def one_step(kernel, info, operands, shapes, scratch, flops):
    scalars = [] if info is None else [info]
    return pl.pallas_call(
        kernel,
        grid_spec=pltpu.PrefetchScalarGridSpec(
            num_scalar_prefetch=len(scalars),
            grid=(1,),
            in_specs=[pl.BlockSpec(a.shape, lambda i, *_, n=a.ndim: (0,) * n) for a in operands],
            out_specs=[pl.BlockSpec(a.shape, lambda i, *_, n=len(a.shape): (0,) * n) for a in shapes],
            scratch_shapes=scratch,
        ),
        out_shape=shapes,
        compiler_params=pltpu.CompilerParams(vmem_limit_bytes=VMEM_LIMIT),
        cost_estimate=pl.CostEstimate(flops=flops, bytes_accessed=flops // 500, transcendentals=0),
    )(*scalars, *operands)


def start(x, gain, shift, w_qkv, query_bias, value_bias):
    rows, width = x.shape
    height = rows + rows // LANES * HEAD_DIM
    shapes = [jax.ShapeDtypeStruct((GROUPS, n * height, LANES), BF16) for n in (1, GROUP_HEADS - 1)]
    operands = (x, gain, shift, w_qkv, query_bias, value_bias)
    return one_step(start_kernel, None, operands, shapes, [], 2 * rows * width * 3 * width)


def middle_kernel(
    x_ref, out_grad_ref, keep_ref, w_proj_ref, proj_bias_ref, gain_ref, shift_ref, w_fc1_ref, fc1_bias_ref, w_fc2_ref,
    fc2_bias_ref, *refs,
):
    attended_refs, refs = refs[: GROUP_HEADS + 1], refs[GROUP_HEADS + 1 :]
    mixed_ref, back_hidden_ref, att_ref, branch_ref, normed_ref, pre_ref, act_ref, out_ref, vec_ref = refs[:9]
    grad_ref, heads = refs[9:]
    width = x_ref.shape[1]
    rows = x_ref.shape[0]
    per = width // LANES
    for head in range(HEADS):
        group, place = head // GROUP_HEADS, head % GROUP_HEADS
        if place < GROUP_HEADS - 1:
            heads[head] = attended_refs[place][group]
        else:
            heads[head, :, : rows // 2] = attended_refs[place][group]
            heads[head, :, rows // 2 :] = attended_refs[place + 1][group]
    attended = heads[...].reshape(width, rows)
    att_ref[...] = attended
    keep = keep_ref[...]
    hidden = x_ref[...].astype(F32) + (dot32(attended, w_proj_ref[...], (0, 0)) + row(proj_bias_ref))
    unit, scale = centre(hidden)
    normed = (unit * row(gain_ref) + row(shift_ref)).astype(BF16)
    normed_ref[...] = normed
    grad_out = out_grad_ref[...].astype(F32) * keep
    low_out = grad_out.astype(BF16)
    out_ref[...] = low_out
    branch2 = jnp.zeros((rows, width), F32)
    back_normed = jnp.zeros((rows, width), F32)

    def put(at, line):
        for piece in range(line.shape[1] // LANES):
            vec_ref[at + piece : at + piece + 1, :] = line[:, piece * LANES : (piece + 1) * LANES]

    blocks = pre_ref.shape[1] // width
    for b in range(blocks):
        cols = slice(b * width, (b + 1) * width)
        pre = dot32(normed, w_fc1_ref[:, cols], (1, 0)) + row(fc1_bias_ref)[:, cols]
        share = 0.5 * (1.0 + lax.erf(pre * (0.5**0.5)))
        low_act = (pre * share).astype(BF16)
        act_ref[:, cols] = low_act
        branch2 += dot32(low_act, w_fc2_ref[cols, :], (1, 0))
        slope = share + pre * jnp.exp(-0.5 * pre * pre) * ((2.0 * math.pi) ** -0.5)
        back_pre = (dot32(low_out, w_fc2_ref[cols, :], (1, 1)) * slope).astype(BF16)
        pre_ref[:, cols] = back_pre
        put((3 + b) * per, jnp.sum(back_pre.astype(F32), axis=0, keepdims=True))
        back_normed += dot32(back_pre, w_fc1_ref[:, cols], (1, 1))
    mixed_ref[...] = ((hidden + (branch2 + row(fc2_bias_ref))) * keep).astype(BF16)
    put((3 + blocks) * per, jnp.sum(low_out.astype(F32), axis=0, keepdims=True))
    put(per, jnp.sum(back_normed * unit, axis=0, keepdims=True))
    put(2 * per, jnp.sum(back_normed, axis=0, keepdims=True))
    back_hidden = grad_out + centre_back(back_normed * row(gain_ref), unit, scale)
    back_hidden_ref[...] = back_hidden
    branch = back_hidden.astype(BF16)
    branch_ref[...] = branch
    put(0, jnp.sum(branch.astype(F32), axis=0, keepdims=True))
    back_attended = dot32(w_proj_ref[...], branch, (1, 1)).astype(BF16)
    grad_ref[...] = back_attended.reshape(grad_ref.shape)


def middle(x, out_grad, keep, w_proj, proj_bias, gain, shift, w_fc1, fc1_bias, w_fc2, fc2_bias, attended):
    rows, width = x.shape
    ff = w_fc1.shape[1]
    low = lambda *shape: jax.ShapeDtypeStruct(shape, BF16)
    shapes = [
        low(rows, width), jax.ShapeDtypeStruct((rows, width), F32), low(width, rows), low(rows, width), low(rows, width),
        low(rows, ff), low(rows, ff), low(rows, width), jax.ShapeDtypeStruct(((4 * width + ff) // LANES, LANES), F32),
        low(GROUPS, width // GROUPS, rows),
    ]
    operands = [x, out_grad, keep, w_proj, proj_bias, gain, shift, w_fc1, fc1_bias, w_fc2, fc2_bias]
    operands += attended
    scratch = [pltpu.VMEM((HEADS, HEAD_DIM, rows), BF16)]
    outs = one_step(middle_kernel, None, operands, shapes, scratch, 2 * rows * width * (2 * width + 4 * ff))
    return outs[0], outs[1], outs[2:9], outs[9]


def finish_kernel(size, info_ref, x_ref, gain_ref, shift_ref, w_ref, back_hidden_ref, *refs):
    back_refs, (input_ref, send_ref, keep_ref, queries, flat, lines) = refs[: GROUP_HEADS + 1], refs[GROUP_HEADS + 1 :]
    rows, width = x_ref.shape
    per = width // LANES

    def parts_of(head):
        place = head % GROUP_HEADS
        return back_refs[place : place + 1] if place < GROUP_HEADS - 1 else back_refs[place:]

    def pair(head):
        refs = parts_of(head)
        parts = [ref[head // GROUP_HEADS, : rows // len(refs)] for ref in refs]
        return (parts[0] if len(refs) == 1 else jnp.concatenate(parts, axis=0)).astype(F32)

    for head in range(HEADS):
        refs = parts_of(head)
        tiles = rows // LANES // len(refs)
        for tile in range(rows // LANES):
            at = rows // len(refs) + tile % tiles * HEAD_DIM
            part = refs[tile // tiles][head // GROUP_HEADS, at : at + HEAD_DIM]
            queries[head, :, tile * LANES : (tile + 1) * LANES] = part
    is_key = lax.broadcasted_iota(jnp.int32, (1, PAIR), 1) < HEAD_DIM
    for j in range(HEADS // 2):
        first, second = pair(2 * j), pair(2 * j + 1)
        flat[:, j * PAIR : (j + 1) * PAIR] = jnp.where(is_key, first, swap_halves(second)).astype(BF16)
        flat[:, width + j * PAIR : width + (j + 1) * PAIR] = jnp.where(is_key, swap_halves(first), second).astype(BF16)
    query = queries[...].reshape(width, rows)
    unit, scale = centre(x_ref[...].astype(F32))
    normed = (unit * row(gain_ref) + row(shift_ref)).astype(BF16)
    spread(lines, 2 * per, 3 * per, dot32(normed, query, (0, 1)))
    for b in range(2):
        spread(lines, (3 + b) * per, 3 * per, dot32(normed, flat[:, b * width : (b + 1) * width], (0, 0)))
    back_normed = dot32(query, w_ref[:, :width], (0, 1)) + dot32(flat[...], w_ref[:, width:], (1, 1))
    input_ref[...] = (back_hidden_ref[...] + centre_back(back_normed * row(gain_ref), unit, scale)).astype(BF16)

    def put(at, line):
        for piece in range(per):
            lines[at + piece : at + piece + 1, :] = line[:, piece * LANES : (piece + 1) * LANES]

    put(0, jnp.sum(back_normed * unit, axis=0, keepdims=True))
    put(per, jnp.sum(back_normed, axis=0, keepdims=True))
    at = (2 + 3 * width) * per
    put(at, dot32(jnp.ones((8, rows), BF16), query, (1, 1))[0:1])
    put(at + per, jnp.sum(flat[:, width:].astype(F32), axis=0, keepdims=True))
    lines[at + 2 * per :, :] = jnp.zeros((lines.shape[0] - at - 2 * per, LANES), F32)
    core = info_ref[0] % 2

    def window(step, _):
        for ref, which in ((send_ref, 1 - core), (keep_ref, core)):
            write_window((2 * step + which) * size, lines, ref, step)
        return 0

    lax.fori_loop(0, LATE_CHUNKS // 2, window, 0)


def finish(size, info, x, gain, shift, w_qkv, back_hidden, back):
    rows, width = x.shape
    window = jax.ShapeDtypeStruct((LATE_CHUNKS // 2, LATE_WINDOW, LANES), BF16)
    shapes = [jax.ShapeDtypeStruct((rows, width), BF16), window, window]
    operands = [x, gain, shift, w_qkv, back_hidden, *back]
    scratch = [
        pltpu.VMEM((HEADS, HEAD_DIM, rows), BF16),
        pltpu.VMEM((rows, 2 * width), BF16),
        pltpu.VMEM((-(-(LATE_CHUNKS - 1) * size // 8) * 8 + LATE_WINDOW + 8, LANES), F32),
    ]
    kernel = functools.partial(finish_kernel, size)
    return one_step(kernel, info, operands, shapes, scratch, rows * width)


def along_g(values):
    return lax.all_to_all(values, "g", 0, 0, tiled=True)


def hold(values, after):
    return lax.optimization_barrier((values, list(after)))[0] if len(after) > 0 else values


def exchange(parts):
    return [lax.ppermute(part, ("x", "c"), [(i, i ^ n) for i in range(4)]) for part, n in zip(parts, (2, 1, 3))]


class Plane:
    def gather_keys(self, kv):
        return [kv[None], swap(kv, "f")[None]]

    def gather_queries(self, q):
        return [q] + exchange([q] * 3)

    gather_grads = gather_queries

    def gather_first(self, values):
        over = swap(values, "x")
        return [values, over, swap(values, "c"), swap(over, "c")]

    def gather_parts(self, outs):
        return [outs[0]] + exchange(outs[1:4])

    def gather_back(self, outs):
        kept, sent = outs[4][0], outs[5][0]
        shape = (kept.shape[0], -1, PAIR)
        return kept.reshape(shape), swap(sent, "f").reshape(shape), self.gather_parts(outs)

    def sum_back(self, after, parts):
        return sum_back(after, *parts)


class AnyPlane:
    def __init__(self, clips, times, part):
        self.clips, self.times, self.part = clips, times, part

    def split(self, values):
        groups, rows, width = values.shape
        values = values.reshape(groups, rows, self.clips, self.times, -1).transpose(3, 0, 1, 2, 4)
        return values.reshape(self.times, groups, rows, width // self.times)

    def gather_keys(self, kv):
        return [lax.all_gather(kv, "f")]

    def gather_queries(self, q):
        groups, tiles, rows, lanes = q.shape
        q = lax.all_gather(q.transpose(0, 2, 1, 3).reshape(groups, rows, -1, self.part), "t")
        return [q.transpose(1, 3, 2, 0, 4).reshape(groups, -1, rows, self.times * self.part)]

    def gather_grads(self, values):
        groups, rows, _ = values.shape
        values = lax.all_gather(values.reshape(groups, rows, -1, self.part), "t")
        return [values.transpose(1, 2, 3, 0, 4).reshape(groups, rows, -1)]

    gather_first = gather_grads

    def gather_parts(self, outs):
        return list(lax.all_to_all(self.split(outs[0]), "t", 0, 0, tiled=True))

    def gather_back(self, outs):
        return outs

    def sum_back(self, after, outs):
        back_q = lax.psum_scatter(self.split(outs[0]), "t", scatter_dimension=0, tiled=False)
        back_kv = lax.psum_scatter(outs[1], "f", scatter_dimension=0, tiled=False).reshape(GROUPS, -1, PAIR)
        back_q = back_q.reshape(GROUPS, HEAD_DIM, -1, LANES).transpose(0, 2, 1, 3).reshape(GROUPS, -1, LANES)
        return jnp.concatenate([back_kv, back_q], axis=1)


def layer_norm(values, scaling, offset):
    row_mean = jnp.mean(values, axis=-1, keepdims=True)
    centred = values - row_mean
    spread = jnp.mean(centred * centred, axis=-1, keepdims=True)
    return centred * lax.rsqrt(spread + EPSILON) * scaling + offset


def gelu_exact(values):
    return jax.nn.gelu(values, approximate=False)


def per_device(
    time_axes,
    tokens,
    out_grad,
    lengths,
    norm1_gain,
    norm1_shift,
    w_qkv,
    query_bias,
    value_bias,
    w_proj,
    proj_bias,
    norm2_gain,
    norm2_shift,
    w_fc1,
    fc1_bias,
    w_fc2,
    fc2_bias,
    moment,
    ema_decay,
):
    clips, freq_rows, frames, width = tokens.shape
    part = freq_rows * frames
    rows = clips * part
    times = lax.axis_size(time_axes)
    devices = lax.axis_size("f") * GROUPS * times
    early_index = lax.axis_index(time_axes)
    fast = time_axes == ("x", "c")
    plane = Plane() if fast else AnyPlane(clips, times, part)
    first_frame = (lax.axis_index("g") * times + early_index) * frames
    frame = first_frame + lax.broadcasted_iota(jnp.int32, (1, freq_rows, frames), 2)
    keep_rows = (frame < lengths[:, None, None]).astype(F32).reshape(rows, 1)
    info = jnp.concatenate([early_index.astype(jnp.int32).reshape(1), lengths])

    x = tokens.reshape(rows, width)
    packs = start(x, norm1_gain, norm1_shift, w_qkv, query_bias, value_bias)
    attended, kept = [], []

    def fetch(values, heads, after):
        got = along_g(values)
        pairs, queries = hold((got[:, : heads * rows], got[:, heads * rows :]), after)
        kv = plane.gather_keys(pairs.reshape(GROUPS, heads * clips, part, PAIR))
        return kv, plane.gather_queries(queries.reshape(GROUPS, -1, HEAD_DIM, LANES))

    def merged(after, parts):
        out, low = merge(parts, after)
        kept.append(out)
        attended.append(along_g(hold(low, attended[-1:])))
        return low

    def alone(head):
        return fast and head == GROUP_HEADS - 1

    def run(head, clip, outs, after):
        kv, q = fetched[min(head, 1)]
        place = max(head - 1, 0) * clips + clip
        outs, held = ((), 1) if alone(head) else (outs, clips)
        *outs, token = attend(info, kv, q, place, clip, held, times, frames, outs, after)
        return outs, token

    fetched = [fetch(packs[0], 1, [])]
    fetched.append(fetch(packs[1], GROUP_HEADS - 1, fetched[0][0][1:] + fetched[0][1][1:]))
    parts = None
    for head in range(GROUP_HEADS):
        outs, token = run(head, 0, (), [] if head == 0 else [token])
        after = [token]
        if head > 0:
            after.append(merged(token, parts))
        come = fetched[1][0][1:] + fetched[1][1][1:] if head == 0 else []
        if alone(head):
            half = plane.gather_parts(outs)
            come = half[1:]
        for clip in range(1, clips):
            outs, token = run(head, clip, outs, after)
        parts = plane.gather_parts(hold(outs, come))
    if fast:
        merged(token, half)
    merged(token, parts)
    if fast:
        size = moment.shape[0] // LANES
        block_out, back_hidden, early, grad = middle(
            x, out_grad.reshape(rows, width), keep_rows, w_proj, proj_bias, norm2_gain, norm2_shift, w_fc1, fc1_bias,
            w_fc2, fc2_bias, attended,
        )
        block_out = block_out.reshape(tokens.shape)
        early_windows = pack_early(devices, size, *early)
    else:
        attended_low = jnp.concatenate(attended, axis=1).reshape(width, rows)
        branch = dot32(attended_low, w_proj, (0, 0)) + proj_bias
        hidden = x.astype(F32) + branch
        normed2, norm2_pull = jax.vjp(layer_norm, hidden, norm2_gain, norm2_shift)
        normed2_low = normed2.astype(BF16)
        preactive = dot32(normed2_low, w_fc1, (1, 0)) + fc1_bias
        activated, gelu_pull = jax.vjp(gelu_exact, preactive)
        activated_low = activated.astype(BF16)
        branch2 = dot32(activated_low, w_fc2, (1, 0)) + fc2_bias
        block_out = ((hidden + branch2) * keep_rows).astype(BF16).reshape(tokens.shape)
        grad_out = out_grad.astype(F32).reshape(rows, width) * keep_rows
        back_branch2 = grad_out.astype(BF16)
        grad_fc2_bias = jnp.sum(back_branch2.astype(F32), axis=0)
        back_activated = dot32(back_branch2, w_fc2, (1, 1))
        back_preactive = gelu_pull(back_activated)[0].astype(BF16)
        grad_fc1_bias = jnp.sum(back_preactive.astype(F32), axis=0)
        back_normed2 = dot32(back_preactive, w_fc1, (1, 1))
        back_hidden_norm, grad_norm2_gain, grad_norm2_shift = norm2_pull(back_normed2)
        back_hidden = grad_out + back_hidden_norm
        back_branch = back_hidden.astype(BF16)
        grad_proj_bias = jnp.sum(back_branch.astype(F32), axis=0)
        back_attended = dot32(w_proj, back_branch, (1, 1)).astype(BF16)
        early_windows = info
        grad = back_attended.reshape(GROUPS, -1, rows)
    ready = grad_rows_of(along_g(grad), kept, early_windows)
    back, parts, token = [], None, None
    grads = plane.gather_first(ready[0])
    if fast:
        early_sum = hold(early_windows, grads[:1]).reshape(2, 2, 2, GROUPS, EARLY_WINDOW, LANES)
        early_sum = lax.psum_scatter(early_sum, "c", scatter_dimension=0, tiled=False)

    def run_back(head, clip, outs, after):
        kv, q = fetched[min(head, 1)]
        place = max(head - 1, 0) * clips + clip
        outs, held = ((), 1) if alone(head) else (outs, clips)
        *outs, token = attend_back(info, kv, q, grads, place, clip, held, times, frames, outs, after)
        return outs, token

    for head in range(GROUP_HEADS):
        outs, token = run_back(head, 0, (), [] if head == 0 else [token])
        after = [token]
        if head > 0:
            after += [plane.sum_back(token, parts)] + back
            back.append(along_g(hold(after[1], back)))
        if fast and head == 0:
            early_sum = hold(early_sum, [token])
            after.append(early_sum)
        come = []
        if head + 1 < GROUP_HEADS:
            later = plane.gather_grads(hold(ready[head + 1], after))
            come = later[1:]
        if alone(head):
            half = plane.gather_back(outs)
            come = [half[1]] + half[2][1:]
        for clip in range(1, clips):
            outs, token = run_back(head, clip, outs, after)
        outs = hold(outs, come)
        if fast and head == 0:
            early_sum = hold(early_sum, come + [token]).reshape(4, GROUPS, EARLY_WINDOW, LANES)
            early_sum = lax.psum_scatter(early_sum, ("x", "f"), scatter_dimension=0, tiled=False)
        if head + 1 < GROUP_HEADS:
            grads = later
        parts = plane.gather_back(outs)
    if fast:
        back.append(along_g(hold(plane.sum_back(token, half), back[-1:])))
    back.append(along_g(hold(plane.sum_back(token, parts), back[-1:])))
    if fast:
        input_grad, *late_windows = finish(
            size, info, x, norm1_gain, norm1_shift, w_qkv, back_hidden, back
        )
        input_grad = input_grad.reshape(tokens.shape)
        early_sum = lax.psum_scatter(hold(early_sum, [back[-1]]), "g", scatter_dimension=0, tiled=False).astype(F32)
        late_sum = reduce_late(*late_windows, early_sum)
        weight_grad = own_chunk(lax.optimization_barrier(early_sum), late_sum, moment.shape[0])
    else:
        back = jnp.stack(back, axis=1)
        back_kv = back[:, :, :rows].transpose(2, 0, 1, 3).reshape(rows, 2 * width)
        back_q = back[:, :, rows:].reshape(GROUPS, GROUP_HEADS, -1, HEAD_DIM, LANES).transpose(0, 1, 3, 2, 4).reshape(width, rows)
        grad_query_bias = jnp.sum(back_q.astype(F32), axis=1)
        grad_kv_bias = jnp.sum(back_kv.astype(F32), axis=0)
        grad_value_bias = grad_kv_bias.reshape(HEADS, 2, HEAD_DIM)[:, 1].reshape(width)
        normed, norm1_pull = jax.vjp(layer_norm, x.astype(F32), norm1_gain, norm1_shift)
        normed_low = normed.astype(BF16)
        head_dims = (width, GROUPS, GROUP_HEADS, HEAD_DIM)
        w_q = w_qkv[:, :width]
        w_kv = [w_qkv[:, width : 2 * width].reshape(head_dims), w_qkv[:, 2 * width :].reshape(head_dims)]
        w_kv = jnp.stack(w_kv, axis=3).reshape(width, 2 * width)
        back_normed = dot32(back_q, w_q, (0, 1)) + dot32(back_kv, w_kv, (1, 1))
        back_input_norm, grad_norm1_gain, grad_norm1_shift = norm1_pull(back_normed)
        input_grad = (back_hidden + back_input_norm).astype(BF16).reshape(tokens.shape)
        grad_proj = dot32(attended_low, back_branch, (1, 0))
        grad_fc1 = dot32(normed2_low, back_preactive, (0, 0))
        grad_fc2 = dot32(activated_low, back_branch2, (0, 0))
        grad_q = dot32(normed_low, back_q, (0, 1))
        grad_kv = dot32(normed_low, back_kv, (0, 0)).reshape(width, HEADS, 2, HEAD_DIM)
        grad_qkv = jnp.concatenate([grad_q, grad_kv[:, :, 0].reshape(width, width), grad_kv[:, :, 1].reshape(width, width)], axis=1)
        joined = jnp.concatenate(
            [
                grad_norm1_gain,
                grad_norm1_shift,
                grad_qkv.reshape(-1),
                grad_query_bias,
                grad_value_bias,
                grad_proj.reshape(-1),
                grad_proj_bias,
                grad_norm2_gain,
                grad_norm2_shift,
                grad_fc1.reshape(-1),
                grad_fc1_bias,
                grad_fc2.reshape(-1),
                grad_fc2_bias,
            ]
        ).astype(BF16)
        padding = moment.shape[0] * devices - joined.shape[0]
        joined = jnp.concatenate([joined, jnp.zeros((padding,), BF16)])
        weight_grad = lax.psum_scatter(joined, ("f", "g") + time_axes, scatter_dimension=0, tiled=True).astype(F32)
    new_moment = ema_decay[0] * moment + (1.0 - ema_decay[0]) * weight_grad
    return (block_out, input_grad, weight_grad, new_moment)


def solution(mesh):
    freqs, times = mesh.shape["freq"], mesh.shape["tm"]
    if (freqs, times) == (2, 16):
        time_sizes, time_axes = (2, 2), ("x", "c")
    else:
        time_sizes, time_axes = (times // GROUPS,), ("t",)
    fine = Mesh(mesh.devices.reshape(freqs, GROUPS, *time_sizes), ("f", "g") + time_axes)
    patches = P(None, "f", ("g",) + time_axes, None)
    flat = P(("f", "g") + time_axes)
    return jax.shard_map(
        functools.partial(per_device, time_axes),
        mesh=fine,
        in_specs=(patches, patches) + (P(),) * 14 + (flat, P()),
        out_specs=(patches, patches, flat, flat),
        check_vma=False,
    )
```

```python
import functools
import math

import jax
import jax.numpy as jnp
from jax import lax
from jax.experimental import pallas as pl
from jax.experimental.pallas import tpu as pltpu
from jax.sharding import Mesh
from jax.sharding import PartitionSpec as P

HEADS = 12
HEAD_DIM = 64
GROUPS = 4
GROUP_HEADS = HEADS // GROUPS
PAIR = 2 * HEAD_DIM
LANES = 128
OUT_ROWS = HEAD_DIM + 8
GRAD_ROWS = HEAD_DIM + 16
EPSILON = 1e-06
NEGATIVE = -1e30
LOG2E = math.log2(math.e)
LN2 = math.log(2.0)
SCALE = HEAD_DIM**-0.5
VMEM_LIMIT = 60 * 2**20
BF16 = jnp.bfloat16
F32 = jnp.float32


TOKEN = jax.ShapeDtypeStruct((8, LANES), F32)
TOKEN_SPEC = pl.BlockSpec((8, LANES), lambda i, *_: (0, 0))


def dot32(left, right, contract):
    return lax.dot_general(left, right, ((contract[:1], contract[1:]), ((), ())), preferred_element_type=F32)


def work(info_ref, clip, times, frames):
    t, full, rest = info_ref[0], info_ref[1 + clip] // frames, info_ref[1 + clip] % frames
    live = full + (rest > 0).astype(jnp.int32)
    query_blocks = (live + times - 1) // times
    key_blocks = jnp.maximum(full - t + times - 1, 0) // times
    partial = (rest > 0) & (full % times == t)
    return query_blocks, key_blocks, partial, rest


def joined(ref, late):
    tiles = [ref[late, j] for j in range(ref.shape[1])]
    return tiles[0] if len(tiles) == 1 else jnp.concatenate(tiles, axis=1)


def load_pairs(kv_refs, slot):
    return [ref[f, slot, 0] for ref in kv_refs for f in range(ref.shape[0])]


def attend_kernel(clip, times, frames, n_kv, n_q, n_out, info_ref, *refs):
    kv_refs, q_refs, refs = refs[:n_kv], refs[n_kv : n_kv + n_q], refs[n_kv + n_q :]
    refs = refs[-n_out - 6 :]
    out_refs, (token_ref, acc, top, q_pad, scores, tops) = refs[:n_out], refs[n_out:]
    token_ref[...] = jnp.zeros_like(token_ref)
    query_blocks, key_blocks, partial, rest = work(info_ref, clip, times, frames)
    width = q_refs[0].shape[1] * q_refs[0].shape[3]
    rows = scores.shape[1]
    for late in range(GROUPS):
        for p, ref in enumerate(q_refs):
            q_pad[late, :HEAD_DIM, p * width : (p + 1) * width] = joined(ref, late)
        q_pad[late, HEAD_DIM:, :] = jnp.zeros((HEAD_DIM, q_pad.shape[2]), BF16)
    acc[...] = jnp.zeros_like(acc)
    top[...] = jnp.full_like(top, NEGATIVE)
    ones = jnp.ones((16, rows), BF16)

    def load(block):
        return jnp.concatenate(load_pairs(kv_refs, block), axis=0)

    def consume(u, pair, block_scores, block_top):
        old = top[u]
        new = jnp.maximum(old, block_top)
        probs = jnp.exp2(block_scores - new).astype(BF16)
        top[u] = new
        values = jnp.concatenate([pair.T[HEAD_DIM:], ones], axis=0)
        acc[u] = acc[u] * jnp.exp2(old - new) + dot32(values, probs, (1, 0))

    def masked(u, _):
        pair = load(key_blocks)
        alive = lax.broadcasted_iota(jnp.int32, (rows, 1), 0) % frames < rest
        block_scores = jnp.where(alive, dot32(pair, q_pad[u], (1, 0)), NEGATIVE)
        consume(u, pair, block_scores, jnp.max(block_scores, axis=0, keepdims=True))
        return 0

    lax.fori_loop(0, jnp.where(partial, query_blocks, 0), masked, 0)
    total = query_blocks * key_blocks
    per = jnp.maximum(key_blocks, 1)

    def score(step, slot):
        block_scores = dot32(load(step % per), q_pad[step // per], (1, 0))
        scores[slot] = block_scores
        tops[slot] = jnp.max(block_scores, axis=0, keepdims=True)

    @pl.when(total > 0)
    def _():
        score(0, 0)

    def two_steps(double, _):
        for slot in range(2):
            step = 2 * double + slot
            score(jnp.minimum(step + 1, total - 1), 1 - slot)
            consume(step // per, load(step % per), scores[slot], tops[slot])
        return 0

    lax.fori_loop(0, total // 2, two_steps, 0)

    @pl.when(total % 2 == 1)
    def _():
        consume((total - 1) // per, load((total - 1) % per), scores[0], tops[0])

    for late in range(GROUPS):
        norm = acc[late, HEAD_DIM : HEAD_DIM + 1, :]
        some = norm > 0.0
        safe = jnp.where(some, norm, 1.0)
        out = acc[late, :HEAD_DIM, :] / safe
        lse = jnp.where(some, top[late] + jnp.log2(safe), NEGATIVE)
        fill = jnp.zeros((GRAD_ROWS - HEAD_DIM - 3, out.shape[1]), F32)
        full = jnp.concatenate([out, thirds(lse), fill], axis=0).astype(BF16)
        for p, ref in enumerate(out_refs):
            ref[late] = full[:, p * width : (p + 1) * width]


def specs_of(kv, q, place, places):
    kv_specs = [pl.BlockSpec((a.shape[0], GROUPS, 1, *a.shape[3:]), lambda i, *_: (0, 0, place, 0, 0)) for a in kv]
    _, tiles, _, lanes = q[0].shape
    q_specs = [pl.BlockSpec((GROUPS, tiles // places, HEAD_DIM, lanes), lambda i, *_: (0, place, 0, 0)) for a in q]
    return kv_specs, q_specs, tiles * lanes // places


def attend(info, kv, q, place, clip, clips, times, frames, before, after):
    kv_specs, q_specs, width = specs_of(kv, q, place, kv[0].shape[2])
    queries = len(q) * width
    rows = sum(a.shape[0] for a in kv) * kv[0].shape[3]
    pairs = GROUPS * rows * GROUPS * queries
    out_specs = [pl.BlockSpec((GROUPS, GRAD_ROWS, width), lambda i, *_: (0, 0, clip % clips))] * len(q) + [TOKEN_SPEC]
    n_in = 1 + len(kv) + len(q)
    return pl.pallas_call(
        functools.partial(attend_kernel, clip, times, frames, len(kv), len(q), len(q)),
        grid_spec=pltpu.PrefetchScalarGridSpec(
            num_scalar_prefetch=1,
            grid=(1,),
            in_specs=kv_specs + q_specs + [pl.BlockSpec(memory_space=pl.ANY)] * (len(before) + len(after)),
            out_specs=out_specs,
            scratch_shapes=[
                pltpu.VMEM((GROUPS, GRAD_ROWS, queries), F32),
                pltpu.VMEM((GROUPS, 1, queries), F32),
                pltpu.VMEM((GROUPS, PAIR, queries), BF16),
                pltpu.VMEM((2, rows, queries), F32),
                pltpu.VMEM((2, 1, queries), F32),
            ],
        ),
        out_shape=[jax.ShapeDtypeStruct((GROUPS, GRAD_ROWS, clips * width), BF16)] * len(q) + [TOKEN],
        input_output_aliases={n_in + i: i for i in range(len(before))},
        compiler_params=pltpu.CompilerParams(vmem_limit_bytes=VMEM_LIMIT),
        cost_estimate=pl.CostEstimate(flops=256 * pairs, bytes_accessed=pairs // 16, transcendentals=pairs),
    )(info, *kv, *q, *before, *after)


def attend_back_kernel(clip, times, frames, cuts, n_kv, n_q, n_out, info_ref, *refs):
    kv_refs, q_refs, grad_refs = refs[:n_kv], refs[n_kv : n_kv + n_q], refs[n_kv + n_q : n_kv + 2 * n_q]
    refs = refs[-n_out - n_kv - 7 :]
    back_q_refs, back_kv_refs, refs = refs[:n_out], refs[n_out : n_out + n_kv], refs[n_out + n_kv :]
    refs[0][...] = jnp.zeros_like(refs[0])
    _, back_q, back_kv, q_cols, grad_cols, lse, delta = refs
    query_blocks, key_blocks, partial, rest = work(info_ref, clip, times, frames)
    width = grad_refs[0].shape[-1]
    part_rows = kv_refs[0].shape[3]
    rows = back_kv.shape[1]
    cut = rows // cuts
    zero = jnp.zeros((HEAD_DIM, width), BF16)

    def prepare(late, _):
        for p, (q_ref, grad_ref) in enumerate(zip(q_refs, grad_refs)):
            cols = slice(p * width, (p + 1) * width)
            q_cols[late, :, cols] = jnp.concatenate([joined(q_ref, late), zero], axis=0)
            grad_cols[late, :, cols] = jnp.concatenate([zero, grad_ref[late, :HEAD_DIM]], axis=0)
            extra = grad_ref[late, HEAD_DIM:].astype(F32)
            lse[late, :, cols] = extra[0:1] + extra[1:2] + extra[2:3]
            delta[late, :, cols] = extra[3:4] + extra[4:5] + extra[5:6]
        return 0

    lax.fori_loop(0, query_blocks, prepare, 0)
    back_q[...] = jnp.zeros_like(back_q)
    back_kv[...] = jnp.zeros_like(back_kv)

    def step(u, block, masked):
        pairs = load_pairs(kv_refs, block)
        for k in range(cuts):
            part = pairs[k * len(pairs) // cuts : (k + 1) * len(pairs) // cuts]
            pair = part[0] if len(part) == 1 else jnp.concatenate(part, axis=0)
            probs = jnp.exp2(dot32(pair, q_cols[u], (1, 0)) - lse[u])
            if masked:
                row = lax.broadcasted_iota(jnp.int32, (cut, 1), 0)
                probs = jnp.where(row % frames < rest, probs, 0.0)
            back_probs = dot32(pair, grad_cols[u], (1, 0))
            back_scores = (probs * (back_probs - delta[u])).astype(BF16)
            back_pair = dot32(probs.astype(BF16), grad_cols[u], (1, 1)) + dot32(back_scores, q_cols[u], (1, 1))
            back_q[u] += dot32(pair, back_scores, (0, 0))
            back_kv[block, k * cut : (k + 1) * cut, :] += back_pair
        return 0

    lax.fori_loop(0, jnp.where(partial, query_blocks, 0), lambda u, _: step(u, key_blocks, True), 0)
    per = jnp.maximum(key_blocks, 1)
    lax.fori_loop(0, query_blocks * key_blocks, lambda i, _: step(i // per, i % per, False), 0)
    is_key = lax.broadcasted_iota(jnp.int32, (1, PAIR), 1) < HEAD_DIM
    factor = jnp.where(is_key, jnp.float32(LN2), jnp.float32(1.0))
    for late in range(GROUPS):
        for p, ref in enumerate(back_q_refs):
            ref[late] = (back_q[late, :HEAD_DIM, p * width : (p + 1) * width] * SCALE).astype(BF16)
        p = 0
        for ref in back_kv_refs:
            for f in range(ref.shape[0]):
                ref[f, late, 0] = (back_kv[late, p * part_rows : (p + 1) * part_rows, :] * factor).astype(BF16)
                p += 1


def attend_back(info, kv, q, grad, place, clip, clips, times, frames, before, after):
    kv_specs, q_specs, width = specs_of(kv, q, place, kv[0].shape[2])
    queries = len(q) * width
    rows = sum(a.shape[0] for a in kv) * kv[0].shape[3]
    pairs = GROUPS * rows * GROUPS * queries
    grad_specs = [pl.BlockSpec((GROUPS, GRAD_ROWS, width), lambda i, *_: (0, 0, clip)) for a in grad]
    q_out = [pl.BlockSpec((GROUPS, HEAD_DIM, width), lambda i, *_: (0, 0, clip % clips))] * len(q)
    kv_out = [pl.BlockSpec((a.shape[0], GROUPS, 1, *a.shape[3:]), lambda i, *_: (0, 0, clip % clips, 0, 0)) for a in kv]
    n_in = 1 + len(kv) + len(q) + len(grad)
    return pl.pallas_call(
        functools.partial(attend_back_kernel, clip, times, frames, 2, len(kv), len(q), len(q)),
        grid_spec=pltpu.PrefetchScalarGridSpec(
            num_scalar_prefetch=1,
            grid=(1,),
            in_specs=kv_specs + q_specs + grad_specs + [pl.BlockSpec(memory_space=pl.ANY)] * (len(before) + len(after)),
            out_specs=q_out + kv_out + [TOKEN_SPEC],
            scratch_shapes=[
                pltpu.VMEM((GROUPS, PAIR, queries), F32),
                pltpu.VMEM((GROUPS, rows, PAIR), F32),
                pltpu.VMEM((GROUPS, PAIR, queries), BF16),
                pltpu.VMEM((GROUPS, PAIR, queries), BF16),
                pltpu.VMEM((GROUPS, 1, queries), F32),
                pltpu.VMEM((GROUPS, 1, queries), F32),
            ],
        ),
        out_shape=[jax.ShapeDtypeStruct((GROUPS, HEAD_DIM, clips * width), BF16)] * len(q)
        + [jax.ShapeDtypeStruct((a.shape[0], GROUPS, clips, *a.shape[3:]), BF16) for a in kv]
        + [TOKEN],
        input_output_aliases={n_in + i: i for i in range(len(before))},
        compiler_params=pltpu.CompilerParams(vmem_limit_bytes=VMEM_LIMIT),
        cost_estimate=pl.CostEstimate(flops=640 * pairs, bytes_accessed=pairs // 8, transcendentals=pairs),
    )(info, *kv, *q, *grad, *before, *after)


def thirds(values):
    high = values.astype(BF16).astype(F32)
    middle = (values - high).astype(BF16).astype(F32)
    return jnp.concatenate([high, middle, values - high - middle], axis=0)


def merge_kernel(_, *refs):
    part_refs, (out_ref, low_ref) = refs[:-2], refs[-2:]
    for n in range(GROUPS):
        parts = [ref[n].astype(F32) for ref in part_refs]
        lses = [p[HEAD_DIM : HEAD_DIM + 1] + p[HEAD_DIM + 1 : HEAD_DIM + 2] + p[HEAD_DIM + 2 : HEAD_DIM + 3] for p in parts]
        most = functools.reduce(jnp.maximum, lses)
        shares = [jnp.exp2(lse - most) for lse in lses]
        total = sum(shares)
        out = sum(p[:HEAD_DIM] * share for p, share in zip(parts, shares)) / total
        low_ref[n] = out.astype(BF16)
        out_ref[n, :HEAD_DIM] = out
        out_ref[n, HEAD_DIM:] = jnp.broadcast_to(most + jnp.log2(total), (OUT_ROWS - HEAD_DIM, out.shape[1]))


def merge(parts, after):
    _, _, width = parts[0].shape
    return pl.pallas_call(
        merge_kernel,
        in_specs=[pl.BlockSpec(memory_space=pl.ANY)] + [pl.BlockSpec(memory_space=pltpu.VMEM)] * len(parts),
        out_shape=[jax.ShapeDtypeStruct((GROUPS, OUT_ROWS, width), F32), jax.ShapeDtypeStruct((GROUPS, HEAD_DIM, width), BF16)],
        compiler_params=pltpu.CompilerParams(vmem_limit_bytes=VMEM_LIMIT),
    )(after, *parts)


def grad_rows_kernel(n_out, grad_ref, *refs):
    out_refs, ready_refs = refs[:n_out], refs[-GROUP_HEADS:]
    for head in range(GROUP_HEADS):
        for n in range(GROUPS):
            grad = grad_ref[n, head * HEAD_DIM : (head + 1) * HEAD_DIM].astype(F32)
            out = out_refs[head][n]
            if head == GROUP_HEADS - 1 and n_out > GROUP_HEADS:
                out = jnp.concatenate([ref[n] for ref in out_refs[head:]], axis=1)
            delta = jnp.sum(grad * out[:HEAD_DIM], axis=0, keepdims=True)
            fill = jnp.zeros((GRAD_ROWS - HEAD_DIM - 6, grad.shape[1]), F32)
            rows = jnp.concatenate([grad, thirds(out[HEAD_DIM : HEAD_DIM + 1]), thirds(delta), fill], axis=0)
            ready_refs[head][n] = rows.astype(BF16)


def grad_rows_of(grad, outs, after):
    width = grad.shape[-1]
    whole = pl.BlockSpec(memory_space=pltpu.VMEM)
    return pl.pallas_call(
        functools.partial(grad_rows_kernel, len(outs)),
        in_specs=[whole] * (1 + len(outs)) + [pl.BlockSpec(memory_space=pl.ANY)],
        out_shape=[jax.ShapeDtypeStruct((GROUPS, GRAD_ROWS, width), BF16)] * GROUP_HEADS,
        compiler_params=pltpu.CompilerParams(vmem_limit_bytes=VMEM_LIMIT),
    )(grad, *outs, after)


def sum_back_kernel(_, kept_ref, came_ref, *refs):
    q_refs, ready_ref = refs[:-1], refs[-1]
    rows = kept_ref.shape[1]
    for n in range(GROUPS):
        ready_ref[n, :rows] = (kept_ref[n].astype(F32) + came_ref[n].astype(F32)).astype(BF16)
        query = sum(ref[n].astype(F32) for ref in q_refs).astype(BF16)
        for j in range(rows // LANES):
            at = rows + j * HEAD_DIM
            ready_ref[n, at : at + HEAD_DIM] = query[:, j * LANES : (j + 1) * LANES]


def sum_back(after, kept, came, queries):
    groups, rows, _ = kept.shape
    return pl.pallas_call(
        sum_back_kernel,
        in_specs=[pl.BlockSpec(memory_space=pl.ANY)] + [pl.BlockSpec(memory_space=pltpu.VMEM)] * (2 + len(queries)),
        out_shape=jax.ShapeDtypeStruct((groups, rows + rows // LANES * HEAD_DIM, LANES), BF16),
        compiler_params=pltpu.CompilerParams(vmem_limit_bytes=VMEM_LIMIT),
    )(after, kept, came, *queries)


def spread(lines, at, stride, values):
    rows, width = values.shape
    for piece in range(width // LANES):
        lines[pl.ds(at + piece, rows, stride=stride), :] = values[:, piece * LANES : (piece + 1) * LANES]


def write_window(start, lines, ref, at=0):
    skip = start % 8
    rows = ref.shape[1]
    base = pl.multiple_of(start - skip, 8)
    for s in range(8):

        @pl.when(skip == s)
        def _():
            ref[at] = lines[pl.ds(base, rows + 8), :][s : s + rows].astype(BF16)


def pack_early_kernel(size, att_ref, branch_ref, normed_ref, pre_ref, act_ref, out_ref, vec_ref, window_ref, lines):
    step = pl.program_id(0)

    @pl.when(step == 0)
    def _():
        width = branch_ref.shape[1]
        blocks = pre_ref.shape[1] // width
        per = width // LANES
        spread(lines, 0, per, dot32(att_ref[...], branch_ref[...], (1, 0)))
        at = width * per
        lines[at : at + 3 * per, :] = vec_ref[0 : 3 * per]
        at += 3 * per
        for b in range(blocks):
            cols = slice(b * width, (b + 1) * width)
            spread(lines, at + b * per, blocks * per, dot32(normed_ref[...], pre_ref[:, cols], (0, 0)))
        at += blocks * width * per
        lines[at : at + blocks * per, :] = vec_ref[3 * per : (3 + blocks) * per]
        at += blocks * per
        for b in range(blocks):
            cols = slice(b * width, (b + 1) * width)
            spread(lines, at + b * width * per, per, dot32(act_ref[:, cols], out_ref[...], (0, 0)))
        at += blocks * width * per
        lines[at : at + per, :] = vec_ref[(3 + blocks) * per :]
        lines[at + per :, :] = jnp.zeros((lines.shape[0] - at - per, LANES), F32)

    write_window(step * size, lines, window_ref)


def early_order(chunk):
    f, g, x, c = chunk // 16, chunk // 4 % 4, chunk // 2 % 2, chunk % 2
    return ((c * 2 + x) * 2 + f) * 4 + g


def pack_early(devices, size, *operands):
    chunks = devices - LATE_CHUNKS
    whole = [pl.BlockSpec(a.shape, lambda j: (0, 0)) for a in operands]
    entries = chunks * size * LANES
    return pl.pallas_call(
        functools.partial(pack_early_kernel, size),
        grid=(chunks,),
        in_specs=whole,
        out_specs=pl.BlockSpec((1, EARLY_WINDOW, LANES), lambda j: (early_order(j + LATE_CHUNKS), 0, 0)),
        scratch_shapes=[pltpu.VMEM((-(-(chunks - 1) * size // 8) * 8 + EARLY_WINDOW + 8, LANES), F32)],
        out_shape=jax.ShapeDtypeStruct((devices, EARLY_WINDOW, LANES), BF16),
        compiler_params=pltpu.CompilerParams(vmem_limit_bytes=VMEM_LIMIT),
        cost_estimate=pl.CostEstimate(flops=1024 * entries, bytes_accessed=4 * entries, transcendentals=0),
    )(*operands)


SWAP = [(0, 1), (1, 0)]


def swap(values, axis):
    return lax.ppermute(values, axis, SWAP)


def add(left, right):
    return (left.astype(F32) + right.astype(F32)).astype(BF16)


def trade(values, dim, keep, axis):
    sent = lax.dynamic_index_in_dim(values, 1 - keep, dim, keepdims=False)
    kept = lax.dynamic_index_in_dim(values, keep, dim, keepdims=False)
    return add(kept, swap(sent, axis))


EARLY_WINDOW = 1744
LATE_CHUNKS = 8
LATE_WINDOW = 1792


def reduce_late(send, keep, after):
    f, x = lax.axis_index("f"), lax.axis_index("x")
    pairs = add(keep, swap(send, "c")).reshape(2, 2, 4, -1, LANES)
    first = trade(trade(pairs[:, :, :2], 1, x, "x"), 1, f, "f")
    second = trade(trade(pairs[:, :, 2:], 2, f, "f"), 1, x, "x")
    parts = along_g(jnp.stack([first[0], first[1], second[1], second[0]]))
    mine = sum(parts[n].astype(F32) for n in range(GROUPS)).astype(BF16)
    mine = hold(mine, [after])
    routes = ([(4, 0), (5, 1)], [(2, 1), (3, 0)], [(6, 1), (7, 0)])
    came = [lax.ppermute(mine, ("f", "g"), route) for route in routes]
    return jnp.concatenate([mine] + came, axis=0).astype(F32)


def own_chunk(early, late, size):
    is_late = (lax.axis_index("f") == 0) & (lax.axis_index("g") < 2)
    return jnp.where(is_late, late[: size // LANES], early[: size // LANES]).reshape(size)


def centre(values):
    centred = values - jnp.mean(values, axis=-1, keepdims=True)
    scale = lax.rsqrt(jnp.mean(centred * centred, axis=-1, keepdims=True) + EPSILON)
    return centred * scale, scale


def centre_back(grad, unit, scale):
    mean = jnp.mean(grad, axis=-1, keepdims=True)
    along = jnp.mean(grad * unit, axis=-1, keepdims=True)
    return scale * (grad - mean - unit * along)


def row(ref):
    return ref[...].reshape(1, -1)


def swap_halves(values):
    return pltpu.roll(values, HEAD_DIM, axis=1)


def start_kernel(x_ref, gain_ref, shift_ref, w_ref, query_bias_ref, value_bias_ref, *refs):
    rows, width = x_ref.shape

    def put(head, values):
        at = max(head % GROUP_HEADS - 1, 0) * rows
        refs[min(head % GROUP_HEADS, 1)][head // GROUP_HEADS, at : at + rows] = values.astype(BF16)

    unit, _ = centre(x_ref[...].astype(F32))
    normed = (unit * row(gain_ref) + row(shift_ref)).astype(BF16)
    keys = dot32(normed, w_ref[:, width : 2 * width], (1, 0))
    values = dot32(normed, w_ref[:, 2 * width :], (1, 0)) + row(value_bias_ref)
    is_key = lax.broadcasted_iota(jnp.int32, (1, PAIR), 1) < HEAD_DIM
    for j in range(HEADS // 2):
        key, value = keys[:, j * PAIR : (j + 1) * PAIR], values[:, j * PAIR : (j + 1) * PAIR]
        put(2 * j, jnp.where(is_key, key, swap_halves(value)))
        put(2 * j + 1, jnp.where(is_key, swap_halves(key), value))
    query = (dot32(normed, w_ref[:, :width], (1, 0)) + row(query_bias_ref)) * (SCALE * LOG2E)
    query = query.astype(BF16).T
    for head in range(HEADS):
        part = query[head * HEAD_DIM : (head + 1) * HEAD_DIM]
        ref = refs[min(head % GROUP_HEADS, 1)]
        first = ref.shape[1] // (rows + rows // LANES * HEAD_DIM) * rows
        first += max(head % GROUP_HEADS - 1, 0) * rows // LANES * HEAD_DIM
        for tile in range(rows // LANES):
            at = first + tile * HEAD_DIM
            ref[head // GROUP_HEADS, at : at + HEAD_DIM] = part[:, tile * LANES : (tile + 1) * LANES]


def one_step(kernel, info, operands, shapes, scratch, flops):
    scalars = [] if info is None else [info]
    return pl.pallas_call(
        kernel,
        grid_spec=pltpu.PrefetchScalarGridSpec(
            num_scalar_prefetch=len(scalars),
            grid=(1,),
            in_specs=[pl.BlockSpec(a.shape, lambda i, *_, n=a.ndim: (0,) * n) for a in operands],
            out_specs=[pl.BlockSpec(a.shape, lambda i, *_, n=len(a.shape): (0,) * n) for a in shapes],
            scratch_shapes=scratch,
        ),
        out_shape=shapes,
        compiler_params=pltpu.CompilerParams(vmem_limit_bytes=VMEM_LIMIT),
        cost_estimate=pl.CostEstimate(flops=flops, bytes_accessed=flops // 500, transcendentals=0),
    )(*scalars, *operands)


def start(x, gain, shift, w_qkv, query_bias, value_bias):
    rows, width = x.shape
    height = rows + rows // LANES * HEAD_DIM
    shapes = [jax.ShapeDtypeStruct((GROUPS, n * height, LANES), BF16) for n in (1, GROUP_HEADS - 1)]
    operands = (x, gain, shift, w_qkv, query_bias, value_bias)
    return one_step(start_kernel, None, operands, shapes, [], 2 * rows * width * 3 * width)


def middle_kernel(
    x_ref, out_grad_ref, keep_ref, w_proj_ref, proj_bias_ref, gain_ref, shift_ref, w_fc1_ref, fc1_bias_ref, w_fc2_ref,
    fc2_bias_ref, *refs,
):
    attended_refs, refs = refs[: GROUP_HEADS + 1], refs[GROUP_HEADS + 1 :]
    mixed_ref, back_hidden_ref, att_ref, branch_ref, normed_ref, pre_ref, act_ref, out_ref, vec_ref = refs[:9]
    grad_ref, heads = refs[9:]
    width = x_ref.shape[1]
    rows = x_ref.shape[0]
    per = width // LANES
    for head in range(HEADS):
        group, place = head // GROUP_HEADS, head % GROUP_HEADS
        if place < GROUP_HEADS - 1:
            heads[head] = attended_refs[place][group]
        else:
            heads[head, :, : rows // 2] = attended_refs[place][group]
            heads[head, :, rows // 2 :] = attended_refs[place + 1][group]
    attended = heads[...].reshape(width, rows)
    att_ref[...] = attended
    keep = keep_ref[...]
    hidden = x_ref[...].astype(F32) + (dot32(attended, w_proj_ref[...], (0, 0)) + row(proj_bias_ref))
    unit, scale = centre(hidden)
    normed = (unit * row(gain_ref) + row(shift_ref)).astype(BF16)
    normed_ref[...] = normed
    grad_out = out_grad_ref[...].astype(F32) * keep
    low_out = grad_out.astype(BF16)
    out_ref[...] = low_out
    branch2 = jnp.zeros((rows, width), F32)
    back_normed = jnp.zeros((rows, width), F32)

    def put(at, line):
        for piece in range(line.shape[1] // LANES):
            vec_ref[at + piece : at + piece + 1, :] = line[:, piece * LANES : (piece + 1) * LANES]

    blocks = pre_ref.shape[1] // width
    for b in range(blocks):
        cols = slice(b * width, (b + 1) * width)
        pre = dot32(normed, w_fc1_ref[:, cols], (1, 0)) + row(fc1_bias_ref)[:, cols]
        share = 0.5 * (1.0 + lax.erf(pre * (0.5**0.5)))
        low_act = (pre * share).astype(BF16)
        act_ref[:, cols] = low_act
        branch2 += dot32(low_act, w_fc2_ref[cols, :], (1, 0))
        slope = share + pre * jnp.exp(-0.5 * pre * pre) * ((2.0 * math.pi) ** -0.5)
        back_pre = (dot32(low_out, w_fc2_ref[cols, :], (1, 1)) * slope).astype(BF16)
        pre_ref[:, cols] = back_pre
        put((3 + b) * per, jnp.sum(back_pre.astype(F32), axis=0, keepdims=True))
        back_normed += dot32(back_pre, w_fc1_ref[:, cols], (1, 1))
    mixed_ref[...] = ((hidden + (branch2 + row(fc2_bias_ref))) * keep).astype(BF16)
    put((3 + blocks) * per, jnp.sum(low_out.astype(F32), axis=0, keepdims=True))
    put(per, jnp.sum(back_normed * unit, axis=0, keepdims=True))
    put(2 * per, jnp.sum(back_normed, axis=0, keepdims=True))
    back_hidden = grad_out + centre_back(back_normed * row(gain_ref), unit, scale)
    back_hidden_ref[...] = back_hidden
    branch = back_hidden.astype(BF16)
    branch_ref[...] = branch
    put(0, jnp.sum(branch.astype(F32), axis=0, keepdims=True))
    back_attended = dot32(w_proj_ref[...], branch, (1, 1)).astype(BF16)
    grad_ref[...] = back_attended.reshape(grad_ref.shape)


def middle(x, out_grad, keep, w_proj, proj_bias, gain, shift, w_fc1, fc1_bias, w_fc2, fc2_bias, attended):
    rows, width = x.shape
    ff = w_fc1.shape[1]
    low = lambda *shape: jax.ShapeDtypeStruct(shape, BF16)
    shapes = [
        low(rows, width), jax.ShapeDtypeStruct((rows, width), F32), low(width, rows), low(rows, width), low(rows, width),
        low(rows, ff), low(rows, ff), low(rows, width), jax.ShapeDtypeStruct(((4 * width + ff) // LANES, LANES), F32),
        low(GROUPS, width // GROUPS, rows),
    ]
    operands = [x, out_grad, keep, w_proj, proj_bias, gain, shift, w_fc1, fc1_bias, w_fc2, fc2_bias]
    operands += attended
    scratch = [pltpu.VMEM((HEADS, HEAD_DIM, rows), BF16)]
    outs = one_step(middle_kernel, None, operands, shapes, scratch, 2 * rows * width * (2 * width + 4 * ff))
    return outs[0], outs[1], outs[2:9], outs[9]


def finish_kernel(size, info_ref, x_ref, gain_ref, shift_ref, w_ref, back_hidden_ref, *refs):
    back_refs, (input_ref, send_ref, keep_ref, queries, flat, lines) = refs[: GROUP_HEADS + 1], refs[GROUP_HEADS + 1 :]
    rows, width = x_ref.shape
    per = width // LANES

    def parts_of(head):
        place = head % GROUP_HEADS
        return back_refs[place : place + 1] if place < GROUP_HEADS - 1 else back_refs[place:]

    def pair(head):
        refs = parts_of(head)
        parts = [ref[head // GROUP_HEADS, : rows // len(refs)] for ref in refs]
        return (parts[0] if len(refs) == 1 else jnp.concatenate(parts, axis=0)).astype(F32)

    for head in range(HEADS):
        refs = parts_of(head)
        tiles = rows // LANES // len(refs)
        for tile in range(rows // LANES):
            at = rows // len(refs) + tile % tiles * HEAD_DIM
            part = refs[tile // tiles][head // GROUP_HEADS, at : at + HEAD_DIM]
            queries[head, :, tile * LANES : (tile + 1) * LANES] = part
    is_key = lax.broadcasted_iota(jnp.int32, (1, PAIR), 1) < HEAD_DIM
    for j in range(HEADS // 2):
        first, second = pair(2 * j), pair(2 * j + 1)
        flat[:, j * PAIR : (j + 1) * PAIR] = jnp.where(is_key, first, swap_halves(second)).astype(BF16)
        flat[:, width + j * PAIR : width + (j + 1) * PAIR] = jnp.where(is_key, swap_halves(first), second).astype(BF16)
    query = queries[...].reshape(width, rows)
    unit, scale = centre(x_ref[...].astype(F32))
    normed = (unit * row(gain_ref) + row(shift_ref)).astype(BF16)
    spread(lines, 2 * per, 3 * per, dot32(normed, query, (0, 1)))
    for b in range(2):
        spread(lines, (3 + b) * per, 3 * per, dot32(normed, flat[:, b * width : (b + 1) * width], (0, 0)))
    back_normed = dot32(query, w_ref[:, :width], (0, 1)) + dot32(flat[...], w_ref[:, width:], (1, 1))
    input_ref[...] = (back_hidden_ref[...] + centre_back(back_normed * row(gain_ref), unit, scale)).astype(BF16)

    def put(at, line):
        for piece in range(per):
            lines[at + piece : at + piece + 1, :] = line[:, piece * LANES : (piece + 1) * LANES]

    put(0, jnp.sum(back_normed * unit, axis=0, keepdims=True))
    put(per, jnp.sum(back_normed, axis=0, keepdims=True))
    at = (2 + 3 * width) * per
    put(at, dot32(jnp.ones((8, rows), BF16), query, (1, 1))[0:1])
    put(at + per, jnp.sum(flat[:, width:].astype(F32), axis=0, keepdims=True))
    lines[at + 2 * per :, :] = jnp.zeros((lines.shape[0] - at - 2 * per, LANES), F32)
    core = info_ref[0] % 2

    def window(step, _):
        for ref, which in ((send_ref, 1 - core), (keep_ref, core)):
            write_window((2 * step + which) * size, lines, ref, step)
        return 0

    lax.fori_loop(0, LATE_CHUNKS // 2, window, 0)


def finish(size, info, x, gain, shift, w_qkv, back_hidden, back):
    rows, width = x.shape
    window = jax.ShapeDtypeStruct((LATE_CHUNKS // 2, LATE_WINDOW, LANES), BF16)
    shapes = [jax.ShapeDtypeStruct((rows, width), BF16), window, window]
    operands = [x, gain, shift, w_qkv, back_hidden, *back]
    scratch = [
        pltpu.VMEM((HEADS, HEAD_DIM, rows), BF16),
        pltpu.VMEM((rows, 2 * width), BF16),
        pltpu.VMEM((-(-(LATE_CHUNKS - 1) * size // 8) * 8 + LATE_WINDOW + 8, LANES), F32),
    ]
    kernel = functools.partial(finish_kernel, size)
    return one_step(kernel, info, operands, shapes, scratch, rows * width)


def along_g(values):
    return lax.all_to_all(values, "g", 0, 0, tiled=True)


def hold(values, after):
    return lax.optimization_barrier((values, list(after)))[0] if len(after) > 0 else values


def exchange(parts):
    return [lax.ppermute(part, ("x", "c"), [(i, i ^ n) for i in range(4)]) for part, n in zip(parts, (2, 1, 3))]


class Plane:
    def gather_keys(self, kv):
        return [kv[None], swap(kv, "f")[None]]

    def gather_queries(self, q):
        return [q] + exchange([q] * 3)

    gather_grads = gather_queries

    def gather_first(self, values):
        over = swap(values, "x")
        return [values, over, swap(values, "c"), swap(over, "c")]

    def gather_parts(self, outs):
        return [outs[0]] + exchange(outs[1:4])

    def gather_back(self, outs):
        kept, sent = outs[4][0], outs[5][0]
        shape = (kept.shape[0], -1, PAIR)
        return kept.reshape(shape), swap(sent, "f").reshape(shape), self.gather_parts(outs)

    def sum_back(self, after, parts):
        return sum_back(after, *parts)


class AnyPlane:
    def __init__(self, clips, times, part):
        self.clips, self.times, self.part = clips, times, part

    def split(self, values):
        groups, rows, width = values.shape
        values = values.reshape(groups, rows, self.clips, self.times, -1).transpose(3, 0, 1, 2, 4)
        return values.reshape(self.times, groups, rows, width // self.times)

    def gather_keys(self, kv):
        return [lax.all_gather(kv, "f")]

    def gather_queries(self, q):
        groups, tiles, rows, lanes = q.shape
        q = lax.all_gather(q.transpose(0, 2, 1, 3).reshape(groups, rows, -1, self.part), "t")
        return [q.transpose(1, 3, 2, 0, 4).reshape(groups, -1, rows, self.times * self.part)]

    def gather_grads(self, values):
        groups, rows, _ = values.shape
        values = lax.all_gather(values.reshape(groups, rows, -1, self.part), "t")
        return [values.transpose(1, 2, 3, 0, 4).reshape(groups, rows, -1)]

    gather_first = gather_grads

    def gather_parts(self, outs):
        return list(lax.all_to_all(self.split(outs[0]), "t", 0, 0, tiled=True))

    def gather_back(self, outs):
        return outs

    def sum_back(self, after, outs):
        back_q = lax.psum_scatter(self.split(outs[0]), "t", scatter_dimension=0, tiled=False)
        back_kv = lax.psum_scatter(outs[1], "f", scatter_dimension=0, tiled=False).reshape(GROUPS, -1, PAIR)
        back_q = back_q.reshape(GROUPS, HEAD_DIM, -1, LANES).transpose(0, 2, 1, 3).reshape(GROUPS, -1, LANES)
        return jnp.concatenate([back_kv, back_q], axis=1)


def layer_norm(values, scaling, offset):
    row_mean = jnp.mean(values, axis=-1, keepdims=True)
    centred = values - row_mean
    spread = jnp.mean(centred * centred, axis=-1, keepdims=True)
    return centred * lax.rsqrt(spread + EPSILON) * scaling + offset


def gelu_exact(values):
    return jax.nn.gelu(values, approximate=False)


def per_device(
    time_axes,
    tokens,
    out_grad,
    lengths,
    norm1_gain,
    norm1_shift,
    w_qkv,
    query_bias,
    value_bias,
    w_proj,
    proj_bias,
    norm2_gain,
    norm2_shift,
    w_fc1,
    fc1_bias,
    w_fc2,
    fc2_bias,
    moment,
    ema_decay,
):
    clips, freq_rows, frames, width = tokens.shape
    part = freq_rows * frames
    rows = clips * part
    times = lax.axis_size(time_axes)
    devices = lax.axis_size("f") * GROUPS * times
    early_index = lax.axis_index(time_axes)
    fast = time_axes == ("x", "c")
    plane = Plane() if fast else AnyPlane(clips, times, part)
    first_frame = (lax.axis_index("g") * times + early_index) * frames
    frame = first_frame + lax.broadcasted_iota(jnp.int32, (1, freq_rows, frames), 2)
    keep_rows = (frame < lengths[:, None, None]).astype(F32).reshape(rows, 1)
    info = jnp.concatenate([early_index.astype(jnp.int32).reshape(1), lengths])

    x = tokens.reshape(rows, width)
    packs = start(x, norm1_gain, norm1_shift, w_qkv, query_bias, value_bias)
    attended, kept = [], []

    def fetch(values, heads, after):
        got = along_g(values)
        pairs, queries = hold((got[:, : heads * rows], got[:, heads * rows :]), after)
        kv = plane.gather_keys(pairs.reshape(GROUPS, heads * clips, part, PAIR))
        return kv, plane.gather_queries(queries.reshape(GROUPS, -1, HEAD_DIM, LANES))

    def merged(after, parts):
        out, low = merge(parts, after)
        kept.append(out)
        attended.append(along_g(hold(low, attended[-1:])))
        return low

    def alone(head):
        return fast and head == GROUP_HEADS - 1

    def run(head, clip, outs, after):
        kv, q = fetched[min(head, 1)]
        place = max(head - 1, 0) * clips + clip
        outs, held = ((), 1) if alone(head) else (outs, clips)
        *outs, token = attend(info, kv, q, place, clip, held, times, frames, outs, after)
        return outs, token

    fetched = [fetch(packs[0], 1, [])]
    fetched.append(fetch(packs[1], GROUP_HEADS - 1, fetched[0][0][1:] + fetched[0][1][1:]))
    parts = None
    for head in range(GROUP_HEADS):
        outs, token = run(head, 0, (), [] if head == 0 else [token])
        after = [token]
        if head > 0:
            after.append(merged(token, parts))
        come = fetched[1][0][1:] + fetched[1][1][1:] if head == 0 else []
        if alone(head):
            half = plane.gather_parts(outs)
            come = half[1:]
        for clip in range(1, clips):
            outs, token = run(head, clip, outs, after)
        parts = plane.gather_parts(hold(outs, come))
    if fast:
        merged(token, half)
    merged(token, parts)
    if fast:
        size = moment.shape[0] // LANES
        block_out, back_hidden, early, grad = middle(
            x, out_grad.reshape(rows, width), keep_rows, w_proj, proj_bias, norm2_gain, norm2_shift, w_fc1, fc1_bias,
            w_fc2, fc2_bias, attended,
        )
        block_out = block_out.reshape(tokens.shape)
        early_windows = pack_early(devices, size, *early)
    else:
        attended_low = jnp.concatenate(attended, axis=1).reshape(width, rows)
        branch = dot32(attended_low, w_proj, (0, 0)) + proj_bias
        hidden = x.astype(F32) + branch
        normed2, norm2_pull = jax.vjp(layer_norm, hidden, norm2_gain, norm2_shift)
        normed2_low = normed2.astype(BF16)
        preactive = dot32(normed2_low, w_fc1, (1, 0)) + fc1_bias
        activated, gelu_pull = jax.vjp(gelu_exact, preactive)
        activated_low = activated.astype(BF16)
        branch2 = dot32(activated_low, w_fc2, (1, 0)) + fc2_bias
        block_out = ((hidden + branch2) * keep_rows).astype(BF16).reshape(tokens.shape)
        grad_out = out_grad.astype(F32).reshape(rows, width) * keep_rows
        back_branch2 = grad_out.astype(BF16)
        grad_fc2_bias = jnp.sum(back_branch2.astype(F32), axis=0)
        back_activated = dot32(back_branch2, w_fc2, (1, 1))
        back_preactive = gelu_pull(back_activated)[0].astype(BF16)
        grad_fc1_bias = jnp.sum(back_preactive.astype(F32), axis=0)
        back_normed2 = dot32(back_preactive, w_fc1, (1, 1))
        back_hidden_norm, grad_norm2_gain, grad_norm2_shift = norm2_pull(back_normed2)
        back_hidden = grad_out + back_hidden_norm
        back_branch = back_hidden.astype(BF16)
        grad_proj_bias = jnp.sum(back_branch.astype(F32), axis=0)
        back_attended = dot32(w_proj, back_branch, (1, 1)).astype(BF16)
        early_windows = info
        grad = back_attended.reshape(GROUPS, -1, rows)
    ready = grad_rows_of(along_g(grad), kept, early_windows)
    back, parts, token = [], None, None
    grads = plane.gather_first(ready[0])
    if fast:
        early_sum = hold(early_windows, grads[:1]).reshape(2, 2, 2, GROUPS, EARLY_WINDOW, LANES)
        early_sum = lax.psum_scatter(early_sum, "c", scatter_dimension=0, tiled=False)

    def run_back(head, clip, outs, after):
        kv, q = fetched[min(head, 1)]
        place = max(head - 1, 0) * clips + clip
        outs, held = ((), 1) if alone(head) else (outs, clips)
        *outs, token = attend_back(info, kv, q, grads, place, clip, held, times, frames, outs, after)
        return outs, token

    for head in range(GROUP_HEADS):
        outs, token = run_back(head, 0, (), [] if head == 0 else [token])
        after = [token]
        if head > 0:
            after += [plane.sum_back(token, parts)] + back
            back.append(along_g(hold(after[1], back)))
        if fast and head == 0:
            early_sum = hold(early_sum, [token])
            after.append(early_sum)
        come = []
        if head + 1 < GROUP_HEADS:
            later = plane.gather_grads(hold(ready[head + 1], after))
            come = later[1:]
        if alone(head):
            half = plane.gather_back(outs)
            come = [half[1]] + half[2][1:]
        for clip in range(1, clips):
            outs, token = run_back(head, clip, outs, after)
        outs = hold(outs, come)
        if fast and head == 0:
            early_sum = hold(early_sum, come + [token]).reshape(4, GROUPS, EARLY_WINDOW, LANES)
            early_sum = lax.psum_scatter(early_sum, ("x", "f"), scatter_dimension=0, tiled=False)
        if head + 1 < GROUP_HEADS:
            grads = later
        parts = plane.gather_back(outs)
    if fast:
        back.append(along_g(hold(plane.sum_back(token, half), back[-1:])))
    back.append(along_g(hold(plane.sum_back(token, parts), back[-1:])))
    if fast:
        input_grad, *late_windows = finish(
            size, info, x, norm1_gain, norm1_shift, w_qkv, back_hidden, back
        )
        input_grad = input_grad.reshape(tokens.shape)
        early_sum = lax.psum_scatter(hold(early_sum, [back[-1]]), "g", scatter_dimension=0, tiled=False).astype(F32)
        late_sum = reduce_late(*late_windows, early_sum)
        weight_grad = own_chunk(lax.optimization_barrier(early_sum), late_sum, moment.shape[0])
    else:
        back = jnp.stack(back, axis=1)
        back_kv = back[:, :, :rows].transpose(2, 0, 1, 3).reshape(rows, 2 * width)
        back_q = back[:, :, rows:].reshape(GROUPS, GROUP_HEADS, -1, HEAD_DIM, LANES).transpose(0, 1, 3, 2, 4).reshape(width, rows)
        grad_query_bias = jnp.sum(back_q.astype(F32), axis=1)
        grad_kv_bias = jnp.sum(back_kv.astype(F32), axis=0)
        grad_value_bias = grad_kv_bias.reshape(HEADS, 2, HEAD_DIM)[:, 1].reshape(width)
        normed, norm1_pull = jax.vjp(layer_norm, x.astype(F32), norm1_gain, norm1_shift)
        normed_low = normed.astype(BF16)
        head_dims = (width, GROUPS, GROUP_HEADS, HEAD_DIM)
        w_q = w_qkv[:, :width]
        w_kv = [w_qkv[:, width : 2 * width].reshape(head_dims), w_qkv[:, 2 * width :].reshape(head_dims)]
        w_kv = jnp.stack(w_kv, axis=3).reshape(width, 2 * width)
        back_normed = dot32(back_q, w_q, (0, 1)) + dot32(back_kv, w_kv, (1, 1))
        back_input_norm, grad_norm1_gain, grad_norm1_shift = norm1_pull(back_normed)
        input_grad = (back_hidden + back_input_norm).astype(BF16).reshape(tokens.shape)
        grad_proj = dot32(attended_low, back_branch, (1, 0))
        grad_fc1 = dot32(normed2_low, back_preactive, (0, 0))
        grad_fc2 = dot32(activated_low, back_branch2, (0, 0))
        grad_q = dot32(normed_low, back_q, (0, 1))
        grad_kv = dot32(normed_low, back_kv, (0, 0)).reshape(width, HEADS, 2, HEAD_DIM)
        grad_qkv = jnp.concatenate([grad_q, grad_kv[:, :, 0].reshape(width, width), grad_kv[:, :, 1].reshape(width, width)], axis=1)
        joined = jnp.concatenate(
            [
                grad_norm1_gain,
                grad_norm1_shift,
                grad_qkv.reshape(-1),
                grad_query_bias,
                grad_value_bias,
                grad_proj.reshape(-1),
                grad_proj_bias,
                grad_norm2_gain,
                grad_norm2_shift,
                grad_fc1.reshape(-1),
                grad_fc1_bias,
                grad_fc2.reshape(-1),
                grad_fc2_bias,
            ]
        ).astype(BF16)
        padding = moment.shape[0] * devices - joined.shape[0]
        joined = jnp.concatenate([joined, jnp.zeros((padding,), BF16)])
        weight_grad = lax.psum_scatter(joined, ("f", "g") + time_axes, scatter_dimension=0, tiled=True).astype(F32)
    new_moment = ema_decay[0] * moment + (1.0 - ema_decay[0]) * weight_grad
    return (block_out, input_grad, weight_grad, new_moment)


def solution(mesh):
    freqs, times = mesh.shape["freq"], mesh.shape["tm"]
    if (freqs, times) == (2, 16):
        time_sizes, time_axes = (2, 2), ("x", "c")
    else:
        time_sizes, time_axes = (times // GROUPS,), ("t",)
    fine = Mesh(mesh.devices.reshape(freqs, GROUPS, *time_sizes), ("f", "g") + time_axes)
    patches = P(None, "f", ("g",) + time_axes, None)
    flat = P(("f", "g") + time_axes)
    return jax.shard_map(
        functools.partial(per_device, time_axes),
        mesh=fine,
        in_specs=(patches, patches) + (P(),) * 14 + (flat, P()),
        out_specs=(patches, patches, flat, flat),
        check_vma=False,
    )
```
